32 devices in a mesh: section: 2 (over core), grp: 4 (over y, x), dev: 4 (over z).
Axes of the slice: x: 2, y: 2, z: 4, core: 2. Of those that a mesh axis runs over, the one named last changes fastest.
Arguments:
- frames: bfloat16 [4, 64, 512, 256], P('grp', 'dev', 'section'), may hold values from -6 to 6
- templates: bfloat16 [8192, 256], P('dev'), may hold values from -0.375 to 0.375
- pair_block: int32 [2, 4, 32], P('section', 'grp', 'dev'), may hold values from 0 to 63
- pair_tile: int32 [2, 4, 32], P('section', 'grp', 'dev'), may hold values from 0 to 3
- pair_count: int32 [2, 4, 4], P('section', 'grp', 'dev'), may hold values from 1 to 8, 16 in all within a row
- owner_order: int32 [8192], replicated, may hold values from 0 to 8191, each once
Outputs:
- quantities: float32 [4, 8192], P('grp', 'dev')
The draws below stay inside these ranges and needn't reach their ends.
Inputs may be any that keep to these rules, and one draw needn't show every extreme that they name: `pair_count`: each device's count of live slots; the counts of one section half and run sum to half of all slots there, and one of them is 8. `owner_order`: A permutation of the precursors.
All inputs are finite; a program needn't handle non-finite values.
Results may differ from the reference program's by a relative error of at most 0.00037.
Values may be sent and summed in bfloat16 or wider, within the bound.
No kernel may reach another device: no remote copies, remote signals or barrier semaphores. Data moves between devices by JAX's collectives and lax.ppermute only.
A program may use at most 64 MiB of HBM per device.

```python
import math
import jax
import jax.numpy as jnp
import numpy as np
from jax import lax

CH = 256
MOB = 512
SCALES = 6
RAD = 4
TM = 64
PB = 128
PREC = 8192
F_DEV = 16
SLOTS = 8
RUNS = 4
FRAMES = 64
NB = 64
NT = 4
N_SECTION = 2
N_DEV = 4


def set_ends(result, rng, low, largest):
    longest = result.shape.index(max(result.shape))
    spots = []
    for shift in (0, 1):
        where = [jax.random.randint(jax.random.fold_in(rng, axis), (), 0, length) for axis, length in enumerate(result.shape)]
        where[longest] = (where[longest] + shift) % result.shape[longest]
        spots.append(tuple(where))
    return result.at[spots[0]].set(low).at[spots[1]].set(largest)


def level_of(stream_key, shape, shards, least, largest):
    def one(axis_at, shards_of):
        draws = jax.random.uniform(jax.random.fold_in(jax.random.fold_in(stream_key, 6), axis_at), (shards_of,), jnp.float32, least / len(shards), largest / len(shards))
        return jnp.repeat(jnp.exp(draws), shape[axis_at] // shards_of).reshape((-1,) + (1,) * (len(shape) - axis_at - 1))

    factor_of = one(*shards[0])
    for cut in shards[1:]:
        factor_of = factor_of * one(*cut)
    return factor_of


def profile(number_of, total, most, lean):
    weights = [(1 << 20) // math.isqrt(rank ** lean) + 1 for rank in range(2, number_of + 1)]
    surplus, counts = total - most - (number_of - 1), [1] * (number_of - 1)
    while surplus > 0:
        movable = [i for i in range(number_of - 1) if counts[i] < most]
        pool, left = sum([weights[i] for i in movable]), surplus
        for i in movable:
            extra = min(most - counts[i], max(1, left * weights[i] // pool), surplus)
            counts[i] = counts[i] + extra
            surplus = surplus - extra
    return np.array([most] + counts)


def ragged(stream_key, amount, total, most, lean):
    if amount == 2:
        one = jax.random.randint(stream_key, (), max(1, total - most), min(most, total - 1) + 1)
        return jnp.stack([one, total - one])
    lengths = jnp.asarray(profile(amount, total, most, lean), jnp.int32)
    couples = (amount - 1) // 2
    source_of, sink = lengths[1:1 + 2 * couples:2], lengths[2:2 + 2 * couples:2]
    margin = jnp.minimum(source_of - 1, most - sink)
    passed = jax.random.randint(jax.random.fold_in(stream_key, 1), (couples,), 0, 1 << 20) % (margin + 1)
    lengths = lengths.at[1:1 + 2 * couples:2].set(source_of - passed).at[2:2 + 2 * couples:2].set(sink + passed)
    return lengths[jax.random.permutation(jax.random.fold_in(stream_key, 2), amount)]


def scatter_about(own_key, shape, width, limit, shards=(), kind=jnp.bfloat16):
    array = jax.random.normal(own_key, shape, jnp.float32) * width
    if len(shards) > 0:
        array = level_of(own_key, shape, shards, -0.22, 0.18) * array
    return jnp.clip(array, min=-limit, max=limit).astype(kind)


def setup_inputs(seed: int = 0) -> dict:
    seeds = jax.random.split(jax.random.key(seed), 7)
    return {
        "frames": scatter_about(seeds[0], (RUNS, FRAMES, MOB, CH), 1.0, 6.0, ((0, 4), (1, 4), (2, 2))),
        "templates": scatter_about(seeds[1], (PREC, CH), CH ** -0.5, 0.375, ((0, 4),)),
        "pair_block": set_ends(jax.random.randint(seeds[2], (N_SECTION, RUNS, N_DEV * SLOTS), 0, NB), jax.random.fold_in(seeds[2], 1), 0, NB - 1).astype(jnp.int32),
        "pair_tile": set_ends(jax.random.randint(seeds[3], (N_SECTION, RUNS, N_DEV * SLOTS), 0, NT), jax.random.fold_in(seeds[3], 1), 0, NT - 1).astype(jnp.int32),
        "pair_count": jax.vmap(lambda own: ragged(own, N_DEV, N_DEV * SLOTS // 2, SLOTS, 2))(jax.random.split(seeds[4], N_SECTION * RUNS)).reshape((N_SECTION, RUNS, N_DEV)).astype(jnp.int32),
        "owner_order": jax.random.permutation(seeds[5], PREC).astype(jnp.int32),
    }


retention_spread = 2.0

def retention_weights():
    bell_values = [math.exp(-0.5 * (offset / retention_spread) ** 2) for offset in range(-RAD, RAD + 1)]
    bell_total = sum(bell_values)
    return [weight_value / bell_total for weight_value in bell_values]

def mobility_kernels(row_start, row_count):
    row_place = (row_start + jnp.arange(row_count, dtype=jnp.int32)).astype(jnp.float32)
    col_place = jnp.arange(MOB, dtype=jnp.int32).astype(jnp.float32)
    distance = row_place[:, None] - col_place[None, :]
    tables = []
    for level in range(SCALES):
        spread_scans = 2.0 ** level
        scaled = distance / spread_scans
        tables.append((1.0 - scaled * scaled) * jnp.exp(-0.5 * scaled * scaled) / math.sqrt(0.75 * math.sqrt(math.pi) * spread_scans))
    return jnp.stack(tables).astype(jnp.bfloat16)

def smooth_frames(frames_run):
    weights = retention_weights()
    count_frames = frames_run.shape[0]
    padded = jnp.pad(frames_run.astype(jnp.float32), ((RAD, RAD), (0, 0), (0, 0)))
    smoothed = weights[0] * padded[0:count_frames]
    for offset in range(1, 2 * RAD + 1):
        smoothed = smoothed + weights[offset] * padded[offset:offset + count_frames]
    return smoothed.astype(jnp.bfloat16)

def run_quantities(frames_run, blocks_run, tiles_run, counts_run, templates):
    smoothed = smooth_frames(frames_run)
    columns = jnp.moveaxis(smoothed, 1, 0).reshape(MOB, FRAMES * CH)
    kernels = mobility_kernels(0, MOB)
    levels = []
    for level in range(SCALES):
        levels.append(jnp.dot(kernels[level], columns, preferred_element_type=jnp.float32).astype(jnp.bfloat16))
    wavelet_stack = jnp.stack(levels).reshape(SCALES, MOB, FRAMES, CH)
    mob_local = MOB // N_SECTION
    flat_blocks = blocks_run.reshape(-1)
    flat_tiles = tiles_run.reshape(-1)

    def visit_pair(totals, slot_index):
        half_index = slot_index // (N_DEV * SLOTS)
        device = slot_index // SLOTS % N_DEV
        within = slot_index % SLOTS
        live_pairs = counts_run[half_index, device]
        block_id = flat_blocks[slot_index]
        tile_id = flat_tiles[slot_index]
        mob_start = (half_index * mob_local + tile_id * TM).astype(jnp.int32)
        frame_start = (device * F_DEV).astype(jnp.int32)
        tile_cells = lax.dynamic_slice(wavelet_stack, (jnp.int32(0), mob_start, frame_start, jnp.int32(0)), (SCALES, TM, F_DEV, CH)).reshape(-1, CH)
        block_rows = lax.dynamic_slice_in_dim(templates, (block_id * PB).astype(jnp.int32), PB, 0)
        scores = jnp.dot(tile_cells, block_rows.T, preferred_element_type=jnp.float32)
        response = lax.optimization_barrier(jnp.mean(jnp.maximum(scores, 0.0), axis=0)) * (within < live_pairs).astype(jnp.float32)
        block_hit = (jnp.arange(NB, dtype=jnp.int32) == block_id).astype(jnp.float32)
        return (totals + block_hit[:, None] * response[None, :], None)
    totals = lax.scan(visit_pair, jnp.zeros((NB, PB), jnp.float32), jnp.arange(N_SECTION * N_DEV * SLOTS, dtype=jnp.int32))[0]
    return totals.reshape(PREC)

def reference(frames, templates, pair_block, pair_tile, pair_count, owner_order):
    rows_list = []
    for run_index in range(RUNS):
        quantity = run_quantities(frames[run_index], pair_block[:, run_index], pair_tile[:, run_index], pair_count[:, run_index], templates)
        rows_list.append(jnp.zeros((PREC,), jnp.float32).at[owner_order].set(quantity))
    placed = jnp.stack(rows_list)
    run_total = lax.optimization_barrier(jnp.sum(placed, axis=1))
    factor = jnp.mean(run_total) / run_total
    return placed * factor[:, None]
```

```python
import math

import jax
import jax.numpy as jnp
from jax import lax
from jax.experimental import pallas as pl
from jax.experimental.pallas import tpu as pltpu
from jax.sharding import PartitionSpec as P

MOB = 512
SCALES = 6
RAD = 4
TM = 64
PB = 128
PREC = 8192
LANES = 128
TILE_ROWS = SCALES * TM
BLOCKS = PREC // PB

retention_spread = 2.0


def swap(cells, axis, distance):
    count = lax.axis_size(axis)
    return lax.ppermute(cells, axis, [(i, i ^ distance) for i in range(count)])


def retention_weights():
    bell_values = [
        math.exp(-0.5 * (offset / retention_spread) ** 2) for offset in range(-RAD, RAD + 1)
    ]
    bell_total = sum(bell_values)
    return [weight_value / bell_total for weight_value in bell_values]


def mobility_kernels(section_index, mob_local):
    tiles = mob_local // TM
    row_place = (section_index * mob_local + jnp.arange(mob_local, dtype=jnp.int32)).astype(
        jnp.float32
    )
    col_index = jnp.arange(MOB, dtype=jnp.int32)
    col_place = jnp.where(
        col_index < mob_local,
        col_index + section_index * mob_local,
        col_index - mob_local + (1 - section_index) * mob_local,
    ).astype(jnp.float32)
    distance = row_place.reshape(tiles, TM)[:, :, None] - col_place[None, None, :]
    tables = []
    for level in range(SCALES):
        spread_scans = 2.0**level
        scaled = distance / spread_scans
        tables.append(
            (1.0 - scaled * scaled)
            * jnp.exp(-0.5 * scaled * scaled)
            / math.sqrt(0.75 * math.sqrt(math.pi) * spread_scans)
        )
    return jnp.stack(tables, axis=1).astype(jnp.bfloat16).reshape(tiles * TILE_ROWS, MOB)


def weighted(rows, at):
    weights = retention_weights()
    total = weights[RAD] * rows[at]
    for offset in range(1, RAD + 1):
        total = total + weights[RAD + offset] * (rows[at - offset] + rows[at + offset])
    return total.astype(jnp.bfloat16)


def smooth_inner_body(frames_ref, out_ref):
    count = frames_ref.shape[0]
    for r in range(0, frames_ref.shape[1], 16):
        rows = [frames_ref[f, r : r + 16, :].astype(jnp.float32) for f in range(count)]
        for f in range(RAD, count - RAD):
            out_ref[f - RAD, r : r + 16, :] = weighted(rows, f)


def smooth_edges_body(left_ref, frames_ref, right_ref, out_ref):
    count = frames_ref.shape[0]
    for r in range(0, frames_ref.shape[1], 16):
        at = slice(r, r + 16)
        head = [left_ref[f, at, :].astype(jnp.float32) for f in range(RAD)]
        head += [frames_ref[f, at, :].astype(jnp.float32) for f in range(2 * RAD)]
        for f in range(RAD):
            out_ref[f, at, :] = weighted(head, f + RAD)
        tail = [frames_ref[f, at, :].astype(jnp.float32) for f in range(count - 2 * RAD, count)]
        tail += [right_ref[f, at, :].astype(jnp.float32) for f in range(RAD)]
        for f in range(RAD):
            out_ref[RAD + f, at, :] = weighted(tail, f + RAD)


def smooth_inner(frames):
    count, scans, channels = frames.shape
    step = 64
    inner = count - 2 * RAD
    return pl.pallas_call(
        smooth_inner_body,
        grid=(scans // step,),
        in_specs=[pl.BlockSpec((count, step, channels), lambda i: (0, i, 0))],
        out_specs=pl.BlockSpec((inner, step, channels), lambda i: (0, i, 0)),
        out_shape=jax.ShapeDtypeStruct((inner, scans, channels), jnp.bfloat16),
        cost_estimate=pl.CostEstimate(
            flops=13 * inner * scans * channels, bytes_accessed=3 << 20, transcendentals=0
        ),
        name="smooth_inner",
    )(frames)


def smooth_edges(left, frames, right):
    count, scans, channels = frames.shape
    step = 64
    halo_spec = pl.BlockSpec((RAD, step, channels), lambda i: (0, i, 0))
    return pl.pallas_call(
        smooth_edges_body,
        grid=(scans // step,),
        in_specs=[
            halo_spec,
            pl.BlockSpec((count, step, channels), lambda i: (0, i, 0)),
            halo_spec,
        ],
        out_specs=pl.BlockSpec((2 * RAD, step, channels), lambda i: (0, i, 0)),
        out_shape=jax.ShapeDtypeStruct((2 * RAD, scans, channels), jnp.bfloat16),
        cost_estimate=pl.CostEstimate(
            flops=13 * 8 * scans * channels, bytes_accessed=4 << 20, transcendentals=0
        ),
        name="smooth_edges",
    )(left, frames, right)


def wavelet_body(kernels_ref, own_ref, other_ref, out_ref):
    half = own_ref.shape[1]
    rows = kernels_ref.shape[0]
    own = own_ref[0]
    other = other_ref[0]
    step = TILE_ROWS
    for r in range(0, rows, step):
        total = jnp.dot(
            kernels_ref[r : r + step, :half], own, preferred_element_type=jnp.float32
        ) + jnp.dot(kernels_ref[r : r + step, half:], other, preferred_element_type=jnp.float32)
        out_ref[0, r : r + step, :] = total.astype(jnp.bfloat16)


def wavelets(kernels, own, other):
    count, half, channels = own.shape
    rows = kernels.shape[0]
    frame_spec = pl.BlockSpec((1, half, channels), lambda f: (f, 0, 0))
    return pl.pallas_call(
        wavelet_body,
        grid=(count,),
        in_specs=[pl.BlockSpec((rows, 2 * half), lambda f: (0, 0)), frame_spec, frame_spec],
        out_specs=pl.BlockSpec((1, rows, channels), lambda f: (f, 0, 0)),
        out_shape=jax.ShapeDtypeStruct((count, rows, channels), jnp.bfloat16),
        cost_estimate=pl.CostEstimate(
            flops=2 * count * rows * 2 * half * channels,
            bytes_accessed=10 << 20,
            transcendentals=0,
        ),
        compiler_params=pltpu.CompilerParams(vmem_limit_bytes=24 << 20),
        name="wavelets",
    )(kernels, own, other)


def score_body(slots, unit, groups, *refs):
    (block_sm, tile_sm, place_sm, inner_ref, edges_ref, owner_ref, own_ref) = refs[:7]
    piece_refs = refs[7 : 7 + 2 * groups]
    out_ref, panel, totals, sems = refs[7 + 2 * groups :]
    step = pl.program_id(0)
    live = place_sm[0]
    section_index, grp, dev = place_sm[1], place_sm[2], place_sm[3]
    own_rows = own_ref.shape[0]
    share = own_rows // (2 * groups)
    units = PB // unit

    def unit_copy(source, slot, u):
        return pltpu.make_async_copy(
            source, panel.at[slot, pl.ds(u * unit, unit), :], sems.at[slot, u]
        )

    @pl.when(step == 0)
    def _():
        totals[...] = jnp.zeros_like(totals)

        def fetch(slot, carry):
            for u in range(units):
                row = block_sm[slot] * PB + u * unit
                owner = row // own_rows
                within = row - owner * own_rows
                part = within // share
                offset = pl.multiple_of(within - part * share, unit)
                from_dev = jnp.bitwise_xor(dev, owner)
                from_grp = jnp.bitwise_xor(grp, part // 2)
                from_section = jnp.bitwise_xor(section_index, part % 2)

                @pl.when(from_dev == 0)
                def _():
                    unit_copy(
                        own_ref.at[pl.ds(pl.multiple_of(within, unit), unit), :], slot, u
                    ).start()

                for s in range(2):
                    for g in range(groups):

                        @pl.when((from_dev > 0) & (from_section == s) & (from_grp == g))
                        def _():
                            unit_copy(
                                piece_refs[s * groups + g].at[
                                    from_dev - 1, pl.ds(offset, unit), :
                                ],
                                slot,
                                u,
                            ).start()

            return carry

        lax.fori_loop(0, live, fetch, 0)

        def arrive(slot, carry):
            for u in range(units):
                unit_copy(own_ref.at[pl.ds(0, unit), :], slot, u).wait()
            return carry

        lax.fori_loop(0, live, arrive, 0)

    def visit(slot, carry):
        at = pl.ds(pl.multiple_of(tile_sm[slot] * TILE_ROWS, TILE_ROWS), TILE_ROWS)
        block = panel[slot]
        added = totals[slot]
        for cells_ref in (inner_ref, edges_ref):
            scores = lax.dot_general(
                cells_ref[0, at, :],
                block,
                (((1,), (1,)), ((), ())),
                preferred_element_type=jnp.float32,
            )
            added = added + jnp.sum(
                jnp.maximum(scores, 0.0).reshape(TILE_ROWS // 8, 8, PB), axis=0
            )
        totals[slot] = added
        return carry

    lax.fori_loop(0, live, visit, 0)

    @pl.when(step == pl.num_programs(0) - 1)
    def _():
        cells = 2 * pl.num_programs(0) * TILE_ROWS
        high_index = lax.broadcasted_iota(jnp.int32, (BLOCKS, PB), 0)
        low_index = lax.broadcasted_iota(jnp.int32, (LANES, PB), 0)
        out_ref[...] = jnp.zeros_like(out_ref)

        def place(slot, response_total):
            response = jnp.sum(totals[slot], axis=0, keepdims=True) / cells
            owner = owner_ref[pl.ds(block_sm[slot], 1), :]
            high = jnp.where(high_index == owner // LANES, response, 0.0)
            low = (low_index == owner % LANES).astype(jnp.bfloat16)
            added = out_ref[:BLOCKS, :]
            for _ in range(3):
                part = high.astype(jnp.bfloat16)
                high = high - part.astype(jnp.float32)
                added = added + lax.dot_general(
                    part, low, (((1,), (1,)), ((), ())), preferred_element_type=jnp.float32
                )
            out_ref[:BLOCKS, :] = added
            return response_total + response

        response_total = lax.fori_loop(0, live, place, jnp.zeros((1, PB), jnp.float32))
        out_ref[BLOCKS:, :] = jnp.broadcast_to(
            jnp.sum(response_total, axis=1, keepdims=True), (8, LANES)
        )


def score(block_ids, tile_ids, place, inner, edges, owner_order, own_templates, pieces):
    slots = block_ids.shape[0]
    groups = len(pieces) // 2
    share = own_templates.shape[0] // (2 * groups)
    unit = min(share, PB)
    count, rows, channels = inner.shape
    smem = pl.BlockSpec(memory_space=pltpu.SMEM)
    anywhere = pl.BlockSpec(memory_space=pl.ANY)
    frame_spec = pl.BlockSpec((1, rows, channels), lambda f: (f, 0, 0))

    def body(*refs):
        score_body(slots, unit, groups, *refs)

    return pl.pallas_call(
        body,
        grid=(count,),
        in_specs=[smem, smem, smem, frame_spec, frame_spec]
        + [pl.BlockSpec((BLOCKS, PB), lambda f: (0, 0)), anywhere]
        + [anywhere] * len(pieces),
        out_specs=pl.BlockSpec((BLOCKS + 8, LANES), lambda f: (0, 0)),
        out_shape=jax.ShapeDtypeStruct((BLOCKS + 8, LANES), jnp.float32),
        scratch_shapes=[
            pltpu.VMEM((slots, PB, channels), jnp.bfloat16),
            pltpu.VMEM((slots, 8, PB), jnp.float32),
            pltpu.SemaphoreType.DMA((slots, PB // unit)),
        ],
        cost_estimate=pl.CostEstimate(
            flops=2 * slots * 2 * count * TILE_ROWS * PB * channels,
            bytes_accessed=14 << 20,
            transcendentals=0,
        ),
        compiler_params=pltpu.CompilerParams(vmem_limit_bytes=24 << 20),
        name="score",
    )(block_ids, tile_ids, place, inner, edges, owner_order, own_templates, *pieces)


def on_device(frames, templates, pair_block, pair_tile, pair_count, owner_order):
    section_index = lax.axis_index("section")
    grp = lax.axis_index("grp")
    dev = lax.axis_index("dev")
    devs = lax.axis_size("dev")
    groups = lax.axis_size("grp")
    own_frames = frames[0]
    mob_local = own_frames.shape[1]

    share = templates.shape[0] // (2 * groups)
    own_piece = lax.dynamic_slice_in_dim(templates, (grp * 2 + section_index) * share, share, 0)
    remote = jnp.stack([swap(own_piece, "dev", k) for k in range(1, devs)])

    last = devs - 1
    left = lax.ppermute(
        own_frames[own_frames.shape[0] - RAD :], "dev", [(i, i + 1) for i in range(last)]
    )
    right = lax.ppermute(own_frames[:RAD], "dev", [(i + 1, i) for i in range(last)])

    inner_own = smooth_inner(own_frames)
    inner_other = swap(inner_own, "section", 1)
    kernels = mobility_kernels(section_index, mob_local)
    inner = wavelets(kernels, inner_own, inner_other)

    mine = [remote] + [swap(remote, "grp", j) for j in range(1, groups)]
    pieces = mine + [swap(piece, "section", 1) for piece in mine]

    edges_own = smooth_edges(left, own_frames, right)
    edges_other = swap(edges_own, "section", 1)
    edges = wavelets(kernels, edges_own, edges_other)

    place = jnp.stack([pair_count[0, 0, 0], section_index, grp, dev])
    contribution = score(
        pair_block[0, 0],
        pair_tile[0, 0],
        place,
        inner,
        edges,
        owner_order.reshape(BLOCKS, PB),
        templates,
        pieces,
    )
    both = contribution + swap(contribution, "section", 1)
    rows = BLOCKS // devs
    tail = both[BLOCKS:]

    def slice_for(target):
        return jnp.concatenate([lax.dynamic_slice_in_dim(both, target * rows, rows, 0), tail])

    owned = slice_for(dev)
    for k in range(1, devs):
        owned = owned + swap(slice_for(jnp.bitwise_xor(dev, k)), "dev", k)
    run_total = owned[rows:]
    all_total = run_total
    for j in range(1, groups):
        all_total = all_total + swap(run_total, "grp", j)
    factor = (all_total[:1, :1] / groups) / run_total[:1, :1]
    return (owned[:rows] * factor).reshape(1, rows * LANES)


def solution(mesh):
    placed = (
        P("grp", "dev", "section", None),
        P("dev", None),
        P("section", "grp", "dev"),
        P("section", "grp", "dev"),
        P("section", "grp", "dev"),
        P(),
    )
    return jax.shard_map(
        on_device, mesh=mesh, in_specs=placed, out_specs=P("grp", "dev"), check_vma=False
    )
```

```python
import math

import jax
import jax.numpy as jnp
from jax import lax
from jax.experimental import pallas as pl
from jax.experimental.pallas import tpu as pltpu
from jax.sharding import PartitionSpec as P

MOB = 512
SCALES = 6
RAD = 4
TM = 64
PB = 128
PREC = 8192
LANES = 128
TILE_ROWS = SCALES * TM
BLOCKS = PREC // PB
GROUPS = 4

retention_spread = 2.0


def swap(cells, axis, distance):
    count = lax.axis_size(axis)
    return lax.ppermute(cells, axis, [(i, i ^ distance) for i in range(count)])


def split_swap(cells, axis, distance, other_distance):
    count = lax.axis_size(axis)
    pairs = [(i, i ^ distance) for i in range(count)]
    pairs += [(count + i, count + (i ^ other_distance)) for i in range(count)]
    return lax.ppermute(cells, ("section", axis), pairs)


def retention_weights():
    bell_values = [
        math.exp(-0.5 * (offset / retention_spread) ** 2) for offset in range(-RAD, RAD + 1)
    ]
    bell_total = sum(bell_values)
    return [weight_value / bell_total for weight_value in bell_values]


def mobility_kernels(section_index, mob_local):
    tiles = mob_local // TM
    row_place = (section_index * mob_local + jnp.arange(mob_local, dtype=jnp.int32)).astype(
        jnp.float32
    )
    col_index = jnp.arange(MOB, dtype=jnp.int32)
    col_place = jnp.where(
        col_index < mob_local,
        col_index + section_index * mob_local,
        col_index - mob_local + (1 - section_index) * mob_local,
    ).astype(jnp.float32)
    distance = row_place.reshape(tiles, TM)[:, :, None] - col_place[None, None, :]
    tables = []
    for level in range(SCALES):
        spread_scans = 2.0**level
        scaled = distance / spread_scans
        tables.append(
            (1.0 - scaled * scaled)
            * jnp.exp(-0.5 * scaled * scaled)
            / math.sqrt(0.75 * math.sqrt(math.pi) * spread_scans)
        )
    return jnp.stack(tables, axis=1).astype(jnp.bfloat16).reshape(tiles * TILE_ROWS, MOB)


def weighted(rows, at):
    weights = retention_weights()
    total = weights[RAD] * rows[at]
    for offset in range(1, RAD + 1):
        total = total + weights[RAD + offset] * (rows[at - offset] + rows[at + offset])
    return total.astype(jnp.bfloat16)


def smooth_inner_body(frames_ref, out_ref):
    count, scans, channels = frames_ref.shape
    for r in range(0, scans, 16):
        for c in range(0, channels, LANES):
            at = (slice(r, r + 16), slice(c, c + LANES))
            rows = [frames_ref[f, at[0], at[1]].astype(jnp.float32) for f in range(count)]
            for f in range(RAD, count - RAD):
                out_ref[f - RAD, at[0], at[1]] = weighted(rows, f)


def smooth_edges_body(left_ref, frames_ref, right_ref, out_ref):
    count, scans, channels = frames_ref.shape
    for r in range(0, scans, 16):
        for c in range(0, channels, LANES):
            at = (slice(r, r + 16), slice(c, c + LANES))

            def cells(ref, first, last):
                return [ref[f, at[0], at[1]].astype(jnp.float32) for f in range(first, last)]

            head = cells(left_ref, 0, RAD) + cells(frames_ref, 0, 2 * RAD)
            for f in range(RAD):
                out_ref[f, at[0], at[1]] = weighted(head, f + RAD)
            tail = cells(frames_ref, count - 2 * RAD, count) + cells(right_ref, 0, RAD)
            for f in range(RAD):
                out_ref[RAD + f, at[0], at[1]] = weighted(tail, f + RAD)


def smooth_inner(frames):
    count, scans, channels = frames.shape
    step = 64
    inner = count - 2 * RAD
    return pl.pallas_call(
        smooth_inner_body,
        grid=(scans // step,),
        in_specs=[pl.BlockSpec((count, step, channels), lambda i: (0, i, 0))],
        out_specs=pl.BlockSpec((inner, step, channels), lambda i: (0, i, 0)),
        out_shape=jax.ShapeDtypeStruct((inner, scans, channels), jnp.bfloat16),
        cost_estimate=pl.CostEstimate(
            flops=13 * inner * scans * channels, bytes_accessed=3 << 20, transcendentals=0
        ),
        name="smooth_inner",
    )(frames)


def smooth_edges(left, frames, right):
    count, scans, channels = frames.shape
    step = 64
    halo_spec = pl.BlockSpec((RAD, step, channels), lambda i: (0, i, 0))
    return pl.pallas_call(
        smooth_edges_body,
        grid=(scans // step,),
        in_specs=[
            halo_spec,
            pl.BlockSpec((count, step, channels), lambda i: (0, i, 0)),
            halo_spec,
        ],
        out_specs=pl.BlockSpec((2 * RAD, step, channels), lambda i: (0, i, 0)),
        out_shape=jax.ShapeDtypeStruct((2 * RAD, scans, channels), jnp.bfloat16),
        cost_estimate=pl.CostEstimate(
            flops=13 * 8 * scans * channels, bytes_accessed=4 << 20, transcendentals=0
        ),
        name="smooth_edges",
    )(left, frames, right)


def wavelet_body(kernels_ref, own_ref, other_ref, out_ref):
    count, half, _ = own_ref.shape
    rows = kernels_ref.shape[0]

    def frame(f, carry):
        cells = jnp.concatenate([own_ref[f], other_ref[f]], axis=0)
        for r in range(0, rows, TILE_ROWS):
            out_ref[f, r : r + TILE_ROWS, :] = jnp.dot(
                kernels_ref[r : r + TILE_ROWS, :], cells, preferred_element_type=jnp.float32
            ).astype(jnp.bfloat16)
        return carry

    lax.fori_loop(0, count, frame, 0, unroll=2)


def wavelets(kernels, own, other):
    count, half, channels = own.shape
    rows = kernels.shape[0]
    whole = pl.BlockSpec(memory_space=pltpu.VMEM)
    return pl.pallas_call(
        wavelet_body,
        in_specs=[whole] * 3,
        out_specs=whole,
        out_shape=jax.ShapeDtypeStruct((count, rows, channels), jnp.bfloat16),
        cost_estimate=pl.CostEstimate(
            flops=2 * count * rows * 2 * half * channels,
            bytes_accessed=10 << 20,
            transcendentals=0,
        ),
        compiler_params=pltpu.CompilerParams(vmem_limit_bytes=24 << 20),
        name="wavelets",
    )(kernels, own, other)


def gather_rows_body(*refs):
    *parts, out_ref, sems = refs
    copies = []
    first = 0
    for i, part in enumerate(parts):
        count = part.shape[0]
        copies.append(
            pltpu.make_async_copy(part, out_ref.at[pl.ds(first, count), :], sems.at[i])
        )
        first += count
    for copy in copies:
        copy.start()
    for copy in copies:
        copy.wait()


def gather_rows(parts):
    anywhere = pl.BlockSpec(memory_space=pl.ANY)
    rows = sum(part.shape[0] for part in parts)
    return pl.pallas_call(
        gather_rows_body,
        in_specs=[anywhere] * len(parts),
        out_specs=anywhere,
        out_shape=jax.ShapeDtypeStruct((rows, parts[0].shape[1]), parts[0].dtype),
        scratch_shapes=[pltpu.SemaphoreType.DMA((len(parts),))],
        name="gather_rows",
    )(*parts)


def score_body(slots, unit, refs_in):
    (block_sm, tile_sm, place_sm, inner_ref, edges_ref, owner_ref, own_ref) = refs_in[:7]
    piece_refs = refs_in[7:15]
    out_ref, panel, totals, pass_tile, pass_slot, slot_row, sems = refs_in[15:]
    live = place_sm[0]
    section_index, grp, dev = place_sm[1], place_sm[2], place_sm[3]
    own_rows = own_ref.shape[0]
    devs = PREC // own_rows
    quarter = own_rows // GROUPS
    pair_rows = (devs - 1) // 2 * quarter
    units = PB // unit
    tiles = inner_ref.shape[1] // TILE_ROWS

    def unit_copy(source, slot, u):
        row = pl.multiple_of(slot_row[slot] + u * unit, unit)
        return pltpu.make_async_copy(source, panel.at[pl.ds(row, unit), :], sems.at[slot, u])

    def fetch(slot):
        for u in range(units):
            row = block_sm[slot] * PB + u * unit
            owner = row // own_rows
            within = row - owner * own_rows
            part = within // quarter
            offset = within - part * quarter
            from_dev = jnp.bitwise_xor(dev, owner)
            from_grp = jnp.bitwise_xor(grp, part)
            halved = (from_dev == devs - 1) & ((devs - 1) % 2 == 1)
            late = offset // (quarter // 2)
            core = jnp.where(halved, late, (from_dev - 1) % 2)
            at = jnp.where(
                halved,
                pair_rows + offset - late * (quarter // 2),
                (from_dev - 1) // 2 * quarter + offset,
            )
            crossed = (core == 1) & ((from_grp == 1) | (from_grp == 2))
            piece = jnp.where(crossed, 3 - from_grp, from_grp)
            piece = piece + GROUPS * jnp.bitwise_xor(section_index, core)

            @pl.when(from_dev == 0)
            def _():
                unit_copy(
                    own_ref.at[pl.ds(pl.multiple_of(within, unit), unit), :], slot, u
                ).start()

            for p in range(2 * GROUPS):

                @pl.when((from_dev > 0) & (piece == p))
                def _():
                    unit_copy(
                        piece_refs[p].at[pl.ds(pl.multiple_of(at, unit), unit), :], slot, u
                    ).start()

    panel[...] = jnp.zeros_like(panel)
    totals[...] = jnp.zeros_like(totals)

    def of_tile(tile, passes):
        def look(slot, state):
            at_pass, filled = state
            match = tile_sm[slot] == tile

            @pl.when(match)
            def _():
                pass_tile[at_pass] = tile
                slot_row[slot] = at_pass * 2 * PB + filled * PB
                fetch(slot)

            full = match & (filled == 1)
            return (
                at_pass + full.astype(jnp.int32),
                jnp.where(match, 1 - filled, filled),
            )

        at_pass, filled = lax.fori_loop(0, live, look, (passes, jnp.int32(0)))
        return at_pass + filled

    passes = lax.fori_loop(0, tiles, of_tile, jnp.int32(0))

    def arrive(slot, carry):
        for u in range(units):
            unit_copy(own_ref.at[pl.ds(0, unit), :], slot, u).wait()
        return carry

    lax.fori_loop(0, live, arrive, 0)

    def visit(at_pass, carry):
        at = pl.ds(pl.multiple_of(pass_tile[at_pass] * TILE_ROWS, TILE_ROWS), TILE_ROWS)
        blocks = panel[pl.ds(pl.multiple_of(at_pass * 2 * PB, 2 * PB), 2 * PB), :]
        added = jnp.zeros((8, 2 * PB), jnp.float32)
        for cells_ref in (inner_ref, edges_ref):
            for f in range(cells_ref.shape[0]):
                scores = lax.dot_general(
                    cells_ref[f, at, :],
                    blocks,
                    (((1,), (1,)), ((), ())),
                    preferred_element_type=jnp.float32,
                )
                added = added + jnp.sum(
                    jnp.maximum(scores, 0.0).reshape(TILE_ROWS // 8, 8, 2 * PB), axis=0
                )
        totals[2 * at_pass] = added[:, :PB]
        totals[2 * at_pass + 1] = added[:, PB:]
        return carry

    lax.fori_loop(0, passes, visit, 0)

    cells = (inner_ref.shape[0] + edges_ref.shape[0]) * TILE_ROWS
    high_index = lax.broadcasted_iota(jnp.int32, (BLOCKS, PB), 0)
    low_index = lax.broadcasted_iota(jnp.int32, (LANES, PB), 0)
    out_ref[...] = jnp.zeros_like(out_ref)

    def place(slot, response_total):
        total = totals[slot_row[slot] // PB]
        response = jnp.sum(total, axis=0, keepdims=True) / cells
        owner = owner_ref[pl.ds(block_sm[slot], 1), :]
        high = jnp.where(high_index == owner // LANES, response, 0.0)
        low = (low_index == owner % LANES).astype(jnp.bfloat16)
        added = out_ref[:BLOCKS, :]
        for _ in range(3):
            part = high.astype(jnp.bfloat16)
            high = high - part.astype(jnp.float32)
            added = added + lax.dot_general(
                part, low, (((1,), (1,)), ((), ())), preferred_element_type=jnp.float32
            )
        out_ref[:BLOCKS, :] = added
        return response_total + response

    response_total = lax.fori_loop(0, live, place, jnp.zeros((1, PB), jnp.float32))
    out_ref[BLOCKS:, :] = jnp.broadcast_to(
        jnp.sum(response_total, axis=1, keepdims=True), (8, LANES)
    )


def score(block_ids, tile_ids, place, inner, edges, owner_order, own_templates, pieces):
    slots = block_ids.shape[0]
    own_rows, channels = own_templates.shape
    unit = min(own_rows // (2 * GROUPS), PB)
    count, rows, _ = inner.shape
    tiles = rows // TILE_ROWS
    passes = (slots + tiles) // 2
    smem = pl.BlockSpec(memory_space=pltpu.SMEM)
    anywhere = pl.BlockSpec(memory_space=pl.ANY)
    whole = pl.BlockSpec(memory_space=pltpu.VMEM)

    def body(*refs):
        score_body(slots, unit, refs)

    return pl.pallas_call(
        body,
        in_specs=[smem, smem, smem, whole, whole, whole, anywhere] + [anywhere] * len(pieces),
        out_specs=whole,
        out_shape=jax.ShapeDtypeStruct((BLOCKS + 8, LANES), jnp.float32),
        scratch_shapes=[
            pltpu.VMEM((passes * 2 * PB, channels), jnp.bfloat16),
            pltpu.VMEM((passes * 2, 8, PB), jnp.float32),
            pltpu.SMEM((passes,), jnp.int32),
            pltpu.SMEM((slots,), jnp.int32),
            pltpu.SMEM((slots,), jnp.int32),
            pltpu.SemaphoreType.DMA((slots, PB // unit)),
        ],
        cost_estimate=pl.CostEstimate(
            flops=2 * slots * 2 * count * TILE_ROWS * PB * channels,
            bytes_accessed=14 << 20,
            transcendentals=0,
        ),
        compiler_params=pltpu.CompilerParams(vmem_limit_bytes=24 << 20),
        name="score",
    )(block_ids, tile_ids, place, inner, edges, owner_order, own_templates, *pieces)


def on_device(frames, templates, pair_block, pair_tile, pair_count, owner_order):
    section_index = lax.axis_index("section")
    grp = lax.axis_index("grp")
    dev = lax.axis_index("dev")
    devs = lax.axis_size("dev")
    groups = lax.axis_size("grp")
    own_frames = frames[0]
    mob_local = own_frames.shape[1]

    quarter = templates.shape[0] // groups
    own_quarter = lax.dynamic_slice_in_dim(templates, grp * quarter, quarter, 0)
    arrived = []
    for k in range(1, devs - 1, 2):
        arrived.append(split_swap(own_quarter, "dev", k, k + 1))
    if devs % 2 == 0:
        own_half = lax.dynamic_slice_in_dim(
            templates, grp * quarter + section_index * (quarter // 2), quarter // 2, 0
        )
        arrived.append(swap(own_half, "dev", devs - 1))
    remote = gather_rows(arrived)

    last = devs - 1
    left = lax.ppermute(
        own_frames[own_frames.shape[0] - RAD :], "dev", [(i, i + 1) for i in range(last)]
    )
    right = lax.ppermute(own_frames[:RAD], "dev", [(i + 1, i) for i in range(last)])

    inner_own = smooth_inner(own_frames)
    inner_other = swap(inner_own, "section", 1)
    kernels = mobility_kernels(section_index, mob_local)
    inner = wavelets(kernels, inner_own, inner_other)

    first = split_swap(remote, "grp", 1, 2)
    second = split_swap(remote, "grp", 2, 1)
    relayed = split_swap(first, "grp", 2, 1)
    mine = [remote, first, second, relayed]
    pieces = mine + [swap(piece, "section", 1) for piece in mine]

    edges_own = smooth_edges(left, own_frames, right)
    edges_other = swap(edges_own, "section", 1)
    edges = wavelets(kernels, edges_own, edges_other)

    place = jnp.stack([pair_count[0, 0, 0], section_index, grp, dev])
    contribution = score(
        pair_block[0, 0],
        pair_tile[0, 0],
        place,
        inner,
        edges,
        owner_order.reshape(BLOCKS, PB),
        templates,
        pieces,
    )
    both = contribution + swap(contribution, "section", 1)
    rows = BLOCKS // devs
    tail = both[BLOCKS:]

    def slice_for(target):
        return jnp.concatenate([lax.dynamic_slice_in_dim(both, target * rows, rows, 0), tail])

    owned = slice_for(dev)
    for k in range(1, devs):
        owned = owned + swap(slice_for(jnp.bitwise_xor(dev, k)), "dev", k)
    run_total = owned[rows:]
    all_total = run_total
    for j in range(1, groups):
        all_total = all_total + swap(run_total, "grp", j)
    factor = (all_total[:1, :1] / groups) / run_total[:1, :1]
    return (owned[:rows] * factor).reshape(1, rows * LANES)


def solution(mesh):
    placed = (
        P("grp", "dev", "section", None),
        P("dev", None),
        P("section", "grp", "dev"),
        P("section", "grp", "dev"),
        P("section", "grp", "dev"),
        P(),
    )
    return jax.shard_map(
        on_device, mesh=mesh, in_specs=placed, out_specs=P("grp", "dev"), check_vma=False
    )
```

```python
import math

import jax
import jax.numpy as jnp
from jax import lax
from jax.experimental import pallas as pl
from jax.experimental.pallas import tpu as pltpu
from jax.sharding import PartitionSpec as P

MOB = 512
SCALES = 6
RAD = 4
TM = 64
PB = 128
PREC = 8192
LANES = 128
TILE_ROWS = SCALES * TM
BLOCKS = PREC // PB
GROUPS = 4
WHOLE = pl.BlockSpec(memory_space=pltpu.VMEM)
ANYWHERE = pl.BlockSpec(memory_space=pl.ANY)
FAR = pl.BlockSpec(memory_space=pltpu.HBM)
SCALARS = pl.BlockSpec(memory_space=pltpu.SMEM)
BRIEF = pl.CostEstimate(flops=1024, bytes_accessed=1024, transcendentals=0)
SMALL = pltpu.CompilerParams(vmem_limit_bytes=4 << 20)

retention_spread = 2.0


def swap(cells, axis, distance):
    count = lax.axis_size(axis)
    return lax.ppermute(cells, axis, [(i, i ^ distance) for i in range(count)])


def split_swap(cells, axis, distance, other_distance):
    count = lax.axis_size(axis)
    pairs = [(i, i ^ distance) for i in range(count)]
    pairs += [(count + i, count + (i ^ other_distance)) for i in range(count)]
    return lax.ppermute(cells, ("section", axis), pairs)


def retention_weights():
    bell_values = [
        math.exp(-0.5 * (offset / retention_spread) ** 2) for offset in range(-RAD, RAD + 1)
    ]
    bell_total = sum(bell_values)
    return [weight_value / bell_total for weight_value in bell_values]


def mobility_rows(section_index, out_ref):
    mob_local = out_ref.shape[1] // 2

    def tile(t, carry):
        first_row = section_index * mob_local + t * TM
        row_place = first_row + lax.broadcasted_iota(jnp.int32, (TM, LANES), 0)
        for column in range(0, 2 * mob_local, LANES):
            owner = jnp.bitwise_xor(section_index, column // mob_local)
            col_place = (
                lax.broadcasted_iota(jnp.int32, (TM, LANES), 1)
                + column % mob_local
                + owner * mob_local
            )
            distance = (row_place - col_place).astype(jnp.float32)
            for level in range(SCALES):
                spread_scans = 2.0**level
                scaled = distance * (1.0 / spread_scans)
                value = (
                    (1.0 - scaled * scaled)
                    * jnp.exp(-0.5 * scaled * scaled)
                    / math.sqrt(0.75 * math.sqrt(math.pi) * spread_scans)
                )
                row = pl.multiple_of(t * TILE_ROWS + level * TM, TM)
                out_ref[pl.ds(row, TM), column : column + LANES] = value.astype(jnp.bfloat16)
        return carry

    lax.fori_loop(0, out_ref.shape[0] // TILE_ROWS, tile, 0)


def weighted(rows, at):
    weights = retention_weights()
    total = weights[RAD] * rows[at]
    for offset in range(1, RAD + 1):
        total = total + weights[RAD + offset] * (rows[at - offset] + rows[at + offset])
    return total.astype(jnp.bfloat16)


def prepare_body(place_sm, frames_ref, out_ref, held_ref, head_ref, tail_ref, kernels_ref):
    count, scans, channels = frames_ref.shape
    held_ref[...] = frames_ref[...]
    head_ref[...] = frames_ref[:RAD]
    tail_ref[...] = frames_ref[count - RAD :]
    mobility_rows(place_sm[0], kernels_ref)
    for r in range(0, scans, 16):
        for c in range(0, channels, LANES):
            at = (slice(r, r + 16), slice(c, c + LANES))
            rows = [frames_ref[f, at[0], at[1]].astype(jnp.float32) for f in range(count)]
            for f in range(RAD, count - RAD):
                out_ref[f - RAD, at[0], at[1]] = weighted(rows, f)


def smooth_edges_body(left_ref, frames_ref, right_ref, mark_ref, head_ref, tail_ref):
    count, scans, channels = frames_ref.shape
    for r in range(0, scans, 16):
        for c in range(0, channels, LANES):
            at = (slice(r, r + 16), slice(c, c + LANES))

            def cells(ref, first, last):
                return [ref[f, at[0], at[1]].astype(jnp.float32) for f in range(first, last)]

            head = cells(left_ref, 0, RAD) + cells(frames_ref, 0, 2 * RAD)
            for f in range(RAD):
                head_ref[f, at[0], at[1]] = weighted(head, f + RAD)
            tail = cells(frames_ref, count - 2 * RAD, count) + cells(right_ref, 0, RAD)
            for f in range(RAD):
                tail_ref[f, at[0], at[1]] = weighted(tail, f + RAD)


def prepare(place, frames):
    count, scans, channels = frames.shape
    return pl.pallas_call(
        prepare_body,
        in_specs=[SCALARS, WHOLE],
        out_specs=[WHOLE] * 5,
        out_shape=[
            jax.ShapeDtypeStruct((rows, scans, channels), jnp.bfloat16)
            for rows in (count - 2 * RAD, count, RAD, RAD)
        ]
        + [jax.ShapeDtypeStruct((scans // TM * TILE_ROWS, 2 * scans), jnp.bfloat16)],
        cost_estimate=BRIEF,
        compiler_params=SMALL,
        name="prepare",
    )(place, frames)


def smooth_edges(left, frames, right, mark):
    count, scans, channels = frames.shape
    return pl.pallas_call(
        smooth_edges_body,
        in_specs=[WHOLE] * 3 + [ANYWHERE],
        out_specs=[WHOLE] * 2,
        out_shape=[jax.ShapeDtypeStruct((RAD, scans, channels), jnp.bfloat16)] * 2,
        cost_estimate=BRIEF,
        compiler_params=SMALL,
        name="smooth_edges",
    )(left, frames, right, mark)


def wavelet_body(parts, kernels_ref, *refs):
    own_refs, other_refs = refs[:parts], refs[parts : 2 * parts]
    out_ref, mark_ref = refs[2 * parts :]
    mark_ref[...] = jnp.zeros_like(mark_ref)
    rows = kernels_ref.shape[0]

    for part in range(parts):
        count = own_refs[part].shape[0]

        def frame(f, carry):
            cells = jnp.concatenate([own_refs[part][f], other_refs[part][f]], axis=0)
            for r in range(0, rows, TILE_ROWS):
                out_ref[part * count + f, r : r + TILE_ROWS, :] = jnp.dot(
                    kernels_ref[r : r + TILE_ROWS, :], cells, preferred_element_type=jnp.float32
                ).astype(jnp.bfloat16)
            return carry

        lax.fori_loop(0, count, frame, 0, unroll=2)


def wavelets(kernels, own, other):
    parts = len(own)
    count, half, channels = own[0].shape
    rows = kernels.shape[0]

    def body(*refs):
        wavelet_body(parts, *refs)

    return pl.pallas_call(
        body,
        in_specs=[WHOLE] * (1 + 2 * parts),
        out_specs=[WHOLE] * 2,
        out_shape=[
            jax.ShapeDtypeStruct((parts * count, rows, channels), jnp.bfloat16),
            jax.ShapeDtypeStruct((8, LANES), jnp.float32),
        ],
        cost_estimate=BRIEF,
        compiler_params=SMALL,
        name="wavelets",
    )(kernels, *own, *other)


def gather_rows_body(parts, *refs):
    out_ref = refs[-1]
    first = 0
    for part_ref in refs[:parts]:
        count = part_ref.shape[0]
        out_ref[first : first + count, :] = part_ref[...]
        first += count


def gather_rows(parts, passed):
    rows = sum(part.shape[0] for part in parts)

    def body(*refs):
        gather_rows_body(len(parts), *refs)

    return pl.pallas_call(
        body,
        in_specs=[WHOLE] * len(parts) + [ANYWHERE] * len(passed),
        out_specs=[ANYWHERE] * len(passed) + [WHOLE],
        out_shape=[jax.ShapeDtypeStruct(array.shape, array.dtype) for array in passed]
        + [jax.ShapeDtypeStruct((rows, parts[0].shape[1]), parts[0].dtype)],
        input_output_aliases={len(parts) + i: i for i in range(len(passed))},
        cost_estimate=BRIEF,
        compiler_params=SMALL,
        name="gather_rows",
    )(*parts, *passed)


def join_body(one_ref, two_ref, after_ref, out_ref, mark_ref):
    rows = one_ref.shape[0]
    out_ref[:rows, :] = one_ref[...]
    out_ref[rows:, :] = two_ref[...]
    mark_ref[...] = jnp.zeros_like(mark_ref)


def join(one, two, after):
    rows, channels = one.shape
    return pl.pallas_call(
        join_body,
        in_specs=[WHOLE] * 2 + [ANYWHERE],
        out_specs=[WHOLE] * 2,
        out_shape=[
            jax.ShapeDtypeStruct((2 * rows, channels), one.dtype),
            jax.ShapeDtypeStruct((8, LANES), jnp.float32),
        ],
        cost_estimate=BRIEF,
        compiler_params=SMALL,
        name="join",
    )(one, two, after)


def score_body(slots, unit, refs_in):
    (block_sm, tile_sm, place_sm, inner_ref, edges_ref, owner_ref, own_ref) = refs_in[:7]
    piece_refs = refs_in[7:11]
    out_ref, panel, totals, pass_tile, slot_row, sems = refs_in[12:]
    section_index, grp, dev, live = place_sm[0], place_sm[1], place_sm[2], place_sm[3]
    own_rows = own_ref.shape[0]
    devs = PREC // own_rows
    quarter = own_rows // GROUPS
    pair_rows = (devs - 1) // 2 * quarter
    units = PB // unit
    tiles = inner_ref.shape[1] // TILE_ROWS

    def unit_copy(source, slot, u):
        row = pl.multiple_of(slot_row[slot] + u * unit, unit)
        return pltpu.make_async_copy(source, panel.at[pl.ds(row, unit), :], sems.at[slot, u])

    def fetch(slot):
        for u in range(units):
            row = block_sm[slot] * PB + u * unit
            owner = row // own_rows
            within = row - owner * own_rows
            part = within // quarter
            offset = within - part * quarter
            from_dev = jnp.bitwise_xor(dev, owner)
            from_grp = jnp.bitwise_xor(grp, part)
            halved = (from_dev == devs - 1) & ((devs - 1) % 2 == 1)
            late = offset // (quarter // 2)
            core = jnp.where(halved, late, (from_dev - 1) % 2)
            at = jnp.where(
                halved,
                pair_rows + offset - late * (quarter // 2),
                (from_dev - 1) // 2 * quarter + offset,
            )
            crossed = (core == 1) & ((from_grp == 1) | (from_grp == 2))
            piece = jnp.where(crossed, 3 - from_grp, from_grp)
            at = at + (piece % 2) * (piece_refs[0].shape[0] // 2)
            piece = piece // 2 + 2 * jnp.bitwise_xor(section_index, core)

            @pl.when(from_dev == 0)
            def _():
                unit_copy(
                    own_ref.at[pl.ds(pl.multiple_of(within, unit), unit), :], slot, u
                ).start()

            for p in range(len(piece_refs)):

                @pl.when((from_dev > 0) & (piece == p))
                def _():
                    unit_copy(
                        piece_refs[p].at[pl.ds(pl.multiple_of(at, unit), unit), :], slot, u
                    ).start()

    panel[...] = jnp.zeros_like(panel)
    totals[...] = jnp.zeros_like(totals)

    def of_tile(tile, passes):
        def look(slot, state):
            at_pass, filled = state
            match = tile_sm[slot] == tile

            @pl.when(match)
            def _():
                pass_tile[at_pass] = tile
                slot_row[slot] = at_pass * 2 * PB + filled * PB
                fetch(slot)

            full = match & (filled == 1)
            return (
                at_pass + full.astype(jnp.int32),
                jnp.where(match, 1 - filled, filled),
            )

        at_pass, filled = lax.fori_loop(0, live, look, (passes, jnp.int32(0)))
        return at_pass + filled

    passes = lax.fori_loop(0, tiles, of_tile, jnp.int32(0))

    def arrive(slot, carry):
        for u in range(units):
            unit_copy(own_ref.at[pl.ds(0, unit), :], slot, u).wait()
        return carry

    lax.fori_loop(0, live, arrive, 0)

    def visit(at_pass, carry):
        at = pl.ds(pl.multiple_of(pass_tile[at_pass] * TILE_ROWS, TILE_ROWS), TILE_ROWS)
        blocks = panel[pl.ds(pl.multiple_of(at_pass * 2 * PB, 2 * PB), 2 * PB), :]
        added = jnp.zeros((8, 2 * PB), jnp.float32)
        for cells_ref in (inner_ref, edges_ref):
            for f in range(cells_ref.shape[0]):
                scores = lax.dot_general(
                    cells_ref[f, at, :],
                    blocks,
                    (((1,), (1,)), ((), ())),
                    preferred_element_type=jnp.float32,
                )
                added = added + jnp.sum(
                    jnp.maximum(scores, 0.0).reshape(TILE_ROWS // 8, 8, 2 * PB), axis=0
                )
        totals[2 * at_pass] = added[:, :PB]
        totals[2 * at_pass + 1] = added[:, PB:]
        return carry

    lax.fori_loop(0, passes, visit, 0)

    cells = (inner_ref.shape[0] + edges_ref.shape[0]) * TILE_ROWS
    high_index = lax.broadcasted_iota(jnp.int32, (BLOCKS, PB), 0)
    low_index = lax.broadcasted_iota(jnp.int32, (LANES, PB), 0)
    out_ref[...] = jnp.zeros_like(out_ref)

    def place(slot, response_total):
        total = totals[slot_row[slot] // PB]
        response = jnp.sum(total, axis=0, keepdims=True) / cells
        owner = owner_ref[pl.ds(block_sm[slot], 1), :]
        high = jnp.where(high_index == owner // LANES, response, 0.0)
        low = (low_index == owner % LANES).astype(jnp.bfloat16)
        added = out_ref[:BLOCKS, :]
        for _ in range(3):
            part = high.astype(jnp.bfloat16)
            high = high - part.astype(jnp.float32)
            added = added + lax.dot_general(
                part, low, (((1,), (1,)), ((), ())), preferred_element_type=jnp.float32
            )
        out_ref[:BLOCKS, :] = added
        return response_total + response

    response_total = lax.fori_loop(0, live, place, jnp.zeros((1, PB), jnp.float32))
    out_ref[BLOCKS:, :] = jnp.broadcast_to(
        jnp.sum(response_total, axis=1, keepdims=True), (8, LANES)
    )


def score(block_ids, tile_ids, place, inner, edges, owner_order, own_templates, pieces, mark):
    slots = block_ids.shape[0]
    own_rows, channels = own_templates.shape
    unit = min(own_rows // (2 * GROUPS), PB)
    count, rows, _ = inner.shape
    tiles = rows // TILE_ROWS
    passes = (slots + tiles) // 2

    def body(*refs):
        score_body(slots, unit, refs)

    return pl.pallas_call(
        body,
        in_specs=[SCALARS] * 3 + [WHOLE] * 3 + [ANYWHERE] * (2 + len(pieces)),
        out_specs=WHOLE,
        out_shape=jax.ShapeDtypeStruct((BLOCKS + 8, LANES), jnp.float32),
        scratch_shapes=[
            pltpu.VMEM((passes * 2 * PB, channels), jnp.bfloat16),
            pltpu.VMEM((passes * 2, 8, PB), jnp.float32),
            pltpu.SMEM((passes,), jnp.int32),
            pltpu.SMEM((slots,), jnp.int32),
            pltpu.SemaphoreType.DMA((slots, PB // unit)),
        ],
        cost_estimate=BRIEF,
        compiler_params=SMALL,
        name="score",
    )(block_ids, tile_ids, place, inner, edges, owner_order, own_templates, *pieces, mark)


def share_out_body(place_sm, mine_ref, other_ref, *out_refs):
    rows = out_refs[0].shape[0] - 8
    tail = mine_ref[BLOCKS:, :] + other_ref[BLOCKS:, :]
    for k, out_ref in enumerate(out_refs):
        target = jnp.bitwise_xor(place_sm[2], k)
        if rows % 8 == 0:
            at = pl.ds(pl.multiple_of(target * rows, 8), rows)
        else:
            at = pl.ds(target * rows, rows)
        out_ref[:rows, :] = mine_ref[at, :] + other_ref[at, :]
        out_ref[rows:, :] = tail


def share_out(place, mine, other, devs):
    rows = BLOCKS // devs + 8
    return pl.pallas_call(
        share_out_body,
        in_specs=[SCALARS, WHOLE, WHOLE],
        out_specs=[WHOLE] * devs,
        out_shape=[jax.ShapeDtypeStruct((rows, LANES), jnp.float32)] * devs,
        cost_estimate=BRIEF,
        compiler_params=SMALL,
        name="share_out",
    )(place, mine, other)


def collect_body(*refs):
    *part_refs, owned_ref, total_ref = refs
    rows = owned_ref.shape[0]
    owned = part_refs[0][...]
    for part_ref in part_refs[1:]:
        owned = owned + part_ref[...]
    owned_ref[...] = owned[:rows]
    total_ref[...] = owned[rows:]


def collect(parts):
    rows = parts[0].shape[0] - 8
    return pl.pallas_call(
        collect_body,
        in_specs=[WHOLE] * len(parts),
        out_specs=[WHOLE] * 2,
        out_shape=[
            jax.ShapeDtypeStruct((rows, LANES), jnp.float32),
            jax.ShapeDtypeStruct((8, LANES), jnp.float32),
        ],
        cost_estimate=BRIEF,
        compiler_params=SMALL,
        name="collect",
    )(*parts)


def normalize_body(owned_ref, *refs):
    *total_refs, out_ref = refs
    everything = total_refs[0][...]
    for total_ref in total_refs[1:]:
        everything = everything + total_ref[...]
    factor = (everything / len(total_refs)) / total_refs[0][...]
    out_ref[...] = owned_ref[...] * factor[:1, :]


def normalize(owned, totals):
    return pl.pallas_call(
        normalize_body,
        in_specs=[WHOLE] * (1 + len(totals)),
        out_specs=WHOLE,
        out_shape=jax.ShapeDtypeStruct(owned.shape, jnp.float32),
        cost_estimate=BRIEF,
        compiler_params=SMALL,
        name="normalize",
    )(owned, *totals)


def on_device(frames, templates, pair_block, pair_tile, pair_count, owner_order):
    section_index = lax.axis_index("section")
    grp = lax.axis_index("grp")
    dev = lax.axis_index("dev")
    devs = lax.axis_size("dev")
    groups = lax.axis_size("grp")
    own_frames = frames[0]
    place = jnp.stack([section_index, grp, dev, pair_count[0, 0, 0]])

    quarter = templates.shape[0] // groups
    own_quarter = lax.dynamic_slice_in_dim(templates, grp * quarter, quarter, 0)
    own_half = lax.dynamic_slice_in_dim(
        templates, grp * quarter + section_index * (quarter // 2), quarter // 2, 0
    )
    arrived = []
    for k in range(1, devs - 1, 2):
        arrived.append(split_swap(own_quarter, "dev", k, k + 1))
    if devs % 2 == 0:
        arrived.append(swap(own_half, "dev", devs - 1))

    inner_own, held, head, tail, kernels = prepare(place, own_frames)
    inner_own, head, tail, remote = gather_rows(arrived, [inner_own, head, tail])
    inner_other = swap(inner_own, "section", 1)
    first = split_swap(remote, "grp", 1, 2)
    last = devs - 1
    left = lax.ppermute(tail, "dev", [(i, i + 1) for i in range(last)])
    right = lax.ppermute(head, "dev", [(i + 1, i) for i in range(last)])

    inner, inner_mark = wavelets(kernels, [inner_own], [inner_other])
    near, near_mark = join(remote, first, inner_mark)
    far = split_swap(near, "grp", 2, 1)
    edges_own = smooth_edges(left, held, right, near_mark)
    edges_other = [swap(edge, "section", 1) for edge in edges_own]
    edges, edges_mark = wavelets(kernels, edges_own, edges_other)
    far, edges_mark = lax.optimization_barrier((far, edges_mark))
    mine = [near, far]
    pieces = mine + [swap(piece, "section", 1) for piece in mine]

    contribution = score(
        pair_block[0, 0],
        pair_tile[0, 0],
        place,
        inner,
        edges,
        owner_order.reshape(BLOCKS, PB),
        templates,
        pieces,
        edges_mark,
    )
    outgoing = share_out(place, contribution, swap(contribution, "section", 1), devs)
    owned, run_total = collect(
        [outgoing[0]] + [swap(outgoing[k], "dev", k) for k in range(1, devs)]
    )
    totals = [run_total] + [swap(run_total, "grp", j) for j in range(1, groups)]
    return normalize(owned, totals).reshape(1, -1)


def solution(mesh):
    placed = (
        P("grp", "dev", "section", None),
        P("dev", None),
        P("section", "grp", "dev"),
        P("section", "grp", "dev"),
        P("section", "grp", "dev"),
        P(),
    )
    return jax.shard_map(
        on_device, mesh=mesh, in_specs=placed, out_specs=P("grp", "dev"), check_vma=False
    )
```

```python
import math

import jax
import jax.numpy as jnp
from jax import lax
from jax.experimental import pallas as pl
from jax.experimental.pallas import tpu as pltpu
from jax.sharding import PartitionSpec as P

MOB = 512
SCALES = 6
RAD = 4
TM = 64
PB = 128
PREC = 8192
LANES = 128
TILE_ROWS = SCALES * TM
BLOCKS = PREC // PB
GROUPS = 4
WHOLE = pl.BlockSpec(memory_space=pltpu.VMEM)
ANYWHERE = pl.BlockSpec(memory_space=pl.ANY)
FAR = pl.BlockSpec(memory_space=pltpu.HBM)
SCALARS = pl.BlockSpec(memory_space=pltpu.SMEM)
BRIEF = pl.CostEstimate(flops=1024, bytes_accessed=1024, transcendentals=0)
EDGE_PAD = 32
SMALL = pltpu.CompilerParams(vmem_limit_bytes=4 << 20)

retention_spread = 2.0


def swap(cells, axis, distance):
    count = lax.axis_size(axis)
    return lax.ppermute(cells, axis, [(i, i ^ distance) for i in range(count)])


def split_swap(cells, axis, distance, other_distance):
    count = lax.axis_size(axis)
    pairs = [(i, i ^ distance) for i in range(count)]
    pairs += [(count + i, count + (i ^ other_distance)) for i in range(count)]
    return lax.ppermute(cells, ("section", axis), pairs)


def retention_weights():
    bell_values = [
        math.exp(-0.5 * (offset / retention_spread) ** 2) for offset in range(-RAD, RAD + 1)
    ]
    bell_total = sum(bell_values)
    return [weight_value / bell_total for weight_value in bell_values]


def mobility_rows(section_index, out_ref):
    mob_local = out_ref.shape[1] // 2

    def tile(t, carry):
        first_row = section_index * mob_local + t * TM
        row_place = first_row + lax.broadcasted_iota(jnp.int32, (TM, LANES), 0)
        for column in range(0, 2 * mob_local, LANES):
            owner = jnp.bitwise_xor(section_index, column // mob_local)
            col_place = (
                lax.broadcasted_iota(jnp.int32, (TM, LANES), 1)
                + column % mob_local
                + owner * mob_local
            )
            distance = (row_place - col_place).astype(jnp.float32)
            for level in range(SCALES):
                spread_scans = 2.0**level
                scaled = distance * (1.0 / spread_scans)
                value = (
                    (1.0 - scaled * scaled)
                    * jnp.exp(-0.5 * scaled * scaled)
                    / math.sqrt(0.75 * math.sqrt(math.pi) * spread_scans)
                )
                row = pl.multiple_of(t * TILE_ROWS + level * TM, TM)
                out_ref[pl.ds(row, TM), column : column + LANES] = value.astype(jnp.bfloat16)
        return carry

    lax.fori_loop(0, out_ref.shape[0] // TILE_ROWS, tile, 0)


def weighted(rows, at):
    weights = retention_weights()
    total = weights[RAD] * rows[at]
    for offset in range(1, RAD + 1):
        total = total + weights[RAD + offset] * (rows[at - offset] + rows[at + offset])
    return total.astype(jnp.bfloat16)


def prepare_body(own_ref, other_ref, *out_refs):
    own_out_ref, other_out_ref, held_ref, near_ref, far_ref, kernels_ref = out_refs
    count, scans, channels = own_ref.shape
    held_ref[...] = own_ref[...]
    even = 1 - lax.axis_index("dev") % 2
    near_ref[:, :scans, :] = own_ref[pl.ds(even * (count - RAD), RAD)]
    far_ref[:, :scans, :] = own_ref[pl.ds((1 - even) * (count - RAD), RAD)]
    for edge_ref in (near_ref, far_ref):
        edge_ref[:, scans:, :] = jnp.zeros((RAD, EDGE_PAD, channels), edge_ref.dtype)
    mobility_rows(lax.axis_index("section"), kernels_ref)
    for frames_ref, out_ref in ((own_ref, own_out_ref), (other_ref, other_out_ref)):
        for r in range(0, scans, 16):
            for c in range(0, channels, LANES):
                at = (slice(r, r + 16), slice(c, c + LANES))
                rows = [frames_ref[f, at[0], at[1]].astype(jnp.float32) for f in range(count)]
                for f in range(RAD, count - RAD):
                    out_ref[f - RAD, at[0], at[1]] = weighted(rows, f)


def smooth_edges_body(near_ref, frames_ref, far_ref, mark_ref, head_ref, tail_ref):
    count, scans, channels = frames_ref.shape

    def smooth(left_ref, right_ref):
        def some_scans(step, carry):
            for r in range(0, 64, 16):
                for c in range(0, channels, LANES):
                    at = (pl.ds(pl.multiple_of(step * 64 + r, 16), 16), slice(c, c + LANES))

                    def cells(ref, first, last):
                        return [
                            ref[f, at[0], at[1]].astype(jnp.float32) for f in range(first, last)
                        ]

                    head = cells(left_ref, 0, RAD) + cells(frames_ref, 0, 2 * RAD)
                    for f in range(RAD):
                        head_ref[f, at[0], at[1]] = weighted(head, f + RAD)
                    tail = cells(frames_ref, count - 2 * RAD, count) + cells(right_ref, 0, RAD)
                    for f in range(RAD):
                        tail_ref[f, at[0], at[1]] = weighted(tail, f + RAD)
            return carry

        lax.fori_loop(0, scans // 64, some_scans, 0)

    @pl.when(lax.axis_index("dev") % 2 == 0)
    def _():
        smooth(far_ref, near_ref)

    @pl.when(lax.axis_index("dev") % 2 == 1)
    def _():
        smooth(near_ref, far_ref)


def prepare(own, other):
    count, scans, channels = own.shape
    inner = count - 2 * RAD
    return pl.pallas_call(
        prepare_body,
        in_specs=[WHOLE] * 2,
        out_specs=[WHOLE] * 6,
        out_shape=[
            jax.ShapeDtypeStruct((rows, scans, channels), jnp.bfloat16)
            for rows in (inner, inner, count)
        ]
        + [jax.ShapeDtypeStruct((RAD, scans + EDGE_PAD, channels), jnp.bfloat16)] * 2
        + [jax.ShapeDtypeStruct((scans // TM * TILE_ROWS, 2 * scans), jnp.bfloat16)],
        cost_estimate=BRIEF,
        compiler_params=SMALL,
        name="prepare",
    )(own, other)


def smooth_edges(near, frames, far, mark):
    count, scans, channels = frames.shape
    return pl.pallas_call(
        smooth_edges_body,
        in_specs=[WHOLE] * 3 + [ANYWHERE],
        out_specs=[WHOLE] * 2,
        out_shape=[jax.ShapeDtypeStruct((RAD, scans, channels), jnp.bfloat16)] * 2,
        cost_estimate=BRIEF,
        compiler_params=SMALL,
        name="smooth_edges",
    )(near, frames, far, mark)


def wavelet_body(kernels_ref, own_ref, other_ref, after_ref, out_ref, mark_ref):
    mark_ref[...] = jnp.zeros_like(mark_ref)
    rows = kernels_ref.shape[0]

    def frame(f, carry):
        cells = jnp.concatenate([own_ref[f], other_ref[f]], axis=0)
        for r in range(0, rows, TILE_ROWS):
            out_ref[f, r : r + TILE_ROWS, :] = jnp.dot(
                kernels_ref[r : r + TILE_ROWS, :], cells, preferred_element_type=jnp.float32
            ).astype(jnp.bfloat16)
        return carry

    lax.fori_loop(0, out_ref.shape[0], frame, 0, unroll=2)


def wavelets(kernels, own, other, after):
    count, half, channels = own.shape
    rows = kernels.shape[0]
    return pl.pallas_call(
        wavelet_body,
        in_specs=[WHOLE] * 3 + [ANYWHERE],
        out_specs=[WHOLE] * 2,
        out_shape=[
            jax.ShapeDtypeStruct((count, rows, channels), jnp.bfloat16),
            jax.ShapeDtypeStruct((8, LANES), jnp.float32),
        ],
        cost_estimate=BRIEF,
        compiler_params=SMALL,
        name="wavelets",
    )(kernels, own, other, after)


def gather_rows_body(parts, *refs):
    out_ref = refs[-1]
    first = 0
    for part_ref in refs[:parts]:
        count = part_ref.shape[0]
        out_ref[first : first + count, :] = part_ref[...]
        first += count


def gather_rows(parts, passed):
    rows = sum(part.shape[0] for part in parts)

    def body(*refs):
        gather_rows_body(len(parts), *refs)

    return pl.pallas_call(
        body,
        in_specs=[WHOLE] * len(parts) + [ANYWHERE] * len(passed),
        out_specs=[ANYWHERE] * len(passed) + [WHOLE],
        out_shape=[jax.ShapeDtypeStruct(array.shape, array.dtype) for array in passed]
        + [jax.ShapeDtypeStruct((rows, parts[0].shape[1]), parts[0].dtype)],
        input_output_aliases={len(parts) + i: i for i in range(len(passed))},
        cost_estimate=BRIEF,
        compiler_params=SMALL,
        name="gather_rows",
    )(*parts, *passed)


def join_body(one_ref, two_ref, after_ref, out_ref, mark_ref):
    rows = one_ref.shape[0]
    out_ref[:rows, :] = one_ref[...]
    out_ref[rows:, :] = two_ref[...]
    mark_ref[...] = jnp.zeros_like(mark_ref)


def join(one, two, after):
    rows, channels = one.shape
    return pl.pallas_call(
        join_body,
        in_specs=[WHOLE] * 2 + [ANYWHERE],
        out_specs=[WHOLE] * 2,
        out_shape=[
            jax.ShapeDtypeStruct((2 * rows, channels), one.dtype),
            jax.ShapeDtypeStruct((8, LANES), jnp.float32),
        ],
        cost_estimate=BRIEF,
        compiler_params=SMALL,
        name="join",
    )(one, two, after)


def score_body(slots, unit, refs_in):
    block_sm, tile_sm, live_sm, *stack_refs, owner_ref, own_ref = refs_in[:8]
    piece_refs = refs_in[8:12]
    out_ref, panel, totals, pass_tile, slot_row, sems = refs_in[13:]
    live = live_sm[0]
    section_index, grp, dev = (lax.axis_index(axis) for axis in ("section", "grp", "dev"))
    own_rows = own_ref.shape[0]
    devs = PREC // own_rows
    quarter = own_rows // GROUPS
    pair_rows = (devs - 1) // 2 * quarter
    units = PB // unit
    tiles = stack_refs[0].shape[1] // TILE_ROWS

    def unit_copy(source, slot, u):
        row = pl.multiple_of(slot_row[slot] + u * unit, unit)
        return pltpu.make_async_copy(source, panel.at[pl.ds(row, unit), :], sems.at[slot, u])

    def fetch(slot):
        for u in range(units):
            row = block_sm[slot] * PB + u * unit
            owner = row // own_rows
            within = row - owner * own_rows
            part = within // quarter
            offset = within - part * quarter
            from_dev = jnp.bitwise_xor(dev, owner)
            from_grp = jnp.bitwise_xor(grp, part)
            halved = (from_dev == devs - 1) & ((devs - 1) % 2 == 1)
            late = offset // (quarter // 2)
            core = jnp.where(halved, late, (from_dev - 1) % 2)
            at = jnp.where(
                halved,
                pair_rows + offset - late * (quarter // 2),
                (from_dev - 1) // 2 * quarter + offset,
            )
            crossed = (core == 1) & ((from_grp == 1) | (from_grp == 2))
            piece = jnp.where(crossed, 3 - from_grp, from_grp)
            at = at + (piece % 2) * (piece_refs[0].shape[0] // 2)
            piece = piece // 2 + 2 * jnp.bitwise_xor(section_index, core)

            @pl.when(from_dev == 0)
            def _():
                unit_copy(
                    own_ref.at[pl.ds(pl.multiple_of(within, unit), unit), :], slot, u
                ).start()

            for p in range(len(piece_refs)):

                @pl.when((from_dev > 0) & (piece == p))
                def _():
                    unit_copy(
                        piece_refs[p].at[pl.ds(pl.multiple_of(at, unit), unit), :], slot, u
                    ).start()

    panel[...] = jnp.zeros_like(panel)
    totals[...] = jnp.zeros_like(totals)

    def of_tile(tile, passes):
        def look(slot, state):
            at_pass, filled = state
            match = tile_sm[slot] == tile

            @pl.when(match)
            def _():
                pass_tile[at_pass] = tile
                slot_row[slot] = at_pass * 2 * PB + filled * PB
                fetch(slot)

            full = match & (filled == 1)
            return (
                at_pass + full.astype(jnp.int32),
                jnp.where(match, 1 - filled, filled),
            )

        at_pass, filled = lax.fori_loop(0, live, look, (passes, jnp.int32(0)))
        return at_pass + filled

    passes = lax.fori_loop(0, tiles, of_tile, jnp.int32(0))

    def arrive(slot, carry):
        for u in range(units):
            unit_copy(own_ref.at[pl.ds(0, unit), :], slot, u).wait()
        return carry

    lax.fori_loop(0, live, arrive, 0)

    def visit(at_pass, carry):
        at = pl.ds(pl.multiple_of(pass_tile[at_pass] * TILE_ROWS, TILE_ROWS), TILE_ROWS)
        blocks = panel[pl.ds(pl.multiple_of(at_pass * 2 * PB, 2 * PB), 2 * PB), :]
        added = jnp.zeros((8, 2 * PB), jnp.float32)
        for cells_ref in stack_refs:
            for f in range(cells_ref.shape[0]):
                scores = lax.dot_general(
                    cells_ref[f, at, :],
                    blocks,
                    (((1,), (1,)), ((), ())),
                    preferred_element_type=jnp.float32,
                )
                added = added + jnp.sum(
                    jnp.maximum(scores, 0.0).reshape(TILE_ROWS // 8, 8, 2 * PB), axis=0
                )
        totals[2 * at_pass] = added[:, :PB]
        totals[2 * at_pass + 1] = added[:, PB:]
        return carry

    lax.fori_loop(0, passes, visit, 0)

    cells = sum(ref.shape[0] for ref in stack_refs) * TILE_ROWS
    high_index = lax.broadcasted_iota(jnp.int32, (BLOCKS, PB), 0)
    low_index = lax.broadcasted_iota(jnp.int32, (LANES, PB), 0)
    responses, highs, lows = [], [], []
    for slot in range(slots):
        is_live = slot < live
        total = totals[jnp.where(is_live, slot_row[slot] // PB, 0)]
        response = jnp.sum(total, axis=0, keepdims=True) / cells
        response = jnp.where(is_live, response, 0.0)
        owner = owner_ref[pl.ds(block_sm[slot], 1), :]
        responses.append(response)
        highs.append(jnp.where(high_index == owner // LANES, response, 0.0))
        lows.append((low_index == owner % LANES).astype(jnp.bfloat16))
    high = jnp.concatenate(highs, axis=1)
    low = jnp.concatenate(lows, axis=1)
    placed = jnp.zeros((BLOCKS, LANES), jnp.float32)
    for _ in range(3):
        part = high.astype(jnp.bfloat16)
        high = high - part.astype(jnp.float32)
        placed = placed + lax.dot_general(
            part, low, (((1,), (1,)), ((), ())), preferred_element_type=jnp.float32
        )
    out_ref[:BLOCKS, :] = placed
    out_ref[BLOCKS:, :] = jnp.broadcast_to(
        jnp.sum(sum(responses), axis=1, keepdims=True), (8, LANES)
    )


def score(block_ids, tile_ids, live, stacks, owner_order, own_templates, pieces, mark):
    slots = block_ids.shape[0]
    own_rows, channels = own_templates.shape
    unit = min(own_rows // (2 * GROUPS), PB)
    tiles = stacks[0].shape[1] // TILE_ROWS
    passes = (slots + tiles) // 2

    def body(*refs):
        score_body(slots, unit, refs)

    return pl.pallas_call(
        body,
        in_specs=[SCALARS] * 3 + [WHOLE] * (len(stacks) + 1) + [ANYWHERE] * (2 + len(pieces)),
        out_specs=WHOLE,
        out_shape=jax.ShapeDtypeStruct((BLOCKS + 8, LANES), jnp.float32),
        scratch_shapes=[
            pltpu.VMEM((passes * 2 * PB, channels), jnp.bfloat16),
            pltpu.VMEM((passes * 2, 8, PB), jnp.float32),
            pltpu.SMEM((passes,), jnp.int32),
            pltpu.SMEM((slots,), jnp.int32),
            pltpu.SemaphoreType.DMA((slots, PB // unit)),
        ],
        cost_estimate=BRIEF,
        compiler_params=SMALL,
        name="score",
    )(block_ids, tile_ids, live, *stacks, owner_order, own_templates, *pieces, mark)


def share_out_body(mine_ref, other_ref, *out_refs):
    rows = out_refs[0].shape[0] - 8
    tail = mine_ref[BLOCKS:, :] + other_ref[BLOCKS:, :]
    for k, out_ref in enumerate(out_refs):
        target = jnp.bitwise_xor(lax.axis_index("dev"), k)
        if rows % 8 == 0:
            at = pl.ds(pl.multiple_of(target * rows, 8), rows)
        else:
            at = pl.ds(target * rows, rows)
        out_ref[:rows, :] = mine_ref[at, :] + other_ref[at, :]
        out_ref[rows:, :] = tail


def share_out(mine, other, devs):
    rows = BLOCKS // devs + 8
    return pl.pallas_call(
        share_out_body,
        in_specs=[WHOLE, WHOLE],
        out_specs=[WHOLE] * devs,
        out_shape=[jax.ShapeDtypeStruct((rows, LANES), jnp.float32)] * devs,
        cost_estimate=BRIEF,
        compiler_params=SMALL,
        name="share_out",
    )(mine, other)


def collect_body(*refs):
    *part_refs, owned_ref, total_ref = refs
    rows = owned_ref.shape[0]
    owned = part_refs[0][...]
    for part_ref in part_refs[1:]:
        owned = owned + part_ref[...]
    owned_ref[...] = owned[:rows]
    total_ref[...] = owned[rows:]


def collect(parts):
    rows = parts[0].shape[0] - 8
    return pl.pallas_call(
        collect_body,
        in_specs=[WHOLE] * len(parts),
        out_specs=[WHOLE] * 2,
        out_shape=[
            jax.ShapeDtypeStruct((rows, LANES), jnp.float32),
            jax.ShapeDtypeStruct((8, LANES), jnp.float32),
        ],
        cost_estimate=BRIEF,
        compiler_params=SMALL,
        name="collect",
    )(*parts)


def normalize_body(owned_ref, *refs):
    *total_refs, out_ref = refs
    everything = total_refs[0][...]
    for total_ref in total_refs[1:]:
        everything = everything + total_ref[...]
    factor = (everything / len(total_refs)) / total_refs[0][...]
    out_ref[...] = owned_ref[...] * factor[:1, :]


def normalize(owned, totals):
    return pl.pallas_call(
        normalize_body,
        in_specs=[WHOLE] * (1 + len(totals)),
        out_specs=WHOLE,
        out_shape=jax.ShapeDtypeStruct(owned.shape, jnp.float32),
        cost_estimate=BRIEF,
        compiler_params=SMALL,
        name="normalize",
    )(owned, *totals)


def on_device(frames, templates, pair_block, pair_tile, pair_count, owner_order):
    section_index = lax.axis_index("section")
    grp = lax.axis_index("grp")
    devs = lax.axis_size("dev")
    groups = lax.axis_size("grp")
    own_frames = frames[0]

    quarter = templates.shape[0] // groups
    own_quarter = lax.dynamic_slice_in_dim(templates, grp * quarter, quarter, 0)
    own_half = lax.dynamic_slice_in_dim(
        templates, grp * quarter + section_index * (quarter // 2), quarter // 2, 0
    )
    arrived = []
    for k in range(1, devs - 1, 2):
        arrived.append(split_swap(own_quarter, "dev", k, k + 1))
    if devs % 2 == 0:
        arrived.append(swap(own_half, "dev", devs - 1))

    other_frames = swap(own_frames, "section", 1)
    inner_own, inner_other, held, near_edge, far_edge, kernels = prepare(
        own_frames, other_frames
    )
    (remote,) = gather_rows(arrived, [])
    first = split_swap(remote, "grp", 1, 2)
    near_halo = swap(near_edge, "dev", 1)
    between = [pair for i in range(1, devs - 1, 2) for pair in ((i, i + 1), (i + 1, i))]
    far_halo = lax.ppermute(far_edge, "dev", between)

    inner, inner_mark = wavelets(kernels, inner_own, inner_other, remote)
    near, near_mark = join(remote, first, inner_mark)
    far = split_swap(near, "grp", 2, 1)
    near_other, far_other = swap(near_halo, "section", 1), swap(far_halo, "section", 1)
    head_own, tail_own = smooth_edges(near_halo, held, far_halo, near_mark)
    head_other, tail_other = smooth_edges(near_other, other_frames, far_other, near_mark)
    head, head_mark = wavelets(kernels, head_own, head_other, tail_other)
    far, head_mark = lax.optimization_barrier((far, head_mark))
    tail, _ = wavelets(kernels, tail_own, tail_other, head_mark)
    pieces = [near, far, swap(near, "section", 1), swap(far, "section", 1)]

    contribution = score(
        pair_block[0, 0],
        pair_tile[0, 0],
        pair_count[0, 0],
        [inner, head, tail],
        owner_order.reshape(BLOCKS, PB),
        templates,
        pieces,
        head_mark,
    )
    outgoing = share_out(contribution, swap(contribution, "section", 1), devs)
    owned, run_total = collect(
        [outgoing[0]] + [swap(outgoing[k], "dev", k) for k in range(1, devs)]
    )
    totals = [run_total] + [swap(run_total, "grp", j) for j in range(1, groups)]
    return normalize(owned, totals).reshape(1, -1)


def solution(mesh):
    placed = (
        P("grp", "dev", "section", None),
        P("dev", None),
        P("section", "grp", "dev"),
        P("section", "grp", "dev"),
        P("section", "grp", "dev"),
        P(),
    )
    return jax.shard_map(
        on_device, mesh=mesh, in_specs=placed, out_specs=P("grp", "dev"), check_vma=False
    )
```

```python
import math

import jax
import jax.numpy as jnp
from jax import lax
from jax.experimental import pallas as pl
from jax.experimental.pallas import tpu as pltpu
from jax.sharding import PartitionSpec as P

MOB = 512
SCALES = 6
RAD = 4
TM = 64
PB = 128
PREC = 8192
LANES = 128
TILE_ROWS = SCALES * TM
BLOCKS = PREC // PB
GROUPS = 4
WHOLE = pl.BlockSpec(memory_space=pltpu.VMEM)
ANYWHERE = pl.BlockSpec(memory_space=pl.ANY)
FAR = pl.BlockSpec(memory_space=pltpu.HBM)
SCALARS = pl.BlockSpec(memory_space=pltpu.SMEM)
BRIEF = pl.CostEstimate(flops=1024, bytes_accessed=1024, transcendentals=0)
EDGE_PAD = 32
SMALL = pltpu.CompilerParams(vmem_limit_bytes=4 << 20)

retention_spread = 2.0


def swap(cells, axis, distance):
    count = lax.axis_size(axis)
    return lax.ppermute(cells, axis, [(i, i ^ distance) for i in range(count)])


def split_swap(cells, axis, distance, other_distance):
    count = lax.axis_size(axis)
    pairs = [(i, i ^ distance) for i in range(count)]
    pairs += [(count + i, count + (i ^ other_distance)) for i in range(count)]
    return lax.ppermute(cells, ("section", axis), pairs)


def retention_weights():
    bell_values = [
        math.exp(-0.5 * (offset / retention_spread) ** 2) for offset in range(-RAD, RAD + 1)
    ]
    bell_total = sum(bell_values)
    return [weight_value / bell_total for weight_value in bell_values]


def mobility_rows(section_index, out_ref):
    mob_local = out_ref.shape[1] // 2

    def tile(t, carry):
        first_row = section_index * mob_local + t * TM
        row_place = first_row + lax.broadcasted_iota(jnp.int32, (TM, LANES), 0)
        for column in range(0, 2 * mob_local, LANES):
            owner = jnp.bitwise_xor(section_index, column // mob_local)
            col_place = (
                lax.broadcasted_iota(jnp.int32, (TM, LANES), 1)
                + column % mob_local
                + owner * mob_local
            )
            distance = (row_place - col_place).astype(jnp.float32)
            for level in range(SCALES):
                spread_scans = 2.0**level
                scaled = distance * (1.0 / spread_scans)
                value = (
                    (1.0 - scaled * scaled)
                    * jnp.exp(-0.5 * scaled * scaled)
                    / math.sqrt(0.75 * math.sqrt(math.pi) * spread_scans)
                )
                row = pl.multiple_of(t * TILE_ROWS + level * TM, TM)
                out_ref[pl.ds(row, TM), column : column + LANES] = value.astype(jnp.bfloat16)
        return carry

    lax.fori_loop(0, out_ref.shape[0] // TILE_ROWS, tile, 0)


def weighted(rows, at):
    weights = retention_weights()
    total = weights[RAD] * rows[at]
    for offset in range(1, RAD + 1):
        total = total + weights[RAD + offset] * (rows[at - offset] + rows[at + offset])
    return total.astype(jnp.bfloat16)


def prepare_body(own_ref, other_ref, *out_refs):
    own_out_ref, other_out_ref, held_ref, near_ref, far_ref, kernels_ref = out_refs
    count, scans, channels = own_ref.shape
    held_ref[...] = own_ref[...]
    even = 1 - lax.axis_index("dev") % 2
    near_ref[:, :scans, :] = own_ref[pl.ds(even * (count - RAD), RAD)]
    far_ref[:, :scans, :] = own_ref[pl.ds((1 - even) * (count - RAD), RAD)]
    for edge_ref in (near_ref, far_ref):
        edge_ref[:, scans:, :] = jnp.zeros((RAD, EDGE_PAD, channels), edge_ref.dtype)
    mobility_rows(lax.axis_index("section"), kernels_ref)
    for frames_ref, out_ref in ((own_ref, own_out_ref), (other_ref, other_out_ref)):
        for r in range(0, scans, 16):
            for c in range(0, channels, LANES):
                at = (slice(r, r + 16), slice(c, c + LANES))
                rows = [frames_ref[f, at[0], at[1]].astype(jnp.float32) for f in range(count)]
                for f in range(RAD, count - RAD):
                    out_ref[f - RAD, at[0], at[1]] = weighted(rows, f)


def smooth_edges_body(near_ref, frames_ref, far_ref, mark_ref, head_ref, tail_ref):
    count, scans, channels = frames_ref.shape

    def smooth(left_ref, right_ref):
        def some_scans(step, carry):
            for r in range(0, 64, 16):
                for c in range(0, channels, LANES):
                    at = (pl.ds(pl.multiple_of(step * 64 + r, 16), 16), slice(c, c + LANES))

                    def cells(ref, first, last):
                        return [
                            ref[f, at[0], at[1]].astype(jnp.float32) for f in range(first, last)
                        ]

                    head = cells(left_ref, 0, RAD) + cells(frames_ref, 0, 2 * RAD)
                    for f in range(RAD):
                        head_ref[f, at[0], at[1]] = weighted(head, f + RAD)
                    tail = cells(frames_ref, count - 2 * RAD, count) + cells(right_ref, 0, RAD)
                    for f in range(RAD):
                        tail_ref[f, at[0], at[1]] = weighted(tail, f + RAD)
            return carry

        lax.fori_loop(0, scans // 64, some_scans, 0)

    @pl.when(lax.axis_index("dev") % 2 == 0)
    def _():
        smooth(far_ref, near_ref)

    @pl.when(lax.axis_index("dev") % 2 == 1)
    def _():
        smooth(near_ref, far_ref)


def prepare(own, other):
    count, scans, channels = own.shape
    inner = count - 2 * RAD
    return pl.pallas_call(
        prepare_body,
        in_specs=[WHOLE] * 2,
        out_specs=[WHOLE] * 6,
        out_shape=[
            jax.ShapeDtypeStruct((rows, scans, channels), jnp.bfloat16)
            for rows in (inner, inner, count)
        ]
        + [jax.ShapeDtypeStruct((RAD, scans + EDGE_PAD, channels), jnp.bfloat16)] * 2
        + [jax.ShapeDtypeStruct((scans // TM * TILE_ROWS, 2 * scans), jnp.bfloat16)],
        cost_estimate=BRIEF,
        compiler_params=SMALL,
        name="prepare",
    )(own, other)


def smooth_edges(near, frames, far, mark):
    count, scans, channels = frames.shape
    return pl.pallas_call(
        smooth_edges_body,
        in_specs=[WHOLE] * 3 + [ANYWHERE],
        out_specs=[WHOLE] * 2,
        out_shape=[jax.ShapeDtypeStruct((RAD, scans, channels), jnp.bfloat16)] * 2,
        cost_estimate=BRIEF,
        compiler_params=SMALL,
        name="smooth_edges",
    )(near, frames, far, mark)


def wavelet_body(kernels_ref, own_ref, other_ref, *refs):
    out_ref, mark_ref = refs[-2:]
    mark_ref[...] = jnp.zeros_like(mark_ref)
    rows = kernels_ref.shape[0]

    def frame(f, carry):
        cells = jnp.concatenate([own_ref[f], other_ref[f]], axis=0)
        for r in range(0, rows, TILE_ROWS):
            out_ref[f, r : r + TILE_ROWS, :] = jnp.dot(
                kernels_ref[r : r + TILE_ROWS, :], cells, preferred_element_type=jnp.float32
            ).astype(jnp.bfloat16)
        return carry

    lax.fori_loop(0, out_ref.shape[0], frame, 0, unroll=2)


def wavelets(kernels, own, other, after):
    count, half, channels = own.shape
    rows = kernels.shape[0]
    return pl.pallas_call(
        wavelet_body,
        in_specs=[WHOLE] * 3 + [ANYWHERE] * len(after),
        out_specs=[WHOLE] * 2,
        out_shape=[
            jax.ShapeDtypeStruct((count, rows, channels), jnp.bfloat16),
            jax.ShapeDtypeStruct((8, LANES), jnp.float32),
        ],
        cost_estimate=BRIEF,
        compiler_params=SMALL,
        name="wavelets",
    )(kernels, own, other, *after)


def gather_rows_body(parts, *refs):
    out_ref = refs[-1]
    first = 0
    for part_ref in refs[:parts]:
        count = part_ref.shape[0]
        out_ref[first : first + count, :] = part_ref[...]
        first += count


def gather_rows(parts, passed):
    rows = sum(part.shape[0] for part in parts)

    def body(*refs):
        gather_rows_body(len(parts), *refs)

    return pl.pallas_call(
        body,
        in_specs=[WHOLE] * len(parts) + [ANYWHERE] * len(passed),
        out_specs=[ANYWHERE] * len(passed) + [WHOLE],
        out_shape=[jax.ShapeDtypeStruct(array.shape, array.dtype) for array in passed]
        + [jax.ShapeDtypeStruct((rows, parts[0].shape[1]), parts[0].dtype)],
        input_output_aliases={len(parts) + i: i for i in range(len(passed))},
        cost_estimate=BRIEF,
        compiler_params=SMALL,
        name="gather_rows",
    )(*parts, *passed)


def pass_on(array, after):
    return pl.pallas_call(
        lambda *refs: None,
        in_specs=[ANYWHERE] * 2,
        out_specs=ANYWHERE,
        out_shape=jax.ShapeDtypeStruct(array.shape, array.dtype),
        input_output_aliases={0: 0},
        cost_estimate=BRIEF,
        compiler_params=SMALL,
        name="pass_on",
    )(array, after)


def join_body(one_ref, two_ref, after_ref, counts_ref, out_ref, mark_ref):
    rows = one_ref.shape[0]
    out_ref[:rows, :] = one_ref[...]
    out_ref[rows:, :] = two_ref[...]
    mark_ref[...] = jnp.zeros_like(mark_ref)


def join(one, two, after, counts):
    rows, channels = one.shape
    return pl.pallas_call(
        join_body,
        in_specs=[WHOLE] * 2 + [ANYWHERE] * 2,
        out_specs=[WHOLE] * 2,
        out_shape=[
            jax.ShapeDtypeStruct((2 * rows, channels), one.dtype),
            jax.ShapeDtypeStruct((8, LANES), jnp.float32),
        ],
        cost_estimate=BRIEF,
        compiler_params=SMALL,
        name="join",
    )(one, two, after, counts)


def score_body(slots, unit, refs_in):
    block_sm, tile_sm, live_sm, *stack_refs, owner_ref, own_ref = refs_in[:8]
    piece_refs = refs_in[8:12]
    out_ref, panel, totals, pass_tile, slot_row = refs_in[13:]
    live = live_sm[0, 0, 0]
    section_index, grp, dev = (lax.axis_index(axis) for axis in ("section", "grp", "dev"))
    own_rows = own_ref.shape[0]
    devs = PREC // own_rows
    quarter = own_rows // GROUPS
    pair_rows = (devs - 1) // 2 * quarter
    units = PB // unit
    tiles = stack_refs[0].shape[1] // TILE_ROWS

    def take(ref, first, slot, u):
        rows = ref[pl.ds(pl.multiple_of(first, unit), unit), :]
        panel[pl.ds(pl.multiple_of(slot_row[slot] + u * unit, unit), unit), :] = rows

    def fetch(slot):
        for u in range(units):
            row = block_sm[0, 0, slot] * PB + u * unit
            owner = row // own_rows
            within = row - owner * own_rows
            part = within // quarter
            offset = within - part * quarter
            from_dev = jnp.bitwise_xor(dev, owner)
            from_grp = jnp.bitwise_xor(grp, part)
            halved = (from_dev == devs - 1) & ((devs - 1) % 2 == 1)
            late = offset // (quarter // 2)
            core = jnp.where(halved, late, (from_dev - 1) % 2)
            at = jnp.where(
                halved,
                pair_rows + offset - late * (quarter // 2),
                (from_dev - 1) // 2 * quarter + offset,
            )
            crossed = (core == 1) & ((from_grp == 1) | (from_grp == 2))
            piece = jnp.where(crossed, 3 - from_grp, from_grp)
            at = at + (piece % 2) * (piece_refs[0].shape[0] // 2)
            piece = piece // 2 + 2 * jnp.bitwise_xor(section_index, core)

            @pl.when(from_dev == 0)
            def _():
                take(own_ref, within, slot, u)

            for p in range(len(piece_refs)):

                @pl.when((from_dev > 0) & (piece == p))
                def _():
                    take(piece_refs[p], at, slot, u)

    panel[...] = jnp.zeros_like(panel)
    totals[...] = jnp.zeros_like(totals)

    def of_tile(tile, passes):
        def look(slot, state):
            at_pass, filled = state
            match = tile_sm[0, 0, slot] == tile

            @pl.when(match)
            def _():
                pass_tile[at_pass] = tile
                slot_row[slot] = at_pass * 2 * PB + filled * PB
                fetch(slot)

            full = match & (filled == 1)
            return (
                at_pass + full.astype(jnp.int32),
                jnp.where(match, 1 - filled, filled),
            )

        at_pass, filled = lax.fori_loop(0, live, look, (passes, jnp.int32(0)))
        return at_pass + filled

    passes = lax.fori_loop(0, tiles, of_tile, jnp.int32(0))

    def visit(passes_here):
        sources = []
        for at_pass in passes_here:
            at = pl.ds(pl.multiple_of(pass_tile[at_pass] * TILE_ROWS, TILE_ROWS), TILE_ROWS)
            blocks = panel[pl.ds(pl.multiple_of(at_pass * 2 * PB, 2 * PB), 2 * PB), :]
            sources.append((at, blocks))
        added = [jnp.zeros((8, 2 * PB), jnp.float32)] * len(sources)
        for cells_ref in stack_refs:
            for f in range(cells_ref.shape[0]):
                for i, (at, blocks) in enumerate(sources):
                    scores = lax.dot_general(
                        cells_ref[f, at, :],
                        blocks,
                        (((1,), (1,)), ((), ())),
                        preferred_element_type=jnp.float32,
                    )
                    added[i] = added[i] + jnp.sum(
                        jnp.maximum(scores, 0.0).reshape(TILE_ROWS // 8, 8, 2 * PB), axis=0
                    )
        for at_pass, sums in zip(passes_here, added):
            totals[2 * at_pass] = sums[:, :PB]
            totals[2 * at_pass + 1] = sums[:, PB:]

    def visit_two(step, carry):
        visit([2 * step, 2 * step + 1])
        return carry

    lax.fori_loop(0, passes // 2, visit_two, 0)

    @pl.when(passes % 2 == 1)
    def _():
        visit([passes - 1])

    cells = sum(ref.shape[0] for ref in stack_refs) * TILE_ROWS
    high_index = lax.broadcasted_iota(jnp.int32, (BLOCKS, PB), 0)
    low_index = lax.broadcasted_iota(jnp.int32, (LANES, PB), 0)
    responses, highs, lows = [], [], []
    for slot in range(slots):
        is_live = slot < live
        total = totals[jnp.where(is_live, slot_row[slot] // PB, 0)]
        response = jnp.sum(total, axis=0, keepdims=True) / cells
        response = jnp.where(is_live, response, 0.0)
        owner = owner_ref[pl.ds(block_sm[0, 0, slot], 1), :]
        responses.append(response)
        highs.append(jnp.where(high_index == owner // LANES, response, 0.0))
        lows.append((low_index == owner % LANES).astype(jnp.bfloat16))
    high = jnp.concatenate(highs, axis=1)
    low = jnp.concatenate(lows, axis=1)
    placed = jnp.zeros((BLOCKS, LANES), jnp.float32)
    for _ in range(3):
        part = high.astype(jnp.bfloat16)
        high = high - part.astype(jnp.float32)
        placed = placed + lax.dot_general(
            part, low, (((1,), (1,)), ((), ())), preferred_element_type=jnp.float32
        )
    out_ref[:BLOCKS, :] = placed
    out_ref[BLOCKS:, :] = jnp.broadcast_to(
        jnp.sum(sum(responses), axis=1, keepdims=True), (8, LANES)
    )


def score(block_ids, tile_ids, live, stacks, owner_order, own_templates, pieces, mark):
    slots = block_ids.shape[2]
    own_rows, channels = own_templates.shape
    unit = min(own_rows // (2 * GROUPS), PB)
    tiles = stacks[0].shape[1] // TILE_ROWS
    passes = (slots + tiles) // 2

    def body(*refs):
        score_body(slots, unit, refs)

    return pl.pallas_call(
        body,
        in_specs=[SCALARS] * 3 + [WHOLE] * (len(stacks) + 2 + len(pieces)) + [ANYWHERE],
        out_specs=WHOLE,
        out_shape=jax.ShapeDtypeStruct((BLOCKS + 8, LANES), jnp.float32),
        scratch_shapes=[
            pltpu.VMEM((passes * 2 * PB, channels), jnp.bfloat16),
            pltpu.VMEM((passes * 2, 8, PB), jnp.float32),
            pltpu.SMEM((passes,), jnp.int32),
            pltpu.SMEM((slots,), jnp.int32),
        ],
        cost_estimate=BRIEF,
        compiler_params=SMALL,
        name="score",
    )(block_ids, tile_ids, live, *stacks, owner_order, own_templates, *pieces, mark)


def share_out_body(mine_ref, other_ref, *out_refs):
    rows = out_refs[0].shape[0] - 8
    tail = mine_ref[BLOCKS:, :] + other_ref[BLOCKS:, :]
    for k, out_ref in enumerate(out_refs):
        target = jnp.bitwise_xor(lax.axis_index("dev"), k)
        if rows % 8 == 0:
            at = pl.ds(pl.multiple_of(target * rows, 8), rows)
        else:
            at = pl.ds(target * rows, rows)
        out_ref[:rows, :] = mine_ref[at, :] + other_ref[at, :]
        out_ref[rows:, :] = tail


def share_out(mine, other, devs):
    rows = BLOCKS // devs + 8
    return pl.pallas_call(
        share_out_body,
        in_specs=[WHOLE, WHOLE],
        out_specs=[WHOLE] * devs,
        out_shape=[jax.ShapeDtypeStruct((rows, LANES), jnp.float32)] * devs,
        cost_estimate=BRIEF,
        compiler_params=SMALL,
        name="share_out",
    )(mine, other)


def collect_body(*refs):
    *part_refs, owned_ref, total_ref = refs
    rows = owned_ref.shape[0]
    owned = part_refs[0][...]
    for part_ref in part_refs[1:]:
        owned = owned + part_ref[...]
    owned_ref[...] = owned[:rows]
    total_ref[...] = owned[rows:]


def collect(parts):
    rows = parts[0].shape[0] - 8
    return pl.pallas_call(
        collect_body,
        in_specs=[WHOLE] * len(parts),
        out_specs=[WHOLE] * 2,
        out_shape=[
            jax.ShapeDtypeStruct((rows, LANES), jnp.float32),
            jax.ShapeDtypeStruct((8, LANES), jnp.float32),
        ],
        cost_estimate=BRIEF,
        compiler_params=SMALL,
        name="collect",
    )(*parts)


def normalize_body(owned_ref, *refs):
    *total_refs, out_ref = refs
    everything = total_refs[0][...]
    for total_ref in total_refs[1:]:
        everything = everything + total_ref[...]
    factor = (everything / len(total_refs)) / total_refs[0][...]
    out_ref[...] = owned_ref[...] * factor[:1, :]


def normalize(owned, totals):
    return pl.pallas_call(
        normalize_body,
        in_specs=[WHOLE] * (1 + len(totals)),
        out_specs=WHOLE,
        out_shape=jax.ShapeDtypeStruct(owned.shape, jnp.float32),
        cost_estimate=BRIEF,
        compiler_params=SMALL,
        name="normalize",
    )(owned, *totals)


def on_device(frames, templates, pair_block, pair_tile, pair_count, owner_order):
    section_index = lax.axis_index("section")
    grp = lax.axis_index("grp")
    devs = lax.axis_size("dev")
    groups = lax.axis_size("grp")
    own_frames = frames[0]

    quarter = templates.shape[0] // groups
    own_quarter = lax.dynamic_slice_in_dim(templates, grp * quarter, quarter, 0)
    own_half = lax.dynamic_slice_in_dim(
        templates, grp * quarter + section_index * (quarter // 2), quarter // 2, 0
    )
    arrived = []
    for k in range(1, devs - 1, 2):
        arrived.append(split_swap(own_quarter, "dev", k, k + 1))
    if devs % 2 == 0:
        arrived.append(swap(own_half, "dev", devs - 1))

    other_frames = swap(own_frames, "section", 1)
    inner_own, inner_other, held, near_edge, far_edge, kernels = prepare(
        own_frames, other_frames
    )
    (remote,) = gather_rows(arrived, [])
    first = split_swap(remote, "grp", 1, 2)
    near_halo = swap(near_edge, "dev", 1)
    between = [pair for i in range(1, devs - 1, 2) for pair in ((i, i + 1), (i + 1, i))]
    far_halo = lax.ppermute(far_edge, "dev", between)

    inner, inner_mark = wavelets(kernels, inner_own, inner_other, [remote])
    near, near_mark = join(remote, first, inner_mark, pair_count)
    far = split_swap(near, "grp", 2, 1)
    near_other, far_other = swap(near_halo, "section", 1), swap(far_halo, "section", 1)
    head_own, tail_own = smooth_edges(near_halo, held, far_halo, near_mark)
    head_other, tail_other = smooth_edges(near_other, other_frames, far_other, near_mark)
    head, head_mark = wavelets(kernels, head_own, head_other, [tail_other])
    far = pass_on(far, head_mark)
    tail, _ = wavelets(kernels, tail_own, tail_other, [far])
    pieces = [near, far, swap(near, "section", 1), swap(far, "section", 1)]

    contribution = score(
        pair_block,
        pair_tile,
        pair_count,
        [inner, head, tail],
        owner_order.reshape(BLOCKS, PB),
        templates,
        pieces,
        head_mark,
    )
    outgoing = share_out(contribution, swap(contribution, "section", 1), devs)
    owned, run_total = collect(
        [outgoing[0]] + [swap(outgoing[k], "dev", k) for k in range(1, devs)]
    )
    totals = [run_total] + [swap(run_total, "grp", j) for j in range(1, groups)]
    return normalize(owned, totals).reshape(1, -1)


def solution(mesh):
    placed = (
        P("grp", "dev", "section", None),
        P("dev", None),
        P("section", "grp", "dev"),
        P("section", "grp", "dev"),
        P("section", "grp", "dev"),
        P(),
    )
    return jax.shard_map(
        on_device, mesh=mesh, in_specs=placed, out_specs=P("grp", "dev"), check_vma=False
    )
```

```python
import math

import jax
import jax.numpy as jnp
from jax import lax
from jax.experimental import pallas as pl
from jax.experimental.pallas import tpu as pltpu
from jax.sharding import PartitionSpec as P

MOB = 512
SCALES = 6
RAD = 4
TM = 64
PB = 128
PREC = 8192
LANES = 128
TILE_ROWS = SCALES * TM
BLOCKS = PREC // PB
GROUPS = 4
TAIL = 8
WHOLE = pl.BlockSpec(memory_space=pltpu.VMEM)
ANYWHERE = pl.BlockSpec(memory_space=pl.ANY)
FAR = pl.BlockSpec(memory_space=pltpu.HBM)
SCALARS = pl.BlockSpec(memory_space=pltpu.SMEM)
BRIEF = pl.CostEstimate(flops=1024, bytes_accessed=1024, transcendentals=0)
EDGE_PAD = 32
SMALL = pltpu.CompilerParams(vmem_limit_bytes=4 << 20)

retention_spread = 2.0


def swap(cells, axis, distance):
    count = lax.axis_size(axis)
    return lax.ppermute(cells, axis, [(i, i ^ distance) for i in range(count)])


def cross_swap(cells, group_distance, dev_distance):
    groups, devs = lax.axis_size("grp"), lax.axis_size("dev")
    pairs = [
        (g * devs + d, (g ^ group_distance) * devs + (d ^ dev_distance))
        for g in range(groups)
        for d in range(devs)
    ]
    return lax.ppermute(cells, ("grp", "dev"), pairs)


def split_swap(cells, axis, distance, other_distance):
    count = lax.axis_size(axis)
    pairs = [(i, i ^ distance) for i in range(count)]
    pairs += [(count + i, count + (i ^ other_distance)) for i in range(count)]
    return lax.ppermute(cells, ("section", axis), pairs)


def retention_weights():
    bell_values = [
        math.exp(-0.5 * (offset / retention_spread) ** 2) for offset in range(-RAD, RAD + 1)
    ]
    bell_total = sum(bell_values)
    return [weight_value / bell_total for weight_value in bell_values]


def mobility_rows(section_index, out_ref):
    mob_local = out_ref.shape[1] // 2

    def tile(t, carry):
        first_row = section_index * mob_local + t * TM
        row_place = first_row + lax.broadcasted_iota(jnp.int32, (TM, LANES), 0)
        for column in range(0, 2 * mob_local, LANES):
            owner = jnp.bitwise_xor(section_index, column // mob_local)
            col_place = (
                lax.broadcasted_iota(jnp.int32, (TM, LANES), 1)
                + column % mob_local
                + owner * mob_local
            )
            distance = (row_place - col_place).astype(jnp.float32)
            for level in range(SCALES):
                spread_scans = 2.0**level
                scaled = distance * (1.0 / spread_scans)
                value = (
                    (1.0 - scaled * scaled)
                    * jnp.exp(-0.5 * scaled * scaled)
                    / math.sqrt(0.75 * math.sqrt(math.pi) * spread_scans)
                )
                row = pl.multiple_of(t * TILE_ROWS + level * TM, TM)
                out_ref[pl.ds(row, TM), column : column + LANES] = value.astype(jnp.bfloat16)
        return carry

    lax.fori_loop(0, out_ref.shape[0] // TILE_ROWS, tile, 0)


def weighted(rows, at):
    weights = retention_weights()
    total = weights[RAD] * rows[at]
    for offset in range(1, RAD + 1):
        total = total + weights[RAD + offset] * (rows[at - offset] + rows[at + offset])
    return total.astype(jnp.bfloat16)


def prepare_body(own_ref, other_ref, *out_refs):
    own_out_ref, other_out_ref, held_ref, near_ref, far_ref, kernels_ref = out_refs
    count, scans, channels = own_ref.shape
    held_ref[...] = own_ref[...]
    even = 1 - lax.axis_index("dev") % 2
    near_ref[:, :scans, :] = own_ref[pl.ds(even * (count - RAD), RAD)]
    far_ref[:, :scans, :] = own_ref[pl.ds((1 - even) * (count - RAD), RAD)]
    for edge_ref in (near_ref, far_ref):
        edge_ref[:, scans:, :] = jnp.zeros((RAD, EDGE_PAD, channels), edge_ref.dtype)
    mobility_rows(lax.axis_index("section"), kernels_ref)
    for frames_ref, out_ref in ((own_ref, own_out_ref), (other_ref, other_out_ref)):
        for r in range(0, scans, 16):
            for c in range(0, channels, LANES):
                at = (slice(r, r + 16), slice(c, c + LANES))
                rows = [frames_ref[f, at[0], at[1]].astype(jnp.float32) for f in range(count)]
                for f in range(RAD, count - RAD):
                    out_ref[f - RAD, at[0], at[1]] = weighted(rows, f)


def start_edges_body(own_ref, other_ref, mark_ref, *out_refs):
    weights = retention_weights()[RAD:]
    count, scans, channels = own_ref.shape

    def some_scans(step, carry):
        for half, frames_ref in enumerate((own_ref, other_ref)):
            head_ref, tail_ref = out_refs[2 * half : 2 * half + 2]
            for r in range(0, 64, 16):
                for c in range(0, channels, LANES):
                    at = (pl.ds(pl.multiple_of(step * 64 + r, 16), 16), slice(c, c + LANES))

                    def cells(first, last):
                        return [
                            frames_ref[f, at[0], at[1]].astype(jnp.float32)
                            for f in range(first, last)
                        ]

                    head, tail = cells(0, 2 * RAD), cells(count - 2 * RAD, count)[::-1]
                    for rows, out_ref, flip in ((head, head_ref, 0), (tail, tail_ref, 1)):
                        for f in range(RAD):
                            total = weights[0] * rows[f]
                            for offset in range(1, RAD + 1):
                                pair = rows[f + offset]
                                if f >= offset:
                                    pair = pair + rows[f - offset]
                                total = total + weights[offset] * pair
                            out_ref[RAD - 1 - f if flip else f, at[0], at[1]] = total
        return carry

    lax.fori_loop(0, scans // 64, some_scans, 0)


def start_edges(own, other, mark):
    count, scans, channels = own.shape
    return pl.pallas_call(
        start_edges_body,
        in_specs=[WHOLE] * 2 + [ANYWHERE],
        out_specs=[WHOLE] * 4,
        out_shape=[jax.ShapeDtypeStruct((RAD, scans, channels), jnp.float32)] * 4,
        cost_estimate=BRIEF,
        compiler_params=SMALL,
        name="start_edges",
    )(own, other, mark)


def smooth_edges_body(near_ref, far_ref, head_part_ref, tail_part_ref, head_ref, tail_ref):
    weights = retention_weights()[RAD:]
    scans, channels = head_ref.shape[1:]

    def smooth(left_ref, right_ref):
        def some_scans(step, carry):
            for r in range(0, 64, 16):
                for c in range(0, channels, LANES):
                    at = (pl.ds(pl.multiple_of(step * 64 + r, 16), 16), slice(c, c + LANES))
                    left = [left_ref[f, at[0], at[1]].astype(jnp.float32) for f in range(RAD)]
                    right = [right_ref[f, at[0], at[1]].astype(jnp.float32) for f in range(RAD)]
                    for f in range(RAD):
                        total = head_part_ref[f, at[0], at[1]]
                        for i in range(f, RAD):
                            total = total + weights[RAD + f - i] * left[i]
                        head_ref[f, at[0], at[1]] = total.astype(jnp.bfloat16)
                        total = tail_part_ref[f, at[0], at[1]]
                        for i in range(f + 1):
                            total = total + weights[RAD + i - f] * right[i]
                        tail_ref[f, at[0], at[1]] = total.astype(jnp.bfloat16)
            return carry

        lax.fori_loop(0, scans // 64, some_scans, 0)

    @pl.when(lax.axis_index("dev") % 2 == 0)
    def _():
        smooth(far_ref, near_ref)

    @pl.when(lax.axis_index("dev") % 2 == 1)
    def _():
        smooth(near_ref, far_ref)


def prepare(own, other):
    count, scans, channels = own.shape
    inner = count - 2 * RAD
    return pl.pallas_call(
        prepare_body,
        in_specs=[WHOLE] * 2,
        out_specs=[WHOLE] * 6,
        out_shape=[
            jax.ShapeDtypeStruct((rows, scans, channels), jnp.bfloat16)
            for rows in (inner, inner, count)
        ]
        + [jax.ShapeDtypeStruct((RAD, scans + EDGE_PAD, channels), jnp.bfloat16)] * 2
        + [jax.ShapeDtypeStruct((scans // TM * TILE_ROWS, 2 * scans), jnp.bfloat16)],
        cost_estimate=BRIEF,
        compiler_params=SMALL,
        name="prepare",
    )(own, other)


def smooth_edges(near, far, head_part, tail_part):
    return pl.pallas_call(
        smooth_edges_body,
        in_specs=[WHOLE] * 4,
        out_specs=[WHOLE] * 2,
        out_shape=[jax.ShapeDtypeStruct(head_part.shape, jnp.bfloat16)] * 2,
        cost_estimate=BRIEF,
        compiler_params=SMALL,
        name="smooth_edges",
    )(near, far, head_part, tail_part)


def wavelet_body(kernels_ref, own_ref, other_ref, *refs):
    out_ref, mark_ref = refs[-2:]
    mark_ref[...] = jnp.zeros_like(mark_ref)
    rows = kernels_ref.shape[0]

    def frame(f, carry):
        cells = jnp.concatenate([own_ref[f], other_ref[f]], axis=0)
        for r in range(0, rows, TILE_ROWS):
            out_ref[f, r : r + TILE_ROWS, :] = jnp.dot(
                kernels_ref[r : r + TILE_ROWS, :], cells, preferred_element_type=jnp.float32
            ).astype(jnp.bfloat16)
        return carry

    lax.fori_loop(0, out_ref.shape[0], frame, 0, unroll=2)


def wavelets(kernels, own, other, after):
    count, half, channels = own.shape
    rows = kernels.shape[0]
    return pl.pallas_call(
        wavelet_body,
        in_specs=[WHOLE] * 3 + [ANYWHERE] * len(after),
        out_specs=[WHOLE] * 2,
        out_shape=[
            jax.ShapeDtypeStruct((count, rows, channels), jnp.bfloat16),
            jax.ShapeDtypeStruct((8, LANES), jnp.float32),
        ],
        cost_estimate=BRIEF,
        compiler_params=SMALL,
        name="wavelets",
    )(kernels, own, other, *after)


def own_half_body(rows_ref, out_ref):
    rows = out_ref.shape[0]
    first = pl.multiple_of(lax.axis_index("section") * rows, rows)
    out_ref[...] = rows_ref[pl.ds(first, rows), :]


def own_half_of(rows):
    return pl.pallas_call(
        own_half_body,
        in_specs=[WHOLE],
        out_specs=WHOLE,
        out_shape=jax.ShapeDtypeStruct((rows.shape[0] // 2, rows.shape[1]), rows.dtype),
        cost_estimate=BRIEF,
        compiler_params=SMALL,
        name="own_half",
    )(rows)


def gather_rows_body(parts, *refs):
    out_ref = refs[-1]
    first = 0
    for part_ref in refs[:parts]:
        count = part_ref.shape[0]
        out_ref[first : first + count, :] = part_ref[...]
        first += count


def gather_rows(parts, passed):
    rows = sum(part.shape[0] for part in parts)

    def body(*refs):
        gather_rows_body(len(parts), *refs)

    return pl.pallas_call(
        body,
        in_specs=[WHOLE] * len(parts) + [ANYWHERE] * len(passed),
        out_specs=[ANYWHERE] * len(passed) + [WHOLE],
        out_shape=[jax.ShapeDtypeStruct(array.shape, array.dtype) for array in passed]
        + [jax.ShapeDtypeStruct((rows, parts[0].shape[1]), parts[0].dtype)],
        input_output_aliases={len(parts) + i: i for i in range(len(passed))},
        cost_estimate=BRIEF,
        compiler_params=SMALL,
        name="gather_rows",
    )(*parts, *passed)


def pass_on(array, after):
    return pl.pallas_call(
        lambda *refs: None,
        in_specs=[ANYWHERE] * 2,
        out_specs=ANYWHERE,
        out_shape=jax.ShapeDtypeStruct(array.shape, array.dtype),
        input_output_aliases={0: 0},
        cost_estimate=BRIEF,
        compiler_params=SMALL,
        name="pass_on",
    )(array, after)


def join_body(one_ref, two_ref, after_ref, counts_ref, out_ref, mark_ref):
    rows = one_ref.shape[0]
    out_ref[:rows, :] = one_ref[...]
    out_ref[rows:, :] = two_ref[...]
    mark_ref[...] = jnp.zeros_like(mark_ref)


def join(one, two, after, counts):
    rows, channels = one.shape
    return pl.pallas_call(
        join_body,
        in_specs=[WHOLE] * 2 + [ANYWHERE] * 2,
        out_specs=[WHOLE] * 2,
        out_shape=[
            jax.ShapeDtypeStruct((2 * rows, channels), one.dtype),
            jax.ShapeDtypeStruct((8, LANES), jnp.float32),
        ],
        cost_estimate=BRIEF,
        compiler_params=SMALL,
        name="join",
    )(one, two, after, counts)


def score_body(slots, unit, refs_in):
    block_sm, tile_sm, live_sm, *stack_refs, owner_ref, own_ref = refs_in[:8]
    piece_refs = refs_in[8:12]
    out_ref, panel, totals, pass_tile, slot_row = refs_in[13:]
    live = live_sm[0, 0, 0]
    section_index, grp, dev = (lax.axis_index(axis) for axis in ("section", "grp", "dev"))
    own_rows = own_ref.shape[0]
    devs = PREC // own_rows
    quarter = own_rows // GROUPS
    pair_rows = (devs - 1) // 2 * quarter
    units = PB // unit
    tiles = stack_refs[0].shape[1] // TILE_ROWS

    def take(ref, first, slot, u):
        rows = ref[pl.ds(pl.multiple_of(first, unit), unit), :]
        panel[pl.ds(pl.multiple_of(slot_row[slot] + u * unit, unit), unit), :] = rows

    def fetch(slot):
        for u in range(units):
            row = block_sm[0, 0, slot] * PB + u * unit
            owner = row // own_rows
            within = row - owner * own_rows
            part = within // quarter
            offset = within - part * quarter
            from_dev = jnp.bitwise_xor(dev, owner)
            from_grp = jnp.bitwise_xor(grp, part)
            halved = (from_dev == devs - 1) & ((devs - 1) % 2 == 1)
            late = offset // (quarter // 2)
            core = jnp.where(halved, late, (from_dev - 1) % 2)
            at = jnp.where(
                halved,
                pair_rows + offset - late * (quarter // 2),
                (from_dev - 1) // 2 * quarter + offset,
            )
            crossed = (core == 1) & ((from_grp == 1) | (from_grp == 2))
            piece = jnp.where(crossed, 3 - from_grp, from_grp)
            at = at + (piece % 2) * (piece_refs[0].shape[0] // 2)
            piece = piece // 2 + 2 * jnp.bitwise_xor(section_index, core)

            @pl.when(from_dev == 0)
            def _():
                take(own_ref, within, slot, u)

            for p in range(len(piece_refs)):

                @pl.when((from_dev > 0) & (piece == p))
                def _():
                    take(piece_refs[p], at, slot, u)

    panel[...] = jnp.zeros_like(panel)
    totals[...] = jnp.zeros_like(totals)

    def of_tile(tile, passes):
        def look(slot, state):
            at_pass, filled = state
            match = tile_sm[0, 0, slot] == tile

            @pl.when(match)
            def _():
                pass_tile[at_pass] = tile
                slot_row[slot] = at_pass * 2 * PB + filled * PB
                fetch(slot)

            full = match & (filled == 1)
            return (
                at_pass + full.astype(jnp.int32),
                jnp.where(match, 1 - filled, filled),
            )

        at_pass, filled = lax.fori_loop(0, live, look, (passes, jnp.int32(0)))
        return at_pass + filled

    passes = lax.fori_loop(0, tiles, of_tile, jnp.int32(0))

    def visit(passes_here):
        sources = []
        for at_pass in passes_here:
            at = pl.ds(pl.multiple_of(pass_tile[at_pass] * TILE_ROWS, TILE_ROWS), TILE_ROWS)
            blocks = panel[pl.ds(pl.multiple_of(at_pass * 2 * PB, 2 * PB), 2 * PB), :]
            sources.append((at, blocks))
        added = [jnp.zeros((8, 2 * PB), jnp.float32)] * len(sources)
        for cells_ref in stack_refs:
            for f in range(cells_ref.shape[0]):
                for i, (at, blocks) in enumerate(sources):
                    scores = lax.dot_general(
                        cells_ref[f, at, :],
                        blocks,
                        (((1,), (1,)), ((), ())),
                        preferred_element_type=jnp.float32,
                    )
                    added[i] = added[i] + jnp.sum(
                        jnp.maximum(scores, 0.0).reshape(TILE_ROWS // 8, 8, 2 * PB), axis=0
                    )
        for at_pass, sums in zip(passes_here, added):
            totals[2 * at_pass] = sums[:, :PB]
            totals[2 * at_pass + 1] = sums[:, PB:]

    def visit_two(step, carry):
        visit([2 * step, 2 * step + 1])
        return carry

    lax.fori_loop(0, passes // 2, visit_two, 0)

    @pl.when(passes % 2 == 1)
    def _():
        visit([passes - 1])

    cells = sum(ref.shape[0] for ref in stack_refs) * TILE_ROWS
    high_index = lax.broadcasted_iota(jnp.int32, (BLOCKS, PB), 0)
    low_index = lax.broadcasted_iota(jnp.int32, (LANES, PB), 0)
    responses, highs, lows = [], [], []
    for slot in range(slots):
        is_live = slot < live
        total = totals[jnp.where(is_live, slot_row[slot] // PB, 0)]
        response = jnp.sum(total, axis=0, keepdims=True) / cells
        response = jnp.where(is_live, response, 0.0)
        owner = owner_ref[pl.ds(block_sm[0, 0, slot], 1), :]
        responses.append(response)
        highs.append(jnp.where(high_index == owner // LANES, response, 0.0))
        lows.append((low_index == owner % LANES).astype(jnp.bfloat16))
    high = jnp.concatenate(highs, axis=1)
    low = jnp.concatenate(lows, axis=1)
    placed = jnp.zeros((BLOCKS, LANES), jnp.float32)
    for _ in range(3):
        part = high.astype(jnp.bfloat16)
        high = high - part.astype(jnp.float32)
        placed = placed + lax.dot_general(
            part, low, (((1,), (1,)), ((), ())), preferred_element_type=jnp.float32
        )
    out_ref[:BLOCKS, :] = placed
    out_ref[BLOCKS:, :] = jnp.broadcast_to(
        jnp.sum(sum(responses), axis=1, keepdims=True), (8, LANES)
    )


def score(block_ids, tile_ids, live, stacks, owner_order, own_templates, pieces, mark):
    slots = block_ids.shape[2]
    own_rows, channels = own_templates.shape
    unit = min(own_rows // (2 * GROUPS), PB)
    tiles = stacks[0].shape[1] // TILE_ROWS
    passes = (slots + tiles) // 2

    def body(*refs):
        score_body(slots, unit, refs)

    return pl.pallas_call(
        body,
        in_specs=[SCALARS] * 3 + [WHOLE] * (len(stacks) + 2 + len(pieces)) + [ANYWHERE],
        out_specs=WHOLE,
        out_shape=jax.ShapeDtypeStruct((BLOCKS + 8, LANES), jnp.float32),
        scratch_shapes=[
            pltpu.VMEM((passes * 2 * PB, channels), jnp.bfloat16),
            pltpu.VMEM((passes * 2, 8, PB), jnp.float32),
            pltpu.SMEM((passes,), jnp.int32),
            pltpu.SMEM((slots,), jnp.int32),
        ],
        cost_estimate=BRIEF,
        compiler_params=SMALL,
        name="score",
    )(block_ids, tile_ids, live, *stacks, owner_order, own_templates, *pieces, mark)


def summed_tail(mine_ref, other_ref, extra_refs):
    first = mine_ref.shape[0] - TAIL
    tail = mine_ref[first:, :] + other_ref[first:, :]
    for extra_ref in extra_refs:
        row = lax.broadcasted_iota(jnp.int32, (TAIL, LANES), 0)
        tail = tail + jnp.where(row >= TAIL // 2, extra_ref[...], 0.0)
    return tail


def halve_body(bit, mine_ref, other_ref, *refs):
    *extra_refs, keep_ref, send_ref, tail_ref = refs
    rows = keep_ref.shape[0] - TAIL
    side = lax.axis_index("dev") // bit % 2
    tail = summed_tail(mine_ref, other_ref, extra_refs)
    tail_ref[...] = tail
    for half, out_ref in ((side, keep_ref), (1 - side, send_ref)):
        at = pl.ds(pl.multiple_of(half * rows, rows), rows)
        out_ref[:rows, :] = mine_ref[at, :] + other_ref[at, :]
        out_ref[rows:, :] = tail


def halve(mine, other, extra, bit):
    rows = (mine.shape[0] - TAIL) // 2 + TAIL

    def body(*refs):
        halve_body(bit, *refs)

    return pl.pallas_call(
        body,
        in_specs=[WHOLE] * (2 + len(extra)),
        out_specs=[WHOLE] * 3,
        out_shape=[
            jax.ShapeDtypeStruct((count, LANES), jnp.float32) for count in (rows, rows, TAIL)
        ],
        cost_estimate=BRIEF,
        compiler_params=SMALL,
        name="halve",
    )(mine, other, *extra)


def normalize_body(groups, mine_ref, other_ref, *refs):
    *extra_refs, out_ref = refs
    rows = out_ref.shape[0]
    tail = summed_tail(mine_ref, other_ref, extra_refs)
    factor = (tail[TAIL // 2 : TAIL // 2 + 1, :] / groups) / tail[:1, :]
    out_ref[...] = (mine_ref[:rows, :] + other_ref[:rows, :]) * factor


def normalize(mine, other, extra, groups):
    def body(*refs):
        normalize_body(groups, *refs)

    return pl.pallas_call(
        body,
        in_specs=[WHOLE] * (2 + len(extra)),
        out_specs=WHOLE,
        out_shape=jax.ShapeDtypeStruct((mine.shape[0] - TAIL, LANES), jnp.float32),
        cost_estimate=BRIEF,
        compiler_params=SMALL,
        name="normalize",
    )(mine, other, *extra)


def on_device(frames, templates, pair_block, pair_tile, pair_count, owner_order):
    grp = lax.axis_index("grp")
    devs = lax.axis_size("dev")
    groups = lax.axis_size("grp")
    own_frames = frames[0]

    quarter = templates.shape[0] // groups
    own_quarter = lax.dynamic_slice_in_dim(templates, grp * quarter, quarter, 0)
    own_half = own_half_of(own_quarter)
    arrived = []
    for k in range(1, devs - 1, 2):
        arrived.append(split_swap(own_quarter, "dev", k, k + 1))
    if devs % 2 == 0:
        arrived.append(swap(own_half, "dev", devs - 1))

    other_frames = swap(own_frames, "section", 1)
    inner_own, inner_other, held, near_edge, far_edge, kernels = prepare(
        own_frames, other_frames
    )
    (remote,) = gather_rows(arrived, [])
    first = split_swap(remote, "grp", 1, 2)
    near_halo = swap(near_edge, "dev", 1)
    between = [pair for i in range(1, devs - 1, 2) for pair in ((i, i + 1), (i + 1, i))]
    far_halo = lax.ppermute(far_edge, "dev", between)

    inner, inner_mark = wavelets(kernels, inner_own, inner_other, [remote])
    near, near_mark = join(remote, first, inner_mark, pair_count)
    begun = start_edges(held, other_frames, near_mark)
    near_halo = pass_on(near_halo, begun[0])
    far = split_swap(near, "grp", 2, 1)
    near_other, far_other = swap(near_halo, "section", 1), swap(far_halo, "section", 1)
    head_own, tail_own = smooth_edges(near_halo, far_halo, *begun[:2])
    head_other, tail_other = smooth_edges(near_other, far_other, *begun[2:])
    head, head_mark = wavelets(kernels, head_own, head_other, [tail_other])
    far = pass_on(far, head_mark)
    tail, _ = wavelets(kernels, tail_own, tail_other, [far])
    pieces = [near, far, swap(near, "section", 1), swap(far, "section", 1)]

    contribution = score(
        pair_block,
        pair_tile,
        pair_count,
        [inner, head, tail],
        owner_order.reshape(BLOCKS, PB),
        templates,
        pieces,
        head_mark,
    )
    mine, other, extra = contribution, swap(contribution, "section", 1), []
    bit, across = devs, 1
    while bit > 1:
        bit //= 2
        mine, sent, tail = halve(mine, other, extra, bit)
        other, extra = swap(sent, "dev", bit), []
        if across < groups:
            extra = [swap(tail, "grp", across), cross_swap(tail, across, bit)]
            across *= 2
    return normalize(mine, other, extra, groups).reshape(1, -1)


def solution(mesh):
    placed = (
        P("grp", "dev", "section", None),
        P("dev", None),
        P("section", "grp", "dev"),
        P("section", "grp", "dev"),
        P("section", "grp", "dev"),
        P(),
    )
    return jax.shard_map(
        on_device, mesh=mesh, in_specs=placed, out_specs=P("grp", "dev"), check_vma=False
    )
```

```python
import math

import jax
import jax.numpy as jnp
from jax import lax
from jax.experimental import pallas as pl
from jax.experimental.pallas import tpu as pltpu
from jax.sharding import PartitionSpec as P

MOB = 512
SCALES = 6
RAD = 4
TM = 64
PB = 128
PREC = 8192
LANES = 128
TILE_ROWS = SCALES * TM
BLOCKS = PREC // PB
GROUPS = 4
TAIL = 8
WHOLE = pl.BlockSpec(memory_space=pltpu.VMEM)
ANYWHERE = pl.BlockSpec(memory_space=pl.ANY)
FAR = pl.BlockSpec(memory_space=pltpu.HBM)
SCALARS = pl.BlockSpec(memory_space=pltpu.SMEM)
BRIEF = pl.CostEstimate(flops=1024, bytes_accessed=1024, transcendentals=0)
EDGE_PAD = 32
SMALL = pltpu.CompilerParams(vmem_limit_bytes=4 << 20)

retention_spread = 2.0


def swap(cells, axis, distance):
    count = lax.axis_size(axis)
    return lax.ppermute(cells, axis, [(i, i ^ distance) for i in range(count)])


def cross_swap(cells, group_distance, dev_distance):
    groups, devs = lax.axis_size("grp"), lax.axis_size("dev")
    pairs = []
    for section, distance in ((0, 0), (1, dev_distance)):
        for g in range(groups):
            for d in range(devs):
                target = (section * groups + (g ^ group_distance)) * devs + (d ^ distance)
                pairs.append(((section * groups + g) * devs + d, target))
    return lax.ppermute(cells, ("section", "grp", "dev"), pairs)


def split_swap(cells, axis, distance, other_distance):
    count = lax.axis_size(axis)
    pairs = [(i, i ^ distance) for i in range(count)]
    pairs += [(count + i, count + (i ^ other_distance)) for i in range(count)]
    return lax.ppermute(cells, ("section", axis), pairs)


def retention_weights():
    bell_values = [
        math.exp(-0.5 * (offset / retention_spread) ** 2) for offset in range(-RAD, RAD + 1)
    ]
    bell_total = sum(bell_values)
    return [weight_value / bell_total for weight_value in bell_values]


def mobility_rows(section_index, out_ref):
    mob_local = out_ref.shape[1] // 2

    def tile(t, carry):
        first_row = section_index * mob_local + t * TM
        row_place = first_row + lax.broadcasted_iota(jnp.int32, (TM, LANES), 0)
        for column in range(0, 2 * mob_local, LANES):
            owner = jnp.bitwise_xor(section_index, column // mob_local)
            col_place = (
                lax.broadcasted_iota(jnp.int32, (TM, LANES), 1)
                + column % mob_local
                + owner * mob_local
            )
            distance = (row_place - col_place).astype(jnp.float32)
            for level in range(SCALES):
                spread_scans = 2.0**level
                scaled = distance * (1.0 / spread_scans)
                value = (
                    (1.0 - scaled * scaled)
                    * jnp.exp(-0.5 * scaled * scaled)
                    / math.sqrt(0.75 * math.sqrt(math.pi) * spread_scans)
                )
                row = pl.multiple_of(t * TILE_ROWS + level * TM, TM)
                out_ref[pl.ds(row, TM), column : column + LANES] = value.astype(jnp.bfloat16)
        return carry

    lax.fori_loop(0, out_ref.shape[0] // TILE_ROWS, tile, 0)


def weighted(rows, at):
    weights = retention_weights()
    total = weights[RAD] * rows[at]
    for offset in range(1, RAD + 1):
        total = total + weights[RAD + offset] * (rows[at - offset] + rows[at + offset])
    return total.astype(jnp.bfloat16)


def prepare_body(own_ref, other_ref, *out_refs):
    own_out_ref, other_out_ref, held_ref, near_ref, far_ref, kernels_ref = out_refs
    count, scans, channels = own_ref.shape
    held_ref[...] = own_ref[...]
    even = 1 - lax.axis_index("dev") % 2
    near_ref[:, :scans, :] = own_ref[pl.ds(even * (count - RAD), RAD)]
    far_ref[:, :scans, :] = own_ref[pl.ds((1 - even) * (count - RAD), RAD)]
    for edge_ref in (near_ref, far_ref):
        edge_ref[:, scans:, :] = jnp.zeros((RAD, EDGE_PAD, channels), edge_ref.dtype)
    mobility_rows(lax.axis_index("section"), kernels_ref)
    for frames_ref, out_ref in ((own_ref, own_out_ref), (other_ref, other_out_ref)):
        for r in range(0, scans, 16):
            for c in range(0, channels, LANES):
                at = (slice(r, r + 16), slice(c, c + LANES))
                rows = [frames_ref[f, at[0], at[1]].astype(jnp.float32) for f in range(count)]
                for f in range(RAD, count - RAD):
                    out_ref[f - RAD, at[0], at[1]] = weighted(rows, f)


def start_edges_body(own_ref, other_ref, mark_ref, *out_refs):
    weights = retention_weights()[RAD:]
    count, scans, channels = own_ref.shape

    def some_scans(step, carry):
        for half, frames_ref in enumerate((own_ref, other_ref)):
            head_ref, tail_ref = out_refs[2 * half : 2 * half + 2]
            for r in range(0, 64, 16):
                for c in range(0, channels, LANES):
                    at = (pl.ds(pl.multiple_of(step * 64 + r, 16), 16), slice(c, c + LANES))

                    def cells(first, last):
                        return [
                            frames_ref[f, at[0], at[1]].astype(jnp.float32)
                            for f in range(first, last)
                        ]

                    head, tail = cells(0, 2 * RAD), cells(count - 2 * RAD, count)[::-1]
                    for rows, out_ref, flip in ((head, head_ref, 0), (tail, tail_ref, 1)):
                        for f in range(RAD):
                            total = weights[0] * rows[f]
                            for offset in range(1, RAD + 1):
                                pair = rows[f + offset]
                                if f >= offset:
                                    pair = pair + rows[f - offset]
                                total = total + weights[offset] * pair
                            out_ref[RAD - 1 - f if flip else f, at[0], at[1]] = total
        return carry

    lax.fori_loop(0, scans // 64, some_scans, 0)


def start_edges(own, other, mark):
    count, scans, channels = own.shape
    return pl.pallas_call(
        start_edges_body,
        in_specs=[WHOLE] * 2 + [ANYWHERE],
        out_specs=[WHOLE] * 4,
        out_shape=[jax.ShapeDtypeStruct((RAD, scans, channels), jnp.float32)] * 4,
        cost_estimate=BRIEF,
        compiler_params=SMALL,
        name="start_edges",
    )(own, other, mark)


def smooth_edges_body(near_ref, far_ref, head_part_ref, tail_part_ref, head_ref, tail_ref):
    weights = retention_weights()[RAD:]
    scans, channels = head_ref.shape[1:]

    def smooth(left_ref, right_ref):
        def some_scans(step, carry):
            for r in range(0, 64, 16):
                for c in range(0, channels, LANES):
                    at = (pl.ds(pl.multiple_of(step * 64 + r, 16), 16), slice(c, c + LANES))
                    left = [left_ref[f, at[0], at[1]].astype(jnp.float32) for f in range(RAD)]
                    right = [right_ref[f, at[0], at[1]].astype(jnp.float32) for f in range(RAD)]
                    for f in range(RAD):
                        total = head_part_ref[f, at[0], at[1]]
                        for i in range(f, RAD):
                            total = total + weights[RAD + f - i] * left[i]
                        head_ref[f, at[0], at[1]] = total.astype(jnp.bfloat16)
                        total = tail_part_ref[f, at[0], at[1]]
                        for i in range(f + 1):
                            total = total + weights[RAD + i - f] * right[i]
                        tail_ref[f, at[0], at[1]] = total.astype(jnp.bfloat16)
            return carry

        lax.fori_loop(0, scans // 64, some_scans, 0)

    @pl.when(lax.axis_index("dev") % 2 == 0)
    def _():
        smooth(far_ref, near_ref)

    @pl.when(lax.axis_index("dev") % 2 == 1)
    def _():
        smooth(near_ref, far_ref)


def prepare(own, other):
    count, scans, channels = own.shape
    inner = count - 2 * RAD
    return pl.pallas_call(
        prepare_body,
        in_specs=[WHOLE] * 2,
        out_specs=[WHOLE] * 6,
        out_shape=[
            jax.ShapeDtypeStruct((rows, scans, channels), jnp.bfloat16)
            for rows in (inner, inner, count)
        ]
        + [jax.ShapeDtypeStruct((RAD, scans + EDGE_PAD, channels), jnp.bfloat16)] * 2
        + [jax.ShapeDtypeStruct((scans // TM * TILE_ROWS, 2 * scans), jnp.bfloat16)],
        cost_estimate=BRIEF,
        compiler_params=SMALL,
        name="prepare",
    )(own, other)


def smooth_edges(near, far, head_part, tail_part):
    return pl.pallas_call(
        smooth_edges_body,
        in_specs=[WHOLE] * 4,
        out_specs=[WHOLE] * 2,
        out_shape=[jax.ShapeDtypeStruct(head_part.shape, jnp.bfloat16)] * 2,
        cost_estimate=BRIEF,
        compiler_params=SMALL,
        name="smooth_edges",
    )(near, far, head_part, tail_part)


def wavelet_body(kernels_ref, own_ref, other_ref, *refs):
    out_ref, mark_ref = refs[-2:]
    mark_ref[...] = jnp.zeros_like(mark_ref)
    rows = kernels_ref.shape[0]

    def frame(f, carry):
        cells = jnp.concatenate([own_ref[f], other_ref[f]], axis=0)
        for r in range(0, rows, TILE_ROWS):
            out_ref[f, r : r + TILE_ROWS, :] = jnp.dot(
                kernels_ref[r : r + TILE_ROWS, :], cells, preferred_element_type=jnp.float32
            ).astype(jnp.bfloat16)
        return carry

    lax.fori_loop(0, out_ref.shape[0], frame, 0, unroll=2)


def wavelets(kernels, own, other, after):
    count, half, channels = own.shape
    rows = kernels.shape[0]
    return pl.pallas_call(
        wavelet_body,
        in_specs=[WHOLE] * 3 + [ANYWHERE] * len(after),
        out_specs=[WHOLE] * 2,
        out_shape=[
            jax.ShapeDtypeStruct((count, rows, channels), jnp.bfloat16),
            jax.ShapeDtypeStruct((8, LANES), jnp.float32),
        ],
        cost_estimate=BRIEF,
        compiler_params=SMALL,
        name="wavelets",
    )(kernels, own, other, *after)


def own_half_body(rows_ref, out_ref):
    rows = out_ref.shape[0]
    first = pl.multiple_of(lax.axis_index("section") * rows, rows)
    out_ref[...] = rows_ref[pl.ds(first, rows), :]


def own_half_of(rows):
    return pl.pallas_call(
        own_half_body,
        in_specs=[WHOLE],
        out_specs=WHOLE,
        out_shape=jax.ShapeDtypeStruct((rows.shape[0] // 2, rows.shape[1]), rows.dtype),
        cost_estimate=BRIEF,
        compiler_params=SMALL,
        name="own_half",
    )(rows)


def gather_rows_body(parts, *refs):
    out_ref = refs[-1]
    first = 0
    for part_ref in refs[:parts]:
        count = part_ref.shape[0]
        out_ref[first : first + count, :] = part_ref[...]
        first += count


def gather_rows(parts, passed):
    rows = sum(part.shape[0] for part in parts)

    def body(*refs):
        gather_rows_body(len(parts), *refs)

    return pl.pallas_call(
        body,
        in_specs=[WHOLE] * len(parts) + [ANYWHERE] * len(passed),
        out_specs=[ANYWHERE] * len(passed) + [WHOLE],
        out_shape=[jax.ShapeDtypeStruct(array.shape, array.dtype) for array in passed]
        + [jax.ShapeDtypeStruct((rows, parts[0].shape[1]), parts[0].dtype)],
        input_output_aliases={len(parts) + i: i for i in range(len(passed))},
        cost_estimate=BRIEF,
        compiler_params=SMALL,
        name="gather_rows",
    )(*parts, *passed)


def pass_on(array, after):
    return pl.pallas_call(
        lambda *refs: None,
        in_specs=[ANYWHERE] * 2,
        out_specs=ANYWHERE,
        out_shape=jax.ShapeDtypeStruct(array.shape, array.dtype),
        input_output_aliases={0: 0},
        cost_estimate=BRIEF,
        compiler_params=SMALL,
        name="pass_on",
    )(array, after)


def join_body(one_ref, two_ref, after_ref, counts_ref, out_ref, mark_ref):
    rows = one_ref.shape[0]
    out_ref[:rows, :] = one_ref[...]
    out_ref[rows:, :] = two_ref[...]
    mark_ref[...] = jnp.zeros_like(mark_ref)


def join(one, two, after, counts):
    rows, channels = one.shape
    return pl.pallas_call(
        join_body,
        in_specs=[WHOLE] * 2 + [ANYWHERE] * 2,
        out_specs=[WHOLE] * 2,
        out_shape=[
            jax.ShapeDtypeStruct((2 * rows, channels), one.dtype),
            jax.ShapeDtypeStruct((8, LANES), jnp.float32),
        ],
        cost_estimate=BRIEF,
        compiler_params=SMALL,
        name="join",
    )(one, two, after, counts)


def split_by(value, size):
    return value >> (size.bit_length() - 1), value & (size - 1)


def score_body(slots, unit, refs_in):
    block_sm, tile_sm, live_sm, *stack_refs, owner_ref, own_ref = refs_in[:8]
    piece_refs = refs_in[8:12]
    out_ref, panel, totals, pass_tile = refs_in[13:]
    live = live_sm[0, 0, 0]
    section_index, grp, dev = (lax.axis_index(axis) for axis in ("section", "grp", "dev"))
    own_rows = own_ref.shape[0]
    devs = PREC // own_rows
    quarter = own_rows // GROUPS
    half = quarter // 2
    pair_rows = (devs - 1) // 2 * quarter
    piece_rows = piece_refs[0].shape[0] // 2
    tiles = stack_refs[0].shape[1] // TILE_ROWS

    slot_tile = [jnp.where(slot < live, tile_sm[0, 0, slot], -1) for slot in range(slots)]
    first_pass = [jnp.int32(0)]
    for tile in range(tiles):
        count = sum((there == tile).astype(jnp.int32) for there in slot_tile)
        first_pass.append(first_pass[tile] + ((count + 1) >> 1))
    passes = first_pass[tiles]
    slot_panel = []
    for slot, there in enumerate(slot_tile):
        rank = sum([(other == there).astype(jnp.int32) for other in slot_tile[:slot]], jnp.int32(0))
        at_pass = first_pass[0]
        for tile in range(1, tiles):
            at_pass = jnp.where(there == tile, first_pass[tile], at_pass)
        slot_panel.append(jnp.where(slot < live, 2 * at_pass + rank, 0))

    def fetch(slot):
        pass_tile[slot_panel[slot] >> 1] = slot_tile[slot]
        for u in range(PB // unit):
            owner, within = split_by(block_sm[0, 0, slot] * PB + u * unit, own_rows)
            part, offset = split_by(within, quarter)
            from_dev = dev ^ owner
            from_grp = grp ^ part
            halved = (from_dev == devs - 1) & ((devs - 1) % 2 == 1)
            late, offset_in_half = split_by(offset, half)
            core = jnp.where(halved, late, (from_dev - 1) & 1)
            at = jnp.where(
                halved, pair_rows + offset_in_half, ((from_dev - 1) >> 1) * quarter + offset
            )
            crossed = (core == 1) & ((from_grp == 1) | (from_grp == 2))
            piece = jnp.where(crossed, 3 - from_grp, from_grp)
            at = at + (piece & 1) * piece_rows
            piece = (piece >> 1) + 2 * (section_index ^ core)
            to = pl.ds(pl.multiple_of(slot_panel[slot] * PB + u * unit, unit), unit)

            @pl.when(from_dev == 0)
            def _():
                panel[to, :] = own_ref[pl.ds(pl.multiple_of(within, unit), unit), :]

            for p in range(len(piece_refs)):

                @pl.when((from_dev > 0) & (piece == p))
                def _():
                    panel[to, :] = piece_refs[p][pl.ds(pl.multiple_of(at, unit), unit), :]

    panel[...] = jnp.zeros_like(panel)
    totals[...] = jnp.zeros_like(totals)
    for slot in range(slots):

        @pl.when(slot < live)
        def _():
            fetch(slot)

    def visit(passes_here):
        sources = []
        for at_pass in passes_here:
            at = pl.ds(pl.multiple_of(pass_tile[at_pass] * TILE_ROWS, TILE_ROWS), TILE_ROWS)
            blocks = panel[pl.ds(pl.multiple_of(at_pass * 2 * PB, 2 * PB), 2 * PB), :]
            sources.append((at, blocks))
        added = [jnp.zeros((8, 2 * PB), jnp.float32)] * len(sources)
        for cells_ref in stack_refs:
            for f in range(cells_ref.shape[0]):
                for i, (at, blocks) in enumerate(sources):
                    scores = lax.dot_general(
                        cells_ref[f, at, :],
                        blocks,
                        (((1,), (1,)), ((), ())),
                        preferred_element_type=jnp.float32,
                    )
                    added[i] = added[i] + jnp.sum(
                        jnp.maximum(scores, 0.0).reshape(TILE_ROWS // 8, 8, 2 * PB), axis=0
                    )
        for at_pass, sums in zip(passes_here, added):
            totals[2 * at_pass] = sums[:, :PB]
            totals[2 * at_pass + 1] = sums[:, PB:]

    def visit_two(step, carry):
        visit([2 * step, 2 * step + 1])
        return carry

    lax.fori_loop(0, passes // 2, visit_two, 0)

    @pl.when(passes % 2 == 1)
    def _():
        visit([passes - 1])

    cells = sum(ref.shape[0] for ref in stack_refs) * TILE_ROWS
    high_index = lax.broadcasted_iota(jnp.int32, (BLOCKS, PB), 0)
    low_index = lax.broadcasted_iota(jnp.int32, (LANES, PB), 0)
    responses, highs, lows = [], [], []
    for slot in range(slots):
        is_live = slot < live
        total = totals[slot_panel[slot]]
        response = jnp.sum(total, axis=0, keepdims=True) / cells
        response = jnp.where(is_live, response, 0.0)
        owner = owner_ref[pl.ds(block_sm[0, 0, slot], 1), :]
        responses.append(response)
        highs.append(jnp.where(high_index == owner // LANES, response, 0.0))
        lows.append((low_index == owner % LANES).astype(jnp.bfloat16))
    high = jnp.concatenate(highs, axis=1)
    low = jnp.concatenate(lows, axis=1)
    placed = jnp.zeros((BLOCKS, LANES), jnp.float32)
    for _ in range(3):
        part = high.astype(jnp.bfloat16)
        high = high - part.astype(jnp.float32)
        placed = placed + lax.dot_general(
            part, low, (((1,), (1,)), ((), ())), preferred_element_type=jnp.float32
        )
    out_ref[:BLOCKS, :] = placed
    out_ref[BLOCKS:, :] = jnp.broadcast_to(
        jnp.sum(sum(responses), axis=1, keepdims=True), (8, LANES)
    )


def score(block_ids, tile_ids, live, stacks, owner_order, own_templates, pieces, mark):
    slots = block_ids.shape[2]
    own_rows, channels = own_templates.shape
    unit = min(own_rows // (2 * GROUPS), PB)
    tiles = stacks[0].shape[1] // TILE_ROWS
    passes = (slots + tiles) // 2

    def body(*refs):
        score_body(slots, unit, refs)

    return pl.pallas_call(
        body,
        in_specs=[SCALARS] * 3 + [WHOLE] * (len(stacks) + 2 + len(pieces)) + [ANYWHERE],
        out_specs=WHOLE,
        out_shape=jax.ShapeDtypeStruct((BLOCKS + 8, LANES), jnp.float32),
        scratch_shapes=[
            pltpu.VMEM((passes * 2 * PB, channels), jnp.bfloat16),
            pltpu.VMEM((passes * 2, 8, PB), jnp.float32),
            pltpu.SMEM((passes,), jnp.int32),
        ],
        cost_estimate=BRIEF,
        compiler_params=SMALL,
        name="score",
    )(block_ids, tile_ids, live, *stacks, owner_order, own_templates, *pieces, mark)


def summed_tail(mine_ref, other_ref, extra_refs):
    first = mine_ref.shape[0] - TAIL
    tail = mine_ref[first:, :] + other_ref[first:, :]
    for extra_ref in extra_refs:
        row = lax.broadcasted_iota(jnp.int32, (TAIL, LANES), 0)
        tail = tail + jnp.where(row >= TAIL // 2, extra_ref[...], 0.0)
    return tail


def halve_body(bit, mine_ref, other_ref, *refs):
    *extra_refs, keep_ref, send_ref, tail_ref = refs
    rows = keep_ref.shape[0] - TAIL
    side = lax.axis_index("dev") // bit % 2
    tail = summed_tail(mine_ref, other_ref, extra_refs)
    tail_ref[...] = tail
    for half, out_ref in ((side, keep_ref), (1 - side, send_ref)):
        at = pl.ds(pl.multiple_of(half * rows, rows), rows)
        out_ref[:rows, :] = mine_ref[at, :] + other_ref[at, :]
        out_ref[rows:, :] = tail


def halve(mine, other, extra, bit):
    rows = (mine.shape[0] - TAIL) // 2 + TAIL

    def body(*refs):
        halve_body(bit, *refs)

    return pl.pallas_call(
        body,
        in_specs=[WHOLE] * (2 + len(extra)),
        out_specs=[WHOLE] * 3,
        out_shape=[
            jax.ShapeDtypeStruct((count, LANES), jnp.float32) for count in (rows, rows, TAIL)
        ],
        cost_estimate=BRIEF,
        compiler_params=SMALL,
        name="halve",
    )(mine, other, *extra)


def normalize_body(groups, mine_ref, other_ref, *refs):
    *extra_refs, out_ref = refs
    rows = out_ref.shape[0]
    tail = summed_tail(mine_ref, other_ref, extra_refs)
    factor = (tail[TAIL // 2 : TAIL // 2 + 1, :] / groups) / tail[:1, :]
    out_ref[...] = (mine_ref[:rows, :] + other_ref[:rows, :]) * factor


def normalize(mine, other, extra, groups):
    def body(*refs):
        normalize_body(groups, *refs)

    return pl.pallas_call(
        body,
        in_specs=[WHOLE] * (2 + len(extra)),
        out_specs=WHOLE,
        out_shape=jax.ShapeDtypeStruct((mine.shape[0] - TAIL, LANES), jnp.float32),
        cost_estimate=BRIEF,
        compiler_params=SMALL,
        name="normalize",
    )(mine, other, *extra)


def on_device(frames, templates, pair_block, pair_tile, pair_count, owner_order):
    grp = lax.axis_index("grp")
    devs = lax.axis_size("dev")
    groups = lax.axis_size("grp")
    own_frames = frames[0]

    quarter = templates.shape[0] // groups
    own_quarter = lax.dynamic_slice_in_dim(templates, grp * quarter, quarter, 0)
    own_half = own_half_of(own_quarter)
    arrived = []
    for k in range(1, devs - 1, 2):
        arrived.append(split_swap(own_quarter, "dev", k, k + 1))
    if devs % 2 == 0:
        arrived.append(swap(own_half, "dev", devs - 1))

    other_frames = swap(own_frames, "section", 1)
    inner_own, inner_other, held, near_edge, far_edge, kernels = prepare(
        own_frames, other_frames
    )
    (remote,) = gather_rows(arrived, [])
    first = split_swap(remote, "grp", 1, 2)
    near_halo = swap(near_edge, "dev", 1)
    between = [pair for i in range(1, devs - 1, 2) for pair in ((i, i + 1), (i + 1, i))]
    far_halo = lax.ppermute(far_edge, "dev", between)

    inner, inner_mark = wavelets(kernels, inner_own, inner_other, [remote])
    near, near_mark = join(remote, first, inner_mark, pair_count)
    begun = start_edges(held, other_frames, near_mark)
    near_halo = pass_on(near_halo, begun[0])
    far = split_swap(near, "grp", 2, 1)
    near_other, far_other = swap(near_halo, "section", 1), swap(far_halo, "section", 1)
    head_own, tail_own = smooth_edges(near_halo, far_halo, *begun[:2])
    head_other, tail_other = smooth_edges(near_other, far_other, *begun[2:])
    head, head_mark = wavelets(kernels, head_own, head_other, [tail_other])
    far = pass_on(far, head_mark)
    tail, _ = wavelets(kernels, tail_own, tail_other, [far])
    pieces = [near, far, swap(near, "section", 1), swap(far, "section", 1)]

    contribution = score(
        pair_block,
        pair_tile,
        pair_count,
        [inner, head, tail],
        owner_order.reshape(BLOCKS, PB),
        templates,
        pieces,
        head_mark,
    )
    mine, other, extra = contribution, swap(contribution, "section", 1), []
    bit, across = devs, 1
    while bit > 1:
        bit //= 2
        mine, sent, tail = halve(mine, other, extra, bit)
        other, extra = swap(sent, "dev", bit), []
        if across < groups:
            extra = [cross_swap(tail, across, bit)]
            extra.append(swap(extra[0], "section", 1))
            across *= 2
    return normalize(mine, other, extra, groups).reshape(1, -1)


def solution(mesh):
    placed = (
        P("grp", "dev", "section", None),
        P("dev", None),
        P("section", "grp", "dev"),
        P("section", "grp", "dev"),
        P("section", "grp", "dev"),
        P(),
    )
    return jax.shard_map(
        on_device, mesh=mesh, in_specs=placed, out_specs=P("grp", "dev"), check_vma=False
    )
```

```python
import math

import jax
import jax.numpy as jnp
from jax import lax
from jax.experimental import pallas as pl
from jax.experimental.pallas import tpu as pltpu
from jax.sharding import PartitionSpec as P

MOB = 512
SCALES = 6
RAD = 4
TM = 64
PB = 128
PREC = 8192
LANES = 128
TILE_ROWS = SCALES * TM
BLOCKS = PREC // PB
GROUPS = 4
TAIL = 8
WHOLE = pl.BlockSpec(memory_space=pltpu.VMEM)
ANYWHERE = pl.BlockSpec(memory_space=pl.ANY)
FAR = pl.BlockSpec(memory_space=pltpu.HBM)
SCALARS = pl.BlockSpec(memory_space=pltpu.SMEM)
BRIEF = pl.CostEstimate(flops=1024, bytes_accessed=1024, transcendentals=0)
EDGE_PAD = 32
SMALL = pltpu.CompilerParams(vmem_limit_bytes=4 << 20)

retention_spread = 2.0


def swap(cells, axis, distance):
    count = lax.axis_size(axis)
    return lax.ppermute(cells, axis, [(i, i ^ distance) for i in range(count)])


def cross_swap(cells, group_distance, dev_distance):
    groups, devs = lax.axis_size("grp"), lax.axis_size("dev")
    pairs = []
    for section, distance in ((0, 0), (1, dev_distance)):
        for g in range(groups):
            for d in range(devs):
                target = (section * groups + (g ^ group_distance)) * devs + (d ^ distance)
                pairs.append(((section * groups + g) * devs + d, target))
    return lax.ppermute(cells, ("section", "grp", "dev"), pairs)


def split_swap(cells, axis, distance, other_distance):
    count = lax.axis_size(axis)
    pairs = [(i, i ^ distance) for i in range(count)]
    pairs += [(count + i, count + (i ^ other_distance)) for i in range(count)]
    return lax.ppermute(cells, ("section", axis), pairs)


def retention_weights():
    bell_values = [
        math.exp(-0.5 * (offset / retention_spread) ** 2) for offset in range(-RAD, RAD + 1)
    ]
    bell_total = sum(bell_values)
    return [weight_value / bell_total for weight_value in bell_values]


def mobility_rows(section_index, out_ref):
    mob_local = out_ref.shape[1] // 2

    def tile(t, carry):
        first_row = section_index * mob_local + t * TM
        row_place = first_row + lax.broadcasted_iota(jnp.int32, (TM, LANES), 0)
        for column in range(0, 2 * mob_local, LANES):
            owner = jnp.bitwise_xor(section_index, column // mob_local)
            col_place = (
                lax.broadcasted_iota(jnp.int32, (TM, LANES), 1)
                + column % mob_local
                + owner * mob_local
            )
            distance = (row_place - col_place).astype(jnp.float32)
            for level in range(SCALES):
                spread_scans = 2.0**level
                scaled = distance * (1.0 / spread_scans)
                value = (
                    (1.0 - scaled * scaled)
                    * jnp.exp(-0.5 * scaled * scaled)
                    / math.sqrt(0.75 * math.sqrt(math.pi) * spread_scans)
                )
                row = pl.multiple_of(t * TILE_ROWS + level * TM, TM)
                out_ref[pl.ds(row, TM), column : column + LANES] = value.astype(jnp.bfloat16)
        return carry

    lax.fori_loop(0, out_ref.shape[0] // TILE_ROWS, tile, 0)


def weighted(rows, at):
    weights = retention_weights()
    total = weights[RAD] * rows[at]
    for offset in range(1, RAD + 1):
        total = total + weights[RAD + offset] * (rows[at - offset] + rows[at + offset])
    return total.astype(jnp.bfloat16)


def prepare_body(own_ref, other_ref, *out_refs):
    own_out_ref, other_out_ref, held_ref, near_ref, far_ref, kernels_ref = out_refs
    count, scans, channels = own_ref.shape
    held_ref[...] = own_ref[...]
    even = 1 - lax.axis_index("dev") % 2
    near_ref[:, :scans, :] = own_ref[pl.ds(even * (count - RAD), RAD)]
    far_ref[:, :scans, :] = own_ref[pl.ds((1 - even) * (count - RAD), RAD)]
    for edge_ref in (near_ref, far_ref):
        edge_ref[:, scans:, :] = jnp.zeros((RAD, EDGE_PAD, channels), edge_ref.dtype)
    mobility_rows(lax.axis_index("section"), kernels_ref)
    for frames_ref, out_ref in ((own_ref, own_out_ref), (other_ref, other_out_ref)):
        for r in range(0, scans, 16):
            for c in range(0, channels, LANES):
                at = (slice(r, r + 16), slice(c, c + LANES))
                rows = [frames_ref[f, at[0], at[1]].astype(jnp.float32) for f in range(count)]
                for f in range(RAD, count - RAD):
                    out_ref[f - RAD, at[0], at[1]] = weighted(rows, f)


def start_edges_body(own_ref, other_ref, mark_ref, *out_refs):
    weights = retention_weights()[RAD:]
    count, scans, channels = own_ref.shape

    def some_scans(step, carry):
        for half, frames_ref in enumerate((own_ref, other_ref)):
            head_ref, tail_ref = out_refs[2 * half : 2 * half + 2]
            for r in range(0, 64, 16):
                for c in range(0, channels, LANES):
                    at = (pl.ds(pl.multiple_of(step * 64 + r, 16), 16), slice(c, c + LANES))

                    def cells(first, last):
                        return [
                            frames_ref[f, at[0], at[1]].astype(jnp.float32)
                            for f in range(first, last)
                        ]

                    head, tail = cells(0, 2 * RAD), cells(count - 2 * RAD, count)[::-1]
                    for rows, out_ref, flip in ((head, head_ref, 0), (tail, tail_ref, 1)):
                        for f in range(RAD):
                            total = weights[0] * rows[f]
                            for offset in range(1, RAD + 1):
                                pair = rows[f + offset]
                                if f >= offset:
                                    pair = pair + rows[f - offset]
                                total = total + weights[offset] * pair
                            out_ref[RAD - 1 - f if flip else f, at[0], at[1]] = total
        return carry

    lax.fori_loop(0, scans // 64, some_scans, 0)


def start_edges(own, other, mark):
    count, scans, channels = own.shape
    return pl.pallas_call(
        start_edges_body,
        in_specs=[WHOLE] * 2 + [ANYWHERE],
        out_specs=[WHOLE] * 4,
        out_shape=[jax.ShapeDtypeStruct((RAD, scans, channels), jnp.float32)] * 4,
        cost_estimate=BRIEF,
        compiler_params=SMALL,
        name="start_edges",
    )(own, other, mark)


def smooth_edges_body(near_ref, far_ref, head_part_ref, tail_part_ref, head_ref, tail_ref):
    weights = retention_weights()[RAD:]
    scans, channels = head_ref.shape[1:]

    def smooth(left_ref, right_ref):
        def some_scans(step, carry):
            for r in range(0, 64, 16):
                for c in range(0, channels, LANES):
                    at = (pl.ds(pl.multiple_of(step * 64 + r, 16), 16), slice(c, c + LANES))
                    left = [left_ref[f, at[0], at[1]].astype(jnp.float32) for f in range(RAD)]
                    right = [right_ref[f, at[0], at[1]].astype(jnp.float32) for f in range(RAD)]
                    for f in range(RAD):
                        total = head_part_ref[f, at[0], at[1]]
                        for i in range(f, RAD):
                            total = total + weights[RAD + f - i] * left[i]
                        head_ref[f, at[0], at[1]] = total.astype(jnp.bfloat16)
                        total = tail_part_ref[f, at[0], at[1]]
                        for i in range(f + 1):
                            total = total + weights[RAD + i - f] * right[i]
                        tail_ref[f, at[0], at[1]] = total.astype(jnp.bfloat16)
            return carry

        lax.fori_loop(0, scans // 64, some_scans, 0)

    @pl.when(lax.axis_index("dev") % 2 == 0)
    def _():
        smooth(far_ref, near_ref)

    @pl.when(lax.axis_index("dev") % 2 == 1)
    def _():
        smooth(near_ref, far_ref)


def prepare(own, other):
    count, scans, channels = own.shape
    inner = count - 2 * RAD
    return pl.pallas_call(
        prepare_body,
        in_specs=[WHOLE] * 2,
        out_specs=[WHOLE] * 6,
        out_shape=[
            jax.ShapeDtypeStruct((rows, scans, channels), jnp.bfloat16)
            for rows in (inner, inner, count)
        ]
        + [jax.ShapeDtypeStruct((RAD, scans + EDGE_PAD, channels), jnp.bfloat16)] * 2
        + [jax.ShapeDtypeStruct((scans // TM * TILE_ROWS, 2 * scans), jnp.bfloat16)],
        cost_estimate=BRIEF,
        compiler_params=SMALL,
        name="prepare",
    )(own, other)


def smooth_edges(near, far, head_part, tail_part):
    return pl.pallas_call(
        smooth_edges_body,
        in_specs=[WHOLE] * 4,
        out_specs=[WHOLE] * 2,
        out_shape=[jax.ShapeDtypeStruct(head_part.shape, jnp.bfloat16)] * 2,
        cost_estimate=BRIEF,
        compiler_params=SMALL,
        name="smooth_edges",
    )(near, far, head_part, tail_part)


def wavelet_body(kernels_ref, own_ref, other_ref, *refs):
    out_ref, mark_ref = refs[-2:]
    mark_ref[...] = jnp.zeros_like(mark_ref)
    rows = kernels_ref.shape[0]

    def frame(f, carry):
        cells = jnp.concatenate([own_ref[f], other_ref[f]], axis=0)
        for r in range(0, rows, TILE_ROWS):
            out_ref[f, r : r + TILE_ROWS, :] = jnp.dot(
                kernels_ref[r : r + TILE_ROWS, :], cells, preferred_element_type=jnp.float32
            ).astype(jnp.bfloat16)
        return carry

    lax.fori_loop(0, out_ref.shape[0], frame, 0, unroll=2)


def wavelets(kernels, own, other, after):
    count, half, channels = own.shape
    rows = kernels.shape[0]
    return pl.pallas_call(
        wavelet_body,
        in_specs=[WHOLE] * 3 + [ANYWHERE] * len(after),
        out_specs=[WHOLE] * 2,
        out_shape=[
            jax.ShapeDtypeStruct((count, rows, channels), jnp.bfloat16),
            jax.ShapeDtypeStruct((8, LANES), jnp.float32),
        ],
        cost_estimate=BRIEF,
        compiler_params=SMALL,
        name="wavelets",
    )(kernels, own, other, *after)


def own_half_body(rows_ref, out_ref):
    rows = out_ref.shape[0]
    first = pl.multiple_of(lax.axis_index("section") * rows, rows)
    out_ref[...] = rows_ref[pl.ds(first, rows), :]


def own_half_of(rows):
    return pl.pallas_call(
        own_half_body,
        in_specs=[WHOLE],
        out_specs=WHOLE,
        out_shape=jax.ShapeDtypeStruct((rows.shape[0] // 2, rows.shape[1]), rows.dtype),
        cost_estimate=BRIEF,
        compiler_params=SMALL,
        name="own_half",
    )(rows)


def gather_rows_body(parts, *refs):
    out_ref = refs[-1]
    first = 0
    for part_ref in refs[:parts]:
        count = part_ref.shape[0]
        out_ref[first : first + count, :] = part_ref[...]
        first += count


def gather_rows(parts, passed):
    rows = sum(part.shape[0] for part in parts)

    def body(*refs):
        gather_rows_body(len(parts), *refs)

    return pl.pallas_call(
        body,
        in_specs=[WHOLE] * len(parts) + [ANYWHERE] * len(passed),
        out_specs=[ANYWHERE] * len(passed) + [WHOLE],
        out_shape=[jax.ShapeDtypeStruct(array.shape, array.dtype) for array in passed]
        + [jax.ShapeDtypeStruct((rows, parts[0].shape[1]), parts[0].dtype)],
        input_output_aliases={len(parts) + i: i for i in range(len(passed))},
        cost_estimate=BRIEF,
        compiler_params=SMALL,
        name="gather_rows",
    )(*parts, *passed)


def pass_on(array, after):
    return pl.pallas_call(
        lambda *refs: None,
        in_specs=[ANYWHERE] * 2,
        out_specs=ANYWHERE,
        out_shape=jax.ShapeDtypeStruct(array.shape, array.dtype),
        input_output_aliases={0: 0},
        cost_estimate=BRIEF,
        compiler_params=SMALL,
        name="pass_on",
    )(array, after)


def join_body(one_ref, two_ref, after_ref, counts_ref, out_ref, mark_ref):
    rows = one_ref.shape[0]
    out_ref[:rows, :] = one_ref[...]
    out_ref[rows:, :] = two_ref[...]
    mark_ref[...] = jnp.zeros_like(mark_ref)


def join(one, two, after, counts):
    rows, channels = one.shape
    return pl.pallas_call(
        join_body,
        in_specs=[WHOLE] * 2 + [ANYWHERE] * 2,
        out_specs=[WHOLE] * 2,
        out_shape=[
            jax.ShapeDtypeStruct((2 * rows, channels), one.dtype),
            jax.ShapeDtypeStruct((8, LANES), jnp.float32),
        ],
        cost_estimate=BRIEF,
        compiler_params=SMALL,
        name="join",
    )(one, two, after, counts)


def split_by(value, size):
    return value >> (size.bit_length() - 1), value & (size - 1)


def score_body(slots, unit, refs_in):
    block_sm, tile_sm, live_sm, *stack_refs, owner_ref, own_ref = refs_in[:8]
    piece_refs = refs_in[8:12]
    out_ref, panel, totals, pass_tile = refs_in[13:]
    live = live_sm[0, 0, 0]
    section_index, grp, dev = (lax.axis_index(axis) for axis in ("section", "grp", "dev"))
    own_rows = own_ref.shape[0]
    devs = PREC // own_rows
    quarter = own_rows // GROUPS
    half = quarter // 2
    pair_rows = (devs - 1) // 2 * quarter
    piece_rows = piece_refs[0].shape[0] // 2
    tiles = stack_refs[0].shape[1] // TILE_ROWS

    slot_tile = [jnp.where(slot < live, tile_sm[0, 0, slot], -1) for slot in range(slots)]
    first_pass = [jnp.int32(0)]
    for tile in range(tiles):
        count = sum((there == tile).astype(jnp.int32) for there in slot_tile)
        first_pass.append(first_pass[tile] + ((count + 1) >> 1))
    passes = first_pass[tiles]
    slot_panel = []
    for slot, there in enumerate(slot_tile):
        rank = sum([(other == there).astype(jnp.int32) for other in slot_tile[:slot]], jnp.int32(0))
        at_pass = first_pass[0]
        for tile in range(1, tiles):
            at_pass = jnp.where(there == tile, first_pass[tile], at_pass)
        slot_panel.append(jnp.where(slot < live, 2 * at_pass + rank, 0))

    def fetch(slot):
        pass_tile[slot_panel[slot] >> 1] = slot_tile[slot]
        for u in range(PB // unit):
            owner, within = split_by(block_sm[0, 0, slot] * PB + u * unit, own_rows)
            part, offset = split_by(within, quarter)
            from_dev = dev ^ owner
            from_grp = grp ^ part
            halved = (from_dev == devs - 1) & ((devs - 1) % 2 == 1)
            late, offset_in_half = split_by(offset, half)
            core = jnp.where(halved, late, (from_dev - 1) & 1)
            at = jnp.where(
                halved, pair_rows + offset_in_half, ((from_dev - 1) >> 1) * quarter + offset
            )
            crossed = (core == 1) & ((from_grp == 1) | (from_grp == 2))
            piece = jnp.where(crossed, 3 - from_grp, from_grp)
            at = at + (piece & 1) * piece_rows
            piece = (piece >> 1) + 2 * (section_index ^ core)
            to = pl.ds(pl.multiple_of(slot_panel[slot] * PB + u * unit, unit), unit)

            @pl.when(from_dev == 0)
            def _():
                panel[to, :] = own_ref[pl.ds(pl.multiple_of(within, unit), unit), :]

            for p in range(len(piece_refs)):

                @pl.when((from_dev > 0) & (piece == p))
                def _():
                    panel[to, :] = piece_refs[p][pl.ds(pl.multiple_of(at, unit), unit), :]

    panel[...] = jnp.zeros_like(panel)
    totals[...] = jnp.zeros_like(totals)
    for slot in range(slots):

        @pl.when(slot < live)
        def _():
            fetch(slot)

    def visit(passes_here):
        sources = []
        for at_pass in passes_here:
            at = pl.ds(pl.multiple_of(pass_tile[at_pass] * TILE_ROWS, TILE_ROWS), TILE_ROWS)
            blocks = panel[pl.ds(pl.multiple_of(at_pass * 2 * PB, 2 * PB), 2 * PB), :]
            sources.append((at, blocks))
        added = [jnp.zeros((8, 2 * PB), jnp.float32)] * len(sources)
        for cells_ref in stack_refs:
            for f in range(cells_ref.shape[0]):
                for i, (at, blocks) in enumerate(sources):
                    scores = lax.dot_general(
                        cells_ref[f, at, :],
                        blocks,
                        (((1,), (1,)), ((), ())),
                        preferred_element_type=jnp.float32,
                    )
                    added[i] = added[i] + jnp.sum(
                        jnp.maximum(scores, 0.0).reshape(TILE_ROWS // 8, 8, 2 * PB), axis=0
                    )
        for at_pass, sums in zip(passes_here, added):
            totals[2 * at_pass] = sums[:, :PB]
            totals[2 * at_pass + 1] = sums[:, PB:]

    def visit_two(step, carry):
        visit([2 * step, 2 * step + 1])
        return carry

    lax.fori_loop(0, passes // 2, visit_two, 0)

    @pl.when(passes % 2 == 1)
    def _():
        visit([passes - 1])

    cells = sum(ref.shape[0] for ref in stack_refs) * TILE_ROWS
    high_index = lax.broadcasted_iota(jnp.int32, (BLOCKS, PB), 0)
    low_index = lax.broadcasted_iota(jnp.int32, (LANES, PB), 0)
    responses, highs, lows = [], [], []
    for slot in range(slots):
        is_live = slot < live
        total = totals[slot_panel[slot]]
        response = jnp.sum(total, axis=0, keepdims=True) / cells
        response = jnp.where(is_live, response, 0.0)
        owner = owner_ref[pl.ds(block_sm[0, 0, slot], 1), :]
        responses.append(response)
        highs.append(jnp.where(high_index == owner // LANES, response, 0.0))
        lows.append((low_index == owner % LANES).astype(jnp.bfloat16))
    high = jnp.concatenate(highs, axis=1)
    low = jnp.concatenate(lows, axis=1)
    placed = jnp.zeros((BLOCKS, LANES), jnp.float32)
    for _ in range(3):
        part = high.astype(jnp.bfloat16)
        high = high - part.astype(jnp.float32)
        placed = placed + lax.dot_general(
            part, low, (((1,), (1,)), ((), ())), preferred_element_type=jnp.float32
        )
    out_ref[:BLOCKS, :] = placed
    out_ref[BLOCKS:, :] = jnp.broadcast_to(
        jnp.sum(sum(responses), axis=1, keepdims=True), (8, LANES)
    )


def score(block_ids, tile_ids, live, stacks, owner_order, own_templates, pieces, mark):
    slots = block_ids.shape[2]
    own_rows, channels = own_templates.shape
    unit = min(own_rows // (2 * GROUPS), PB)
    tiles = stacks[0].shape[1] // TILE_ROWS
    passes = (slots + tiles) // 2

    def body(*refs):
        score_body(slots, unit, refs)

    return pl.pallas_call(
        body,
        in_specs=[SCALARS] * 3 + [WHOLE] * (len(stacks) + 2 + len(pieces)) + [ANYWHERE],
        out_specs=WHOLE,
        out_shape=jax.ShapeDtypeStruct((BLOCKS + 8, LANES), jnp.float32),
        scratch_shapes=[
            pltpu.VMEM((passes * 2 * PB, channels), jnp.bfloat16),
            pltpu.VMEM((passes * 2, 8, PB), jnp.float32),
            pltpu.SMEM((passes,), jnp.int32),
        ],
        cost_estimate=BRIEF,
        compiler_params=SMALL,
        name="score",
    )(block_ids, tile_ids, live, *stacks, owner_order, own_templates, *pieces, mark)


def summed_tail(mine_ref, other_ref, extra_refs):
    first = mine_ref.shape[0] - TAIL
    tail = mine_ref[first:, :] + other_ref[first:, :]
    for extra_ref in extra_refs:
        row = lax.broadcasted_iota(jnp.int32, (TAIL, LANES), 0)
        tail = tail + jnp.where(row >= TAIL // 2, extra_ref[...], 0.0)
    return tail


def halve_body(bit, mine_ref, other_ref, *refs):
    *extra_refs, keep_ref, send_ref, tail_ref = refs
    rows = keep_ref.shape[0] - TAIL
    side = lax.axis_index("dev") // bit % 2
    tail = summed_tail(mine_ref, other_ref, extra_refs)
    tail_ref[...] = tail
    for half, out_ref in ((side, keep_ref), (1 - side, send_ref)):
        at = pl.ds(pl.multiple_of(half * rows, rows), rows)
        out_ref[:rows, :] = mine_ref[at, :] + other_ref[at, :]
        out_ref[rows:, :] = tail


def halve(mine, other, extra, bit):
    rows = (mine.shape[0] - TAIL) // 2 + TAIL

    def body(*refs):
        halve_body(bit, *refs)

    return pl.pallas_call(
        body,
        in_specs=[WHOLE] * (2 + len(extra)),
        out_specs=[WHOLE] * 3,
        out_shape=[
            jax.ShapeDtypeStruct((count, LANES), jnp.float32) for count in (rows, rows, TAIL)
        ],
        cost_estimate=BRIEF,
        compiler_params=SMALL,
        name="halve",
    )(mine, other, *extra)


def normalize_body(groups, mine_ref, other_ref, *refs):
    *extra_refs, out_ref = refs
    rows = out_ref.shape[0]
    tail = summed_tail(mine_ref, other_ref, extra_refs)
    factor = (tail[TAIL // 2 : TAIL // 2 + 1, :] / groups) / tail[:1, :]
    out_ref[...] = (mine_ref[:rows, :] + other_ref[:rows, :]) * factor


def normalize(mine, other, extra, groups):
    def body(*refs):
        normalize_body(groups, *refs)

    return pl.pallas_call(
        body,
        in_specs=[WHOLE] * (2 + len(extra)),
        out_specs=WHOLE,
        out_shape=jax.ShapeDtypeStruct((mine.shape[0] - TAIL, LANES), jnp.float32),
        cost_estimate=BRIEF,
        compiler_params=SMALL,
        name="normalize",
    )(mine, other, *extra)


def on_device(frames, templates, pair_block, pair_tile, pair_count, owner_order):
    grp = lax.axis_index("grp")
    devs = lax.axis_size("dev")
    groups = lax.axis_size("grp")
    own_frames = frames[0]

    quarter = templates.shape[0] // groups
    own_quarter = lax.dynamic_slice_in_dim(templates, grp * quarter, quarter, 0)
    own_half = own_half_of(own_quarter)
    arrived = []
    for k in range(1, devs - 1, 2):
        arrived.append(split_swap(own_quarter, "dev", k, k + 1))
    if devs % 2 == 0:
        arrived.append(swap(own_half, "dev", devs - 1))

    other_frames = swap(own_frames, "section", 1)
    inner_own, inner_other, held, near_edge, far_edge, kernels = prepare(
        own_frames, other_frames
    )
    (remote,) = gather_rows(arrived, [])
    first = split_swap(remote, "grp", 1, 2)
    near_halo = swap(near_edge, "dev", 1)
    between = [pair for i in range(1, devs - 1, 2) for pair in ((i, i + 1), (i + 1, i))]
    far_halo = lax.ppermute(far_edge, "dev", between)

    inner, inner_mark = wavelets(kernels, inner_own, inner_other, [remote])
    near, near_mark = join(remote, first, inner_mark, pair_count)
    begun = start_edges(held, other_frames, near_mark)
    near_halo = pass_on(near_halo, begun[0])
    far = split_swap(near, "grp", 2, 1)
    near_other, far_other = swap(near_halo, "section", 1), swap(far_halo, "section", 1)
    head_own, tail_own = smooth_edges(near_halo, far_halo, *begun[:2])
    head_other, tail_other = smooth_edges(near_other, far_other, *begun[2:])
    head, head_mark = wavelets(kernels, head_own, head_other, [tail_other])
    far = pass_on(far, head_mark)
    tail, _ = wavelets(kernels, tail_own, tail_other, [far])
    pieces = [near, far, swap(near, "section", 1), swap(far, "section", 1)]

    contribution = score(
        pair_block,
        pair_tile,
        pair_count,
        [inner, head, tail],
        owner_order.reshape(BLOCKS, PB),
        templates,
        pieces,
        head_mark,
    )
    mine, other, extra = contribution, swap(contribution, "section", 1), []
    bit, across = devs, groups // 2
    while bit > 1:
        bit //= 2
        mine, sent, tail = halve(mine, other, extra, bit)
        other, extra = swap(sent, "dev", bit), []
        if across > 0:
            extra = [cross_swap(tail, across, bit)]
            extra.append(swap(extra[0], "section", 1))
            across //= 2
    return normalize(mine, other, extra, groups).reshape(1, -1)


def solution(mesh):
    placed = (
        P("grp", "dev", "section", None),
        P("dev", None),
        P("section", "grp", "dev"),
        P("section", "grp", "dev"),
        P("section", "grp", "dev"),
        P(),
    )
    return jax.shard_map(
        on_device, mesh=mesh, in_specs=placed, out_specs=P("grp", "dev"), check_vma=False
    )
```

```python
import math

import jax
import jax.numpy as jnp
from jax import lax
from jax.experimental import pallas as pl
from jax.experimental.pallas import tpu as pltpu
from jax.sharding import PartitionSpec as P

MOB = 512
SCALES = 6
RAD = 4
TM = 64
PB = 128
PREC = 8192
LANES = 128
TILE_ROWS = SCALES * TM
BLOCKS = PREC // PB
GROUPS = 4
TAIL = 8
WHOLE = pl.BlockSpec(memory_space=pltpu.VMEM)
ANYWHERE = pl.BlockSpec(memory_space=pl.ANY)
FAR = pl.BlockSpec(memory_space=pltpu.HBM)
SCALARS = pl.BlockSpec(memory_space=pltpu.SMEM)
BRIEF = pl.CostEstimate(flops=1024, bytes_accessed=1024, transcendentals=0)
EDGE_PAD = 32
SMALL = pltpu.CompilerParams(vmem_limit_bytes=4 << 20)

retention_spread = 2.0


def swap(cells, axis, distance):
    count = lax.axis_size(axis)
    return lax.ppermute(cells, axis, [(i, i ^ distance) for i in range(count)])


def cross_swap(cells, group_distance, dev_distance):
    groups, devs = lax.axis_size("grp"), lax.axis_size("dev")
    pairs = []
    for section, distance in ((0, 0), (1, dev_distance)):
        for g in range(groups):
            for d in range(devs):
                target = (section * groups + (g ^ group_distance)) * devs + (d ^ distance)
                pairs.append(((section * groups + g) * devs + d, target))
    return lax.ppermute(cells, ("section", "grp", "dev"), pairs)


def split_swap(cells, axis, distance, other_distance):
    count = lax.axis_size(axis)
    pairs = [(i, i ^ distance) for i in range(count)]
    pairs += [(count + i, count + (i ^ other_distance)) for i in range(count)]
    return lax.ppermute(cells, ("section", axis), pairs)


def retention_weights():
    bell_values = [
        math.exp(-0.5 * (offset / retention_spread) ** 2) for offset in range(-RAD, RAD + 1)
    ]
    bell_total = sum(bell_values)
    return [weight_value / bell_total for weight_value in bell_values]


def mobility_rows(section_index, out_ref):
    mob_local = out_ref.shape[1] // 2

    def tile(t, carry):
        first_row = section_index * mob_local + t * TM
        row_place = first_row + lax.broadcasted_iota(jnp.int32, (TM, LANES), 0)
        for column in range(0, 2 * mob_local, LANES):
            owner = jnp.bitwise_xor(section_index, column // mob_local)
            col_place = (
                lax.broadcasted_iota(jnp.int32, (TM, LANES), 1)
                + column % mob_local
                + owner * mob_local
            )
            distance = (row_place - col_place).astype(jnp.float32)
            for level in range(SCALES):
                spread_scans = 2.0**level
                scaled = distance * (1.0 / spread_scans)
                value = (
                    (1.0 - scaled * scaled)
                    * jnp.exp(-0.5 * scaled * scaled)
                    / math.sqrt(0.75 * math.sqrt(math.pi) * spread_scans)
                )
                row = pl.multiple_of(t * TILE_ROWS + level * TM, TM)
                out_ref[pl.ds(row, TM), column : column + LANES] = value.astype(jnp.bfloat16)
        return carry

    lax.fori_loop(0, out_ref.shape[0] // TILE_ROWS, tile, 0)


def weighted(rows, at):
    weights = retention_weights()
    total = weights[RAD] * rows[at]
    for offset in range(1, RAD + 1):
        total = total + weights[RAD + offset] * (rows[at - offset] + rows[at + offset])
    return total.astype(jnp.bfloat16)


def prepare_body(own_ref, other_ref, *out_refs):
    own_out_ref, other_out_ref, held_ref, near_ref, far_ref, kernels_ref = out_refs
    count, scans, channels = own_ref.shape
    held_ref[...] = own_ref[...]
    even = 1 - lax.axis_index("dev") % 2
    near_ref[:, :scans, :] = own_ref[pl.ds(even * (count - RAD), RAD)]
    far_ref[:, :scans, :] = own_ref[pl.ds((1 - even) * (count - RAD), RAD)]
    for edge_ref in (near_ref, far_ref):
        edge_ref[:, scans:, :] = jnp.zeros((RAD, EDGE_PAD, channels), edge_ref.dtype)
    mobility_rows(lax.axis_index("section"), kernels_ref)
    for frames_ref, out_ref in ((own_ref, own_out_ref), (other_ref, other_out_ref)):
        for r in range(0, scans, 16):
            for c in range(0, channels, LANES):
                at = (slice(r, r + 16), slice(c, c + LANES))
                rows = [frames_ref[f, at[0], at[1]].astype(jnp.float32) for f in range(count)]
                for f in range(RAD, count - RAD):
                    out_ref[f - RAD, at[0], at[1]] = weighted(rows, f)


def start_edges_body(own_ref, other_ref, mark_ref, *out_refs):
    weights = retention_weights()[RAD:]
    count, scans, channels = own_ref.shape

    def some_scans(step, carry):
        for half, frames_ref in enumerate((own_ref, other_ref)):
            head_ref, tail_ref = out_refs[2 * half : 2 * half + 2]
            for r in range(0, 64, 16):
                for c in range(0, channels, LANES):
                    at = (pl.ds(pl.multiple_of(step * 64 + r, 16), 16), slice(c, c + LANES))

                    def cells(first, last):
                        return [
                            frames_ref[f, at[0], at[1]].astype(jnp.float32)
                            for f in range(first, last)
                        ]

                    head, tail = cells(0, 2 * RAD), cells(count - 2 * RAD, count)[::-1]
                    for rows, out_ref, flip in ((head, head_ref, 0), (tail, tail_ref, 1)):
                        for f in range(RAD):
                            total = weights[0] * rows[f]
                            for offset in range(1, RAD + 1):
                                pair = rows[f + offset]
                                if f >= offset:
                                    pair = pair + rows[f - offset]
                                total = total + weights[offset] * pair
                            out_ref[RAD - 1 - f if flip else f, at[0], at[1]] = total
        return carry

    lax.fori_loop(0, scans // 64, some_scans, 0)


def start_edges(own, other, mark):
    count, scans, channels = own.shape
    return pl.pallas_call(
        start_edges_body,
        in_specs=[WHOLE] * 2 + [ANYWHERE],
        out_specs=[WHOLE] * 4,
        out_shape=[jax.ShapeDtypeStruct((RAD, scans, channels), jnp.float32)] * 4,
        cost_estimate=BRIEF,
        compiler_params=SMALL,
        name="start_edges",
    )(own, other, mark)


def smooth_edges_body(near_ref, far_ref, head_part_ref, tail_part_ref, head_ref, tail_ref):
    weights = retention_weights()[RAD:]
    scans, channels = head_ref.shape[1:]

    def smooth(left_ref, right_ref):
        def some_scans(step, carry):
            for r in range(0, 64, 16):
                for c in range(0, channels, LANES):
                    at = (pl.ds(pl.multiple_of(step * 64 + r, 16), 16), slice(c, c + LANES))
                    left = [left_ref[f, at[0], at[1]].astype(jnp.float32) for f in range(RAD)]
                    right = [right_ref[f, at[0], at[1]].astype(jnp.float32) for f in range(RAD)]
                    for f in range(RAD):
                        total = head_part_ref[f, at[0], at[1]]
                        for i in range(f, RAD):
                            total = total + weights[RAD + f - i] * left[i]
                        head_ref[f, at[0], at[1]] = total.astype(jnp.bfloat16)
                        total = tail_part_ref[f, at[0], at[1]]
                        for i in range(f + 1):
                            total = total + weights[RAD + i - f] * right[i]
                        tail_ref[f, at[0], at[1]] = total.astype(jnp.bfloat16)
            return carry

        lax.fori_loop(0, scans // 64, some_scans, 0)

    @pl.when(lax.axis_index("dev") % 2 == 0)
    def _():
        smooth(far_ref, near_ref)

    @pl.when(lax.axis_index("dev") % 2 == 1)
    def _():
        smooth(near_ref, far_ref)


def prepare(own, other):
    count, scans, channels = own.shape
    inner = count - 2 * RAD
    return pl.pallas_call(
        prepare_body,
        in_specs=[WHOLE] * 2,
        out_specs=[WHOLE] * 6,
        out_shape=[
            jax.ShapeDtypeStruct((rows, scans, channels), jnp.bfloat16)
            for rows in (inner, inner, count)
        ]
        + [jax.ShapeDtypeStruct((RAD, scans + EDGE_PAD, channels), jnp.bfloat16)] * 2
        + [jax.ShapeDtypeStruct((scans // TM * TILE_ROWS, 2 * scans), jnp.bfloat16)],
        cost_estimate=BRIEF,
        compiler_params=SMALL,
        name="prepare",
    )(own, other)


def smooth_edges(near, far, head_part, tail_part):
    return pl.pallas_call(
        smooth_edges_body,
        in_specs=[WHOLE] * 4,
        out_specs=[WHOLE] * 2,
        out_shape=[jax.ShapeDtypeStruct(head_part.shape, jnp.bfloat16)] * 2,
        cost_estimate=BRIEF,
        compiler_params=SMALL,
        name="smooth_edges",
    )(near, far, head_part, tail_part)


def wavelet_body(kernels_ref, own_ref, other_ref, *refs):
    out_ref, mark_ref = refs[-2:]
    mark_ref[...] = jnp.zeros_like(mark_ref)
    rows = kernels_ref.shape[0]

    def frame(f, carry):
        cells = jnp.concatenate([own_ref[f], other_ref[f]], axis=0)
        for r in range(0, rows, TILE_ROWS):
            out_ref[f, r : r + TILE_ROWS, :] = jnp.dot(
                kernels_ref[r : r + TILE_ROWS, :], cells, preferred_element_type=jnp.float32
            ).astype(jnp.bfloat16)
        return carry

    lax.fori_loop(0, out_ref.shape[0], frame, 0, unroll=2)


def wavelets(kernels, own, other, after):
    count, half, channels = own.shape
    rows = kernels.shape[0]
    return pl.pallas_call(
        wavelet_body,
        in_specs=[WHOLE] * 3 + [ANYWHERE] * len(after),
        out_specs=[WHOLE] * 2,
        out_shape=[
            jax.ShapeDtypeStruct((count, rows, channels), jnp.bfloat16),
            jax.ShapeDtypeStruct((8, LANES), jnp.float32),
        ],
        cost_estimate=BRIEF,
        compiler_params=SMALL,
        name="wavelets",
    )(kernels, own, other, *after)


def own_half_body(rows_ref, out_ref):
    rows = out_ref.shape[0]
    first = pl.multiple_of(lax.axis_index("section") * rows, rows)
    out_ref[...] = rows_ref[pl.ds(first, rows), :]


def own_half_of(rows):
    return pl.pallas_call(
        own_half_body,
        in_specs=[WHOLE],
        out_specs=WHOLE,
        out_shape=jax.ShapeDtypeStruct((rows.shape[0] // 2, rows.shape[1]), rows.dtype),
        cost_estimate=BRIEF,
        compiler_params=SMALL,
        name="own_half",
    )(rows)


def gather_rows_body(parts, *refs):
    out_ref = refs[-1]
    first = 0
    for part_ref in refs[:parts]:
        count = part_ref.shape[0]
        out_ref[first : first + count, :] = part_ref[...]
        first += count


def gather_rows(parts, passed):
    rows = sum(part.shape[0] for part in parts)

    def body(*refs):
        gather_rows_body(len(parts), *refs)

    return pl.pallas_call(
        body,
        in_specs=[WHOLE] * len(parts) + [ANYWHERE] * len(passed),
        out_specs=[ANYWHERE] * len(passed) + [WHOLE],
        out_shape=[jax.ShapeDtypeStruct(array.shape, array.dtype) for array in passed]
        + [jax.ShapeDtypeStruct((rows, parts[0].shape[1]), parts[0].dtype)],
        input_output_aliases={len(parts) + i: i for i in range(len(passed))},
        cost_estimate=BRIEF,
        compiler_params=SMALL,
        name="gather_rows",
    )(*parts, *passed)


def pass_on(array, after):
    return pl.pallas_call(
        lambda *refs: None,
        in_specs=[ANYWHERE] * 2,
        out_specs=ANYWHERE,
        out_shape=jax.ShapeDtypeStruct(array.shape, array.dtype),
        input_output_aliases={0: 0},
        cost_estimate=BRIEF,
        compiler_params=SMALL,
        name="pass_on",
    )(array, after)


def join_body(one_ref, two_ref, after_ref, counts_ref, out_ref, mark_ref):
    rows = one_ref.shape[0]
    out_ref[:rows, :] = one_ref[...]
    out_ref[rows:, :] = two_ref[...]
    mark_ref[...] = jnp.zeros_like(mark_ref)


def join(one, two, after, counts):
    rows, channels = one.shape
    return pl.pallas_call(
        join_body,
        in_specs=[WHOLE] * 2 + [ANYWHERE] * 2,
        out_specs=[WHOLE] * 2,
        out_shape=[
            jax.ShapeDtypeStruct((2 * rows, channels), one.dtype),
            jax.ShapeDtypeStruct((8, LANES), jnp.float32),
        ],
        cost_estimate=BRIEF,
        compiler_params=SMALL,
        name="join",
    )(one, two, after, counts)


def split_by(value, size):
    return value >> (size.bit_length() - 1), value & (size - 1)


def score_body(slots, unit, refs_in):
    block_sm, tile_sm, live_sm, *stack_refs, owner_ref, own_ref = refs_in[:8]
    piece_refs = refs_in[8:12]
    out_ref, panel, totals, pass_tile = refs_in[13:]
    live = live_sm[0, 0, 0]
    section_index, grp, dev = (lax.axis_index(axis) for axis in ("section", "grp", "dev"))
    own_rows = own_ref.shape[0]
    devs = PREC // own_rows
    quarter = own_rows // GROUPS
    half = quarter // 2
    pair_rows = (devs - 1) // 2 * quarter
    piece_rows = piece_refs[0].shape[0] // 2
    tiles = stack_refs[0].shape[1] // TILE_ROWS

    slot_tile = [jnp.where(slot < live, tile_sm[0, 0, slot], -1) for slot in range(slots)]
    first_pass = [jnp.int32(0)]
    for tile in range(tiles):
        count = sum((there == tile).astype(jnp.int32) for there in slot_tile)
        first_pass.append(first_pass[tile] + ((count + 1) >> 1))
    passes = first_pass[tiles]
    slot_panel = []
    for slot, there in enumerate(slot_tile):
        rank = sum([(other == there).astype(jnp.int32) for other in slot_tile[:slot]], jnp.int32(0))
        at_pass = first_pass[0]
        for tile in range(1, tiles):
            at_pass = jnp.where(there == tile, first_pass[tile], at_pass)
        slot_panel.append(jnp.where(slot < live, 2 * at_pass + rank, 0))

    def fetch(slot):
        pass_tile[slot_panel[slot] >> 1] = slot_tile[slot]
        for u in range(PB // unit):
            owner, within = split_by(block_sm[0, 0, slot] * PB + u * unit, own_rows)
            part, offset = split_by(within, quarter)
            from_dev = dev ^ owner
            from_grp = grp ^ part
            halved = (from_dev == devs - 1) & ((devs - 1) % 2 == 1)
            late, offset_in_half = split_by(offset, half)
            core = jnp.where(halved, late, (from_dev - 1) & 1)
            at = jnp.where(
                halved, pair_rows + offset_in_half, ((from_dev - 1) >> 1) * quarter + offset
            )
            crossed = (core == 1) & ((from_grp == 1) | (from_grp == 2))
            piece = jnp.where(crossed, 3 - from_grp, from_grp)
            at = at + (piece & 1) * piece_rows
            piece = (piece >> 1) + 2 * (section_index ^ core)
            to = pl.ds(pl.multiple_of(slot_panel[slot] * PB + u * unit, unit), unit)

            @pl.when(from_dev == 0)
            def _():
                panel[to, :] = own_ref[pl.ds(pl.multiple_of(within, unit), unit), :]

            for p in range(len(piece_refs)):

                @pl.when((from_dev > 0) & (piece == p))
                def _():
                    panel[to, :] = piece_refs[p][pl.ds(pl.multiple_of(at, unit), unit), :]

    for slot in range(slots):

        @pl.when(slot < live)
        def _():
            fetch(slot)

    def visit(passes_here):
        sources = []
        for at_pass in passes_here:
            at = pl.ds(pl.multiple_of(pass_tile[at_pass] * TILE_ROWS, TILE_ROWS), TILE_ROWS)
            blocks = panel[pl.ds(pl.multiple_of(at_pass * 2 * PB, 2 * PB), 2 * PB), :]
            sources.append((at, blocks))
        added = [jnp.zeros((8, 2 * PB), jnp.float32)] * len(sources)
        for cells_ref in stack_refs:
            for f in range(cells_ref.shape[0]):
                for i, (at, blocks) in enumerate(sources):
                    scores = lax.dot_general(
                        cells_ref[f, at, :],
                        blocks,
                        (((1,), (1,)), ((), ())),
                        preferred_element_type=jnp.float32,
                    )
                    added[i] = added[i] + jnp.sum(
                        jnp.maximum(scores, 0.0).reshape(TILE_ROWS // 8, 8, 2 * PB), axis=0
                    )
        for at_pass, sums in zip(passes_here, added):
            totals[2 * at_pass] = sums[:, :PB]
            totals[2 * at_pass + 1] = sums[:, PB:]

    def visit_two(step, carry):
        visit([2 * step, 2 * step + 1])
        return carry

    lax.fori_loop(0, passes // 2, visit_two, 0)

    @pl.when(passes % 2 == 1)
    def _():
        visit([passes - 1])

    cells = sum(ref.shape[0] for ref in stack_refs) * TILE_ROWS
    high_index = lax.broadcasted_iota(jnp.int32, (BLOCKS, PB), 0)
    low_index = lax.broadcasted_iota(jnp.int32, (LANES, PB), 0)
    responses, highs, lows = [], [], []
    for slot in range(slots):
        is_live = slot < live
        total = totals[slot_panel[slot]]
        response = jnp.sum(total, axis=0, keepdims=True) / cells
        response = jnp.where(is_live, response, 0.0)
        owner = owner_ref[pl.ds(block_sm[0, 0, slot], 1), :]
        responses.append(response)
        highs.append(jnp.where(high_index == owner // LANES, response, 0.0))
        lows.append((low_index == owner % LANES).astype(jnp.bfloat16))
    high = jnp.concatenate(highs, axis=1)
    low = jnp.concatenate(lows, axis=1)
    placed = jnp.zeros((BLOCKS, LANES), jnp.float32)
    for _ in range(3):
        part = high.astype(jnp.bfloat16)
        high = high - part.astype(jnp.float32)
        placed = placed + lax.dot_general(
            part, low, (((1,), (1,)), ((), ())), preferred_element_type=jnp.float32
        )
    out_ref[:BLOCKS, :] = placed
    out_ref[BLOCKS:, :] = jnp.broadcast_to(
        jnp.sum(sum(responses), axis=1, keepdims=True), (8, LANES)
    )


def score(block_ids, tile_ids, live, stacks, owner_order, own_templates, pieces, mark):
    slots = block_ids.shape[2]
    own_rows, channels = own_templates.shape
    unit = min(own_rows // (2 * GROUPS), PB)
    tiles = stacks[0].shape[1] // TILE_ROWS
    passes = (slots + tiles) // 2

    def body(*refs):
        score_body(slots, unit, refs)

    return pl.pallas_call(
        body,
        in_specs=[SCALARS] * 3 + [WHOLE] * (len(stacks) + 2 + len(pieces)) + [ANYWHERE],
        out_specs=WHOLE,
        out_shape=jax.ShapeDtypeStruct((BLOCKS + 8, LANES), jnp.float32),
        scratch_shapes=[
            pltpu.VMEM((passes * 2 * PB, channels), jnp.bfloat16),
            pltpu.VMEM((passes * 2, 8, PB), jnp.float32),
            pltpu.SMEM((passes,), jnp.int32),
        ],
        cost_estimate=BRIEF,
        compiler_params=SMALL,
        name="score",
    )(block_ids, tile_ids, live, *stacks, owner_order, own_templates, *pieces, mark)


def summed_tail(mine_ref, other_ref, extra_refs):
    first = mine_ref.shape[0] - TAIL
    tail = mine_ref[first:, :] + other_ref[first:, :]
    for extra_ref in extra_refs:
        row = lax.broadcasted_iota(jnp.int32, (TAIL, LANES), 0)
        tail = tail + jnp.where(row >= TAIL // 2, extra_ref[...], 0.0)
    return tail


def halve_body(bit, mine_ref, other_ref, *refs):
    *extra_refs, keep_ref, send_ref, tail_ref = refs
    rows = keep_ref.shape[0] - TAIL
    side = lax.axis_index("dev") // bit % 2
    tail = summed_tail(mine_ref, other_ref, extra_refs)
    tail_ref[...] = tail
    for half, out_ref in ((side, keep_ref), (1 - side, send_ref)):
        at = pl.ds(pl.multiple_of(half * rows, rows), rows)
        out_ref[:rows, :] = mine_ref[at, :] + other_ref[at, :]
        out_ref[rows:, :] = tail


def halve(mine, other, extra, bit):
    rows = (mine.shape[0] - TAIL) // 2 + TAIL

    def body(*refs):
        halve_body(bit, *refs)

    return pl.pallas_call(
        body,
        in_specs=[WHOLE] * (2 + len(extra)),
        out_specs=[WHOLE] * 3,
        out_shape=[
            jax.ShapeDtypeStruct((count, LANES), jnp.float32) for count in (rows, rows, TAIL)
        ],
        cost_estimate=BRIEF,
        compiler_params=SMALL,
        name="halve",
    )(mine, other, *extra)


def normalize_body(groups, mine_ref, other_ref, *refs):
    *extra_refs, out_ref = refs
    rows = out_ref.shape[0]
    tail = summed_tail(mine_ref, other_ref, extra_refs)
    factor = (tail[TAIL // 2 : TAIL // 2 + 1, :] / groups) / tail[:1, :]
    out_ref[...] = (mine_ref[:rows, :] + other_ref[:rows, :]) * factor


def normalize(mine, other, extra, groups):
    def body(*refs):
        normalize_body(groups, *refs)

    return pl.pallas_call(
        body,
        in_specs=[WHOLE] * (2 + len(extra)),
        out_specs=WHOLE,
        out_shape=jax.ShapeDtypeStruct((mine.shape[0] - TAIL, LANES), jnp.float32),
        cost_estimate=BRIEF,
        compiler_params=SMALL,
        name="normalize",
    )(mine, other, *extra)


def on_device(frames, templates, pair_block, pair_tile, pair_count, owner_order):
    grp = lax.axis_index("grp")
    devs = lax.axis_size("dev")
    groups = lax.axis_size("grp")
    own_frames = frames[0]

    quarter = templates.shape[0] // groups
    own_quarter = lax.dynamic_slice_in_dim(templates, grp * quarter, quarter, 0)
    own_half = own_half_of(own_quarter)
    arrived = []
    for k in range(1, devs - 1, 2):
        arrived.append(split_swap(own_quarter, "dev", k, k + 1))
    if devs % 2 == 0:
        arrived.append(swap(own_half, "dev", devs - 1))

    other_frames = swap(own_frames, "section", 1)
    inner_own, inner_other, held, near_edge, far_edge, kernels = prepare(
        own_frames, other_frames
    )
    (remote,) = gather_rows(arrived, [])
    first = split_swap(remote, "grp", 1, 2)
    near_halo = swap(near_edge, "dev", 1)
    between = [pair for i in range(1, devs - 1, 2) for pair in ((i, i + 1), (i + 1, i))]
    far_halo = lax.ppermute(far_edge, "dev", between)

    inner, inner_mark = wavelets(kernels, inner_own, inner_other, [remote])
    near, near_mark = join(remote, first, inner_mark, pair_count)
    begun = start_edges(held, other_frames, near_mark)
    near_halo = pass_on(near_halo, begun[0])
    far = split_swap(near, "grp", 2, 1)
    near_other, far_other = swap(near_halo, "section", 1), swap(far_halo, "section", 1)
    head_own, tail_own = smooth_edges(near_halo, far_halo, *begun[:2])
    head_other, tail_other = smooth_edges(near_other, far_other, *begun[2:])
    head, head_mark = wavelets(kernels, head_own, head_other, [tail_other])
    far = pass_on(far, head_mark)
    tail, _ = wavelets(kernels, tail_own, tail_other, [far])
    pieces = [near, far, swap(near, "section", 1), swap(far, "section", 1)]

    contribution = score(
        pair_block,
        pair_tile,
        pair_count,
        [inner, head, tail],
        owner_order.reshape(BLOCKS, PB),
        templates,
        pieces,
        head_mark,
    )
    mine, other, extra = contribution, swap(contribution, "section", 1), []
    bit, across = devs, 1
    while bit > 1:
        bit //= 2
        mine, sent, tail = halve(mine, other, extra, bit)
        other, extra = swap(sent, "dev", bit), []
        if across < groups:
            extra = [cross_swap(tail, across, bit)]
            extra.append(swap(extra[0], "section", 1))
            across *= 2
    return normalize(mine, other, extra, groups).reshape(1, -1)


def solution(mesh):
    placed = (
        P("grp", "dev", "section", None),
        P("dev", None),
        P("section", "grp", "dev"),
        P("section", "grp", "dev"),
        P("section", "grp", "dev"),
        P(),
    )
    return jax.shard_map(
        on_device, mesh=mesh, in_specs=placed, out_specs=P("grp", "dev"), check_vma=False
    )
```
